32 devices in a mesh: dp: 8 (over z, x), mp: 4 (over y, core).
Axes of the slice: x: 2, y: 2, z: 4, core: 2. Of those that a mesh axis runs over, the one named last changes fastest.
Arguments:
- block_input: bfloat16 [16384, 1152], P(('dp', 'mp')), may hold values from -6 to 6
- cotangent: bfloat16 [16384, 1152], P(('dp', 'mp')), may hold values from -6 to 6
- expert_ids: int32 [16384], P(('dp', 'mp')), may hold values from 0 to 3, as said below
- slot_ids: int32 [16384], P(('dp', 'mp')), may hold values from 0 to 191, as said below
- inward_proj: float32 [2, 1152, 2304], P(None, None, ('dp', 'mp')), may hold values from -0.1875 to 0.1875
- select_proj: float32 [2304, 104], P(('dp', 'mp')), may hold values from -0.125 to 0.125
- delta_proj: float32 [72, 2304], P(None, ('dp', 'mp')), may hold values from -0.75 to 0.75
- channel_params: float32 [23, 2304], P(None, ('dp', 'mp')), may hold values from -7 to 3, as said below
- outward_proj: float32 [2304, 1152], P(('dp', 'mp')), may hold values from -0.25 to 0.25
- expert_up: float32 [4, 1152, 3072], P('mp', None, 'dp'), may hold values from -0.1875 to 0.1875
- expert_down: float32 [4, 3072, 1152], P('mp', 'dp'), may hold values from -0.4375 to 0.4375
- norm_gains: float32 [2, 1152], replicated, may hold values from 0.5 to 1.5
- router_weight: float32 [1152, 4], replicated, may hold values from -0.125 to 0.125
- inward_velocity: float32 [2, 1152, 2304], P(None, None, ('dp', 'mp')), may hold values from -3 to 3
- select_velocity: float32 [2304, 104], P(('dp', 'mp')), may hold values from -1.75 to 1.75
- delta_velocity: float32 [72, 2304], P(None, ('dp', 'mp')), may hold values from -0.1875 to 0.1875
- channel_velocity: float32 [23, 2304], P(None, ('dp', 'mp')), may hold values from -1.75 to 1.75
- outward_velocity: float32 [2304, 1152], P(('dp', 'mp')), may hold values from -2.5 to 2.5
- upward_velocity: float32 [4, 1152, 3072], P('mp', None, 'dp'), may hold values from -0.875 to 0.875
- downward_velocity: float32 [4, 3072, 1152], P('mp', 'dp'), may hold values from -0.5 to 0.5
- gains_velocity: float32 [2, 1152], replicated, may hold values from -6 to 6
- router_velocity: float32 [1152, 4], replicated, may hold values from -6 to 6
- inward_average: float32 [2, 1152, 2304], P(None, None, ('dp', 'mp')), may hold values from -0.1875 to 0.1875
- select_average: float32 [2304, 104], P(('dp', 'mp')), may hold values from -0.125 to 0.125
- delta_average: float32 [72, 2304], P(None, ('dp', 'mp')), may hold values from -0.75 to 0.75
- channel_average: float32 [23, 2304], P(None, ('dp', 'mp')), may hold values from -7 to 3, as said below
- outward_average: float32 [2304, 1152], P(('dp', 'mp')), may hold values from -0.25 to 0.25
- upward_average: float32 [4, 1152, 3072], P('mp', None, 'dp'), may hold values from -0.1875 to 0.1875
- downward_average: float32 [4, 3072, 1152], P('mp', 'dp'), may hold values from -0.4375 to 0.4375
- gains_average: float32 [2, 1152], replicated, may hold values from 0.5 to 1.5
- router_average: float32 [1152, 4], replicated, may hold values from -0.125 to 0.125
Outputs:
- block_output: bfloat16 [16384, 1152], P(('dp', 'mp'))
- block_grad: float32 [16384, 1152], P(('dp', 'mp'))
- inward_weight: float32 [2, 1152, 2304], P(None, None, ('dp', 'mp'))
- inward_momentum: float32 [2, 1152, 2304], P(None, None, ('dp', 'mp'))
- inward_smoothed: float32 [2, 1152, 2304], P(None, None, ('dp', 'mp'))
- inward_copy: bfloat16 [2, 1152, 2304], P(None, None, ('dp', 'mp'))
- select_weight: float32 [2304, 104], P(('dp', 'mp'))
- select_momentum: float32 [2304, 104], P(('dp', 'mp'))
- select_smoothed: float32 [2304, 104], P(('dp', 'mp'))
- select_copy: bfloat16 [2304, 104], P(('dp', 'mp'))
- delta_weight: float32 [72, 2304], P(None, ('dp', 'mp'))
- delta_momentum: float32 [72, 2304], P(None, ('dp', 'mp'))
- delta_smoothed: float32 [72, 2304], P(None, ('dp', 'mp'))
- delta_copy: bfloat16 [72, 2304], P(None, ('dp', 'mp'))
- channel_weight: float32 [23, 2304], P(None, ('dp', 'mp'))
- channel_momentum: float32 [23, 2304], P(None, ('dp', 'mp'))
- channel_smoothed: float32 [23, 2304], P(None, ('dp', 'mp'))
- channel_copy: bfloat16 [23, 2304], P(None, ('dp', 'mp'))
- outward_weight: float32 [2304, 1152], P(('dp', 'mp'))
- outward_momentum: float32 [2304, 1152], P(('dp', 'mp'))
- outward_smoothed: float32 [2304, 1152], P(('dp', 'mp'))
- outward_copy: bfloat16 [2304, 1152], P(('dp', 'mp'))
- upward_weight: float32 [4, 1152, 3072], P('mp', None, 'dp')
- upward_momentum: float32 [4, 1152, 3072], P('mp', None, 'dp')
- upward_smoothed: float32 [4, 1152, 3072], P('mp', None, 'dp')
- upward_copy: bfloat16 [4, 1152, 3072], P('mp', None, 'dp')
- downward_weight: float32 [4, 3072, 1152], P('mp', 'dp')
- downward_momentum: float32 [4, 3072, 1152], P('mp', 'dp')
- downward_smoothed: float32 [4, 3072, 1152], P('mp', 'dp')
- downward_copy: bfloat16 [4, 3072, 1152], P('mp', 'dp')
- gains_weight: float32 [2, 1152], replicated
- gains_momentum: float32 [2, 1152], replicated
- gains_smoothed: float32 [2, 1152], replicated
- gains_copy: bfloat16 [2, 1152], replicated
- router_new: float32 [1152, 4], replicated
- router_momentum: float32 [1152, 4], replicated
- router_smoothed: float32 [1152, 4], replicated
- router_copy: bfloat16 [1152, 4], replicated
The draws below stay inside these ranges and needn't reach their ends.
Inputs may be any that keep to these rules, and one draw needn't show every extreme that they name: `expert_ids`: in every block of 512 rows that one device holds no expert is named by more than 192 rows. `slot_ids`: rows of one block of 512 that name the same expert hold different slots. `channel_params`: rows 0 to 3 are convolution taps, row 4 their bias, row 5 the step bias, row 6 the skip gain, the last 16 rows the logarithms of the decay rates. `channel_average`: laid out as channel_params.
All inputs are finite; a program needn't handle non-finite values.
Results may differ from the reference program's by a relative error of at most 0.013.
Values may be sent and summed in bfloat16 or wider, within the bound.
No kernel may reach another device: no remote copies, remote signals or barrier semaphores. Data moves between devices by JAX's collectives and lax.ppermute only.
A program may use at most 384 MiB of HBM per device.

```python
import math
import jax
import jax.numpy as jnp
from jax import lax

D = 1152
INNER = 2304
STATE = 16
CONV = 4
DT_RANK = 72
H = 3072
TOK_DEV = 512
SPAN = 256
SUB = 16
EXPERTS = 4
SEQ = 2048
TOKENS = 16384
CAP = 192
XW = 104
VROWS = 23
N_DP = 8
N_MP = 4


def routing_draw(key):
    base_key = jax.random.fold_in(key, 5)
    block_count = TOKENS // TOK_DEV
    group_count = TOKENS // SEQ
    row_key, full_key = jax.random.split(base_key)
    full_rows = jax.random.randint(full_key, (group_count,), 0, EXPERTS)
    full_each = jnp.repeat(full_rows, SEQ // TOK_DEV)
    block_keys = jax.random.split(row_key, block_count)

    def one_block(block_key, full_expert):
        pick_key, shuffle_key = jax.random.split(block_key)
        others = jax.random.permutation(pick_key, (EXPERTS - 1) * CAP)[:TOK_DEV - CAP]
        other_expert = (others // CAP).astype(jnp.int32)
        other_expert = other_expert + (other_expert >= full_expert).astype(jnp.int32)
        expert_list = jnp.concatenate([jnp.full((CAP,), full_expert, jnp.int32), other_expert])
        slot_list = jnp.concatenate([jnp.arange(CAP, dtype=jnp.int32), (others % CAP).astype(jnp.int32)])
        shuffle = jax.random.permutation(shuffle_key, TOK_DEV)
        return (expert_list[shuffle], slot_list[shuffle])
    experts_drawn, slots_drawn = jax.vmap(one_block)(block_keys, full_each)
    return (experts_drawn.reshape(TOKENS), slots_drawn.reshape(TOKENS))


def draw_expert_ids(key, part):
    return routing_draw(key)[0]


def draw_slot_ids(key, part):
    return routing_draw(key)[1]


def channel_draw(key):
    tap_key, bias_key, step_key, skip_key, rate_key = jax.random.split(key, 5)
    taps = jax.random.uniform(tap_key, (CONV, INNER), jnp.float32, -0.6, 0.6)
    conv_bias = jnp.clip(0.2 * jax.random.normal(bias_key, (1, INNER), jnp.float32), -0.8, 0.8)
    step_size = jnp.exp(jax.random.uniform(step_key, (1, INNER), jnp.float32, math.log(0.001), math.log(0.1)))
    step_bias = jnp.log(jnp.expm1(step_size))
    skip_gain = jax.random.uniform(skip_key, (1, INNER), jnp.float32, 0.5, 1.5)
    rate_log = jnp.log(jax.random.uniform(rate_key, (STATE, INNER), jnp.float32, 1.0, 16.0))
    return jnp.concatenate([taps, conv_bias, step_bias, skip_gain, rate_log], axis=0)


def draw_channel_params(key, part):
    return channel_draw(jax.random.fold_in(key, 11))


def draw_channel_average(key, part):
    return channel_draw(jax.random.fold_in(key, 13))


def shard_levels(key, extent, pieces, least, high):
    level, own = 1.0, jax.random.fold_in(key, 6)
    for position, blocks in pieces:
        heights = jnp.exp(jax.random.uniform(jax.random.fold_in(own, position), (blocks,), jnp.float32, least / len(pieces), high / len(pieces)))
        level = level * jnp.repeat(heights, extent[position] // blocks).reshape([-1 if axis == position else 1 for axis in range(len(extent))])
    return level


def normal_values(rng, extent, scale, most, pieces=(), kind=jnp.bfloat16):
    result = jax.random.normal(rng, extent, jnp.float32) * scale
    if len(pieces) > 0:
        result = shard_levels(rng, extent, pieces, -0.22, 0.18) * result
    return jnp.clip(result, min=-most, max=most).astype(kind)


def setup_inputs(seed: int = 0) -> dict:
    arg_keys = jax.random.split(jax.random.key(seed), 32)
    return {
        "block_input": normal_values(arg_keys[0], (TOKENS, D), 1.0, 6.0, ((0, 32),)),
        "cotangent": normal_values(arg_keys[1], (TOKENS, D), 1.0, 6.0, ((0, 32),)),
        "expert_ids": draw_expert_ids(jax.random.fold_in(arg_keys[31], 71), 0),
        "slot_ids": draw_slot_ids(jax.random.fold_in(arg_keys[31], 71), 0),
        "inward_proj": normal_values(arg_keys[4], (2, D, INNER), D ** -0.5, 0.1875, ((2, 32),), jnp.float32),
        "select_proj": normal_values(arg_keys[5], (INNER, XW), INNER ** -0.5, 0.125, ((0, 32),), jnp.float32),
        "delta_proj": normal_values(arg_keys[6], (DT_RANK, INNER), DT_RANK ** -0.5, 0.75, ((1, 32),), jnp.float32),
        "channel_params": draw_channel_params(jax.random.fold_in(arg_keys[31], 71), 0),
        "outward_proj": normal_values(arg_keys[8], (INNER, D), (INNER // 4) ** -0.5, 0.25, ((0, 32),), jnp.float32),
        "expert_up": normal_values(arg_keys[9], (EXPERTS, D, H), D ** -0.5, 0.1875, ((0, 4), (2, 8)), jnp.float32),
        "expert_down": normal_values(arg_keys[10], (EXPERTS, H, D), (H // 16) ** -0.5, 0.4375, ((0, 4), (1, 8)), jnp.float32),
        "norm_gains": jnp.clip(1.0 + 0.1 * jax.random.normal(arg_keys[11], (2, D), jnp.float32), 0.5, 1.5),
        "router_weight": normal_values(arg_keys[12], (D, EXPERTS), (2 * D) ** -0.5, 0.125, (), jnp.float32),
        "inward_velocity": normal_values(arg_keys[13], (2, D, INNER), 0.5, 3.0, ((2, 32),), jnp.float32),
        "select_velocity": normal_values(arg_keys[14], (INNER, XW), 0.3, 1.75, ((0, 32),), jnp.float32),
        "delta_velocity": normal_values(arg_keys[15], (DT_RANK, INNER), 0.03, 0.1875, ((1, 32),), jnp.float32),
        "channel_velocity": normal_values(arg_keys[16], (VROWS, INNER), 0.3, 1.75, ((1, 32),), jnp.float32),
        "outward_velocity": normal_values(arg_keys[17], (INNER, D), 0.4, 2.5, ((0, 32),), jnp.float32),
        "upward_velocity": normal_values(arg_keys[18], (EXPERTS, D, H), 0.15, 0.875, ((0, 4), (2, 8)), jnp.float32),
        "downward_velocity": normal_values(arg_keys[19], (EXPERTS, H, D), 0.08, 0.5, ((0, 4), (1, 8)), jnp.float32),
        "gains_velocity": normal_values(arg_keys[20], (2, D), 1.0, 6.0, (), jnp.float32),
        "router_velocity": normal_values(arg_keys[21], (D, EXPERTS), 1.0, 6.0, (), jnp.float32),
        "inward_average": normal_values(arg_keys[22], (2, D, INNER), D ** -0.5, 0.1875, ((2, 32),), jnp.float32),
        "select_average": normal_values(arg_keys[23], (INNER, XW), INNER ** -0.5, 0.125, ((0, 32),), jnp.float32),
        "delta_average": normal_values(arg_keys[24], (DT_RANK, INNER), DT_RANK ** -0.5, 0.75, ((1, 32),), jnp.float32),
        "channel_average": draw_channel_average(jax.random.fold_in(arg_keys[31], 71), 0),
        "outward_average": normal_values(arg_keys[26], (INNER, D), (INNER // 4) ** -0.5, 0.25, ((0, 32),), jnp.float32),
        "upward_average": normal_values(arg_keys[27], (EXPERTS, D, H), D ** -0.5, 0.1875, ((0, 4), (2, 8)), jnp.float32),
        "downward_average": normal_values(arg_keys[28], (EXPERTS, H, D), (H // 16) ** -0.5, 0.4375, ((0, 4), (1, 8)), jnp.float32),
        "gains_average": jnp.clip(1.0 + 0.1 * jax.random.normal(arg_keys[29], (2, D), jnp.float32), 0.5, 1.5),
        "router_average": normal_values(arg_keys[30], (D, EXPERTS), (2 * D) ** -0.5, 0.125, (), jnp.float32),
    }


@jax.custom_vjp
def low(v):
    return lax.optimization_barrier(v.astype(jnp.bfloat16)).astype(jnp.float32)

@jax.custom_vjp
def low_back(v):
    return v

def low_keep(v):
    return (low(v), None)

def low_pass(kept, grad):
    return (grad,)

def back_keep(v):
    return (v, None)

def back_low(kept, grad):
    return (low(grad),)
low.defvjp(low_keep, low_pass)
low_back.defvjp(back_keep, back_low)
EPSILON = 1e-05
MOMENT = 0.9
SMOOTH = 0.6
LEARNING = (0.02, 0.03, 0.4, 0.3, 0.04, 0.07, 0.3, 0.3, 0.01)
HIGHEST = lax.Precision.HIGHEST

def matmul(left, right):
    return jnp.dot(left, right, precision=HIGHEST, preferred_element_type=jnp.float32)

def rms_norm(values, gain):
    factor = lax.rsqrt(lax.optimization_barrier(jnp.mean(values * values, axis=-1, keepdims=True)) + EPSILON)
    return values * factor * gain

def conv_act(conv_in, channel):
    length = conv_in.shape[0]
    padded = jnp.pad(conv_in, ((CONV - 1, 0), (0, 0)))
    total = channel[CONV] + jnp.zeros_like(conv_in)
    for offset in range(CONV):
        total = total + channel[offset] * padded[offset:offset + length]
    return jax.nn.silu(total)

def block_scan(activated, delta, bmat, cmat, rate, skip_gain):
    length, channels = activated.shape
    states = bmat.shape[1]
    block_count = length // SPAN
    sub_count = SPAN // SUB
    lower_ones = jnp.tril(jnp.ones((SUB, SUB), jnp.float32))
    inputs_all = (activated.reshape(block_count, sub_count, SUB, channels), delta.reshape(block_count, sub_count, SUB, channels), bmat.reshape(block_count, sub_count, SUB, states), cmat.reshape(block_count, sub_count, SUB, states))

    def span_step(carried, inputs_part):
        act_part, delta_part, bmat_part, cmat_part = inputs_part
        elapsed = jnp.cumsum(delta_part, axis=1)
        middle = elapsed[:, SUB // 2:SUB // 2 + 1, :]
        shifted = (elapsed - middle)[:, :, None, :] * rate
        driven = jnp.exp(shifted) * (delta_part * act_part)[:, :, None, :] * bmat_part[:, :, :, None]
        summed = jnp.einsum('tj,sjnc->stnc', lower_ones, driven, precision=HIGHEST)
        local_state = jnp.exp(-shifted) * summed
        decayed = jnp.exp(-elapsed[:, :, None, :] * rate)

        def sub_step(start_state, entry_pair):
            decay_end, local_end = entry_pair
            return (decay_end * start_state + local_end, start_state)
        last_state, starts = lax.scan(sub_step, carried, (decayed[:, -1], local_state[:, -1]))
        full_state = decayed * starts[:, None] + local_state
        output = lax.optimization_barrier(jnp.sum(cmat_part[:, :, :, None] * full_state, axis=2)) + skip_gain * act_part
        return (last_state, output)
    last_state, outputs = lax.scan(jax.checkpoint(span_step), jnp.zeros((states, channels), activated.dtype), inputs_all)
    return outputs.reshape(length, channels)

def mixer_tail(activated, gate_in, delta_lin, select_tail, channel):
    states = select_tail.shape[1] // 2
    delta = jax.nn.softplus(delta_lin + channel[CONV + 1])
    rate = jnp.exp(channel[CONV + 3:])
    scanned = block_scan(activated, delta, select_tail[:, :states], select_tail[:, states:], rate, channel[CONV + 2])
    return scanned * jax.nn.silu(gate_in)

def gelu_exact(values):
    return jax.nn.gelu(values, approximate=False)

def forward_sequence(params, tokens, expert_seq, slot_seq):
    inward, select, delta_raw, channel_raw, outward, upward, downward, gains, router = params
    inward_b = low(inward)
    select_b = low(select)
    delta_b = low(delta_raw)
    channel = low(channel_raw)
    outward_b = low(outward)
    up_b = low(upward)
    down_b = low(downward)
    normed = low(rms_norm(tokens, gains[0]))
    linear = low_back(jnp.einsum('td,kdc->ktc', normed, inward_b, precision=HIGHEST))
    activated = conv_act(linear[0], channel)
    selected = low_back(matmul(low(activated), select_b))
    rank_b = low(selected[:, :DT_RANK])
    delta_lin = low_back(matmul(rank_b, delta_b))
    gated = low(mixer_tail(activated, linear[1], delta_lin, selected[:, DT_RANK:], channel))
    residual = tokens + low_back(matmul(gated, outward_b))
    normed_next = rms_norm(residual, gains[1])
    probs = jax.nn.softmax(matmul(normed_next, router), axis=-1)
    choose = (expert_seq[:, None] == jnp.arange(EXPERTS, dtype=jnp.int32)[None, :]).astype(jnp.float32)
    gate_prob = lax.optimization_barrier(jnp.sum(probs * choose, axis=1))
    block_rows = jnp.arange(SEQ, dtype=jnp.int32) // TOK_DEV
    row_index = (expert_seq * (N_MP * CAP) + block_rows * CAP + slot_seq).astype(jnp.int32)
    rows_in = low_back(low(normed_next))
    buffer = jnp.zeros((EXPERTS * N_MP * CAP, D), jnp.float32).at[row_index].set(rows_in).reshape(EXPERTS, N_MP * CAP, D)
    up_lin = low_back(jnp.einsum('erd,edh->erh', buffer, up_b, precision=HIGHEST))
    activation = low(gelu_exact(up_lin))
    expert_out = low_back(low(jnp.einsum('erh,ehd->erd', activation, down_b, precision=HIGHEST)))
    tokens_out = expert_out.reshape(EXPERTS * N_MP * CAP, D)[row_index]
    return residual + gate_prob[:, None] * tokens_out

def nesterov(weight, velocity, average, gradient, rate):
    step_grad = gradient / math.sqrt(TOKENS)
    momentum = MOMENT * velocity + step_grad
    new_weight = weight - rate * (step_grad + MOMENT * momentum)
    smoothed = SMOOTH * average + (1.0 - SMOOTH) * new_weight
    return (new_weight, momentum, smoothed, new_weight.astype(jnp.bfloat16))

def reference(block_input, cotangent, expert_ids, slot_ids, inward_proj, select_proj, delta_proj, channel_params, outward_proj, expert_up, expert_down, norm_gains, router_weight, inward_velocity, select_velocity, delta_velocity, channel_velocity, outward_velocity, upward_velocity, downward_velocity, gains_velocity, router_velocity, inward_average, select_average, delta_average, channel_average, outward_average, upward_average, downward_average, gains_average, router_average):
    params = (inward_proj, select_proj, delta_proj, channel_params, outward_proj, expert_up, expert_down, norm_gains, router_weight)
    inputs_seq = block_input.astype(jnp.float32).reshape(N_DP, SEQ, D)
    cots_seq = cotangent.astype(jnp.float32).reshape(N_DP, SEQ, D)
    experts_seq = expert_ids.reshape(N_DP, SEQ)
    slots_seq = slot_ids.reshape(N_DP, SEQ)

    def one_sequence(totals, entry_set):
        tokens, cot_seq, expert_seq, slot_seq = entry_set

        def apply_layer(param_set, token_rows):
            return forward_sequence(param_set, token_rows, expert_seq, slot_seq)
        output, back_fn = jax.vjp(apply_layer, params, tokens)
        param_grads, token_grad = back_fn(cot_seq)
        totals = jax.tree.map(jnp.add, totals, param_grads)
        return (totals, (output.astype(jnp.bfloat16), token_grad))
    zero_grads = jax.tree.map(jnp.zeros_like, params)
    gradients, (outputs, token_grads) = lax.scan(one_sequence, zero_grads, (inputs_seq, cots_seq, experts_seq, slots_seq))
    block_output = outputs.reshape(TOKENS, D)
    block_grad = token_grads.reshape(TOKENS, D)
    inward_weight, inward_momentum, inward_smoothed, inward_copy = nesterov(inward_proj, inward_velocity, inward_average, gradients[0], LEARNING[0])
    select_weight, select_momentum, select_smoothed, select_copy = nesterov(select_proj, select_velocity, select_average, gradients[1], LEARNING[1])
    delta_weight, delta_momentum, delta_smoothed, delta_copy = nesterov(delta_proj, delta_velocity, delta_average, gradients[2], LEARNING[2])
    channel_weight, channel_momentum, channel_smoothed, channel_copy = nesterov(channel_params, channel_velocity, channel_average, gradients[3], LEARNING[3])
    outward_weight, outward_momentum, outward_smoothed, outward_copy = nesterov(outward_proj, outward_velocity, outward_average, gradients[4], LEARNING[4])
    upward_weight, upward_momentum, upward_smoothed, upward_copy = nesterov(expert_up, upward_velocity, upward_average, gradients[5], LEARNING[5])
    downward_weight, downward_momentum, downward_smoothed, downward_copy = nesterov(expert_down, downward_velocity, downward_average, gradients[6], LEARNING[6])
    gains_weight, gains_momentum, gains_smoothed, gains_copy = nesterov(norm_gains, gains_velocity, gains_average, gradients[7], LEARNING[7])
    router_new, router_momentum, router_smoothed, router_copy = nesterov(router_weight, router_velocity, router_average, gradients[8], LEARNING[8])
    return (block_output, block_grad, inward_weight, inward_momentum, inward_smoothed, inward_copy, select_weight, select_momentum, select_smoothed, select_copy, delta_weight, delta_momentum, delta_smoothed, delta_copy, channel_weight, channel_momentum, channel_smoothed, channel_copy, outward_weight, outward_momentum, outward_smoothed, outward_copy, upward_weight, upward_momentum, upward_smoothed, upward_copy, downward_weight, downward_momentum, downward_smoothed, downward_copy, gains_weight, gains_momentum, gains_smoothed, gains_copy, router_new, router_momentum, router_smoothed, router_copy)
```

```python
import functools
import math

import jax
import jax.numpy as jnp
from jax import lax
from jax.experimental import pallas as pl
from jax.experimental.pallas import tpu as pltpu
from jax.sharding import PartitionSpec as P

bf16=jnp.bfloat16; f32=jnp.float32
CONV=4; DT_RANK=72; SUBT=16; NST=16
LOG2E=1.0/math.log(2.0)

def dotf(a,b,dims=((1,),(0,))):
    return lax.dot_general(a,b,(dims,((),())),preferred_element_type=f32)

def block_mask():
    r=lax.broadcasted_iota(jnp.int32,(SUBT,SUBT*NST),0)
    c=lax.broadcasted_iota(jnp.int32,(SUBT,SUBT*NST),1)
    return (c//NST==r).astype(f32)

def spread(first, rows):
    r=lax.broadcasted_iota(jnp.int32,(rows,SUBT*NST),0)
    c=lax.broadcasted_iota(jnp.int32,(rows,SUBT*NST),1)
    return (c%NST+first==r).astype(bf16)

def soft_parts(x):
    e=jnp.exp(-jnp.abs(x))
    return jnp.maximum(x,0.0)+jnp.log1p(e), jnp.where(x>=0,1.0,e)/(1.0+e)

def row8(ref,k,t):
    d=ref[k,pl.ds(t,8,stride=0),:]
    return jnp.concatenate([d,d],0)

def split_states(sel_ref,bts,cts,T):
    wide=sel_ref.shape[1]
    selT=jnp.concatenate([sel_ref[...],jnp.zeros((T,128-wide),f32)],1).T
    for k in range(T//SUBT):
        bts[k]=selT[DT_RANK:DT_RANK+NST,SUBT*k:SUBT*k+SUBT]
        cts[k]=selT[DT_RANK+NST:DT_RANK+2*NST,SUBT*k:SUBT*k+SUBT]

def blocked(sel_ref,k,place,mask):
    sel=sel_ref[pl.ds(pl.multiple_of(k*SUBT,SUBT),SUBT),:]
    return (dotf(sel.astype(bf16),place)*mask).astype(bf16)

def scan_fwd_kernel(rank_ref, delta_w_ref, act_ref, gate_ref, sel_ref, chan_ref, out_w_ref,
                    s_ref, xlin_ref, scanned_ref, gated_ref, mix_ref,
                    state, dscr, uscr, yscr, bts, cts, sA, sB, *, T):
    C=act_ref.shape[1]; NCH=T//SUBT
    @pl.when(pl.program_id(0)==0)
    def _():
        state[...]=jnp.zeros_like(state)
    x=dotf(rank_ref[...],delta_w_ref[...])+chan_ref[CONV+1:CONV+2,:]
    xlin_ref[...]=x
    sp,_=soft_parts(x)
    dscr[...]=sp.reshape(NCH,SUBT,C)
    uscr[...]=(sp*act_ref[...]).reshape(NCH,SUBT,C)
    split_states(sel_ref,bts,cts,T)
    nrate=-LOG2E*jnp.exp(chan_ref[CONV+3:CONV+3+NST,:])
    mask=block_mask()
    ec=spread(DT_RANK+NST,sel_ref.shape[1])
    def one(k,S,cur,prev):
        before=jnp.maximum(k-1,0)
        yv=dotf(blocked(sel_ref,before,ec,mask),prev[...])
        bt=bts[k]
        for t in range(SUBT):
            d=row8(dscr,k,t); u=row8(uscr,k,t)
            S=jnp.exp2(d*nrate)*S+u*jnp.broadcast_to(bt[:,t:t+1],(NST,C))
            cur[t*NST:t*NST+NST,:]=S.astype(bf16)
        yscr[before]=yv
        s_ref[k]=cur[...]
        return S
    def pair(j,S):
        S=one(2*j,S,sA,sB)
        return one(2*j+1,S,sB,sA)
    sB[...]=jnp.zeros_like(sB)
    state[...]=lax.fori_loop(0,NCH//2,pair,state[...])
    yscr[NCH-1]=dotf(blocked(sel_ref,NCH-1,ec,mask),sB[...])
    scanned=yscr[...].reshape(T,C)+chan_ref[CONV+2:CONV+3,:]*act_ref[...]
    scanned_ref[...]=scanned
    g=gate_ref[...]
    gated=(scanned*(g/(1.0+jnp.exp(-g)))).astype(bf16)
    gated_ref[...]=gated
    mix_ref[...]=dotf(gated,out_w_ref[...]).astype(mix_ref.dtype)

def row_spec(T,w,rev=None):
    return pl.BlockSpec((T,w),(lambda i:(i,0)) if rev is None else (lambda i:(rev-1-i,0)))
def full_spec(a): return pl.BlockSpec(a.shape,lambda i:(0,)*a.ndim)

def scan_fwd(rank_b, delta_w, act, gate, sel, chan, out_w, T=256):
    N,C=act.shape; W=out_w.shape[1]; g=N//T; nch=T//SUBT
    row=functools.partial(row_spec,T); full=full_spec
    return pl.pallas_call(
        functools.partial(scan_fwd_kernel,T=T),
        grid=(g,),
        in_specs=[row(rank_b.shape[1]),full(delta_w),row(C),row(C),row(sel.shape[1]),full(chan),full(out_w)],
        out_specs=[pl.BlockSpec((nch,SUBT*NST,C),lambda i:(i,0,0)),row(C),row(C),row(C),row(W)],
        out_shape=[jax.ShapeDtypeStruct((N//SUBT,SUBT*NST,C),bf16),jax.ShapeDtypeStruct((N,C),f32),jax.ShapeDtypeStruct((N,C),f32),
                   jax.ShapeDtypeStruct((N,C),bf16),jax.ShapeDtypeStruct((N,W),bf16)],
        scratch_shapes=[pltpu.VMEM((NST,C),f32)]+[pltpu.VMEM((nch,SUBT,C),f32)]*3+[pltpu.VMEM((nch,NST,SUBT),f32)]*2+[pltpu.VMEM((SUBT*NST,C),bf16)]*2,
        compiler_params=pltpu.CompilerParams(vmem_limit_bytes=48*2**20),
        cost_estimate=pl.CostEstimate(flops=2*N*C*W,bytes_accessed=N*C*50+N*W*2,transcendentals=N*C*NST),
    )(rank_b,delta_w,act,gate,sel,chan,out_w)

def scan_bwd_kernel(dmix_ref, out_w_ref, s_ref, before_ref, act_ref, gate_ref, xlin_ref, scanned_ref, sel_ref, chan_ref, delta_w_ref,
                    dgate_ref, dact_ref, ddl_ref, dsel_ref, gch_ref,
                    qscr, dscr, uscr, dyscr, lbscr, wsscr, bts, cts, dbs, dcs, dselT, lA, wA, *, T, g):
    C=act_ref.shape[1]; NCH=T//SUBT
    step=pl.program_id(0)
    @pl.when(step==0)
    def _():
        qscr[...]=jnp.zeros_like(qscr)
        gch_ref[...]=jnp.zeros_like(gch_ref)
        dselT[...]=jnp.zeros_like(dselT)
    dg=dotf(dmix_ref[...],out_w_ref[...],((1,),(1,)))
    gt=gate_ref[...]; sg=1.0/(1.0+jnp.exp(-gt))
    dgate_ref[...]=(dg*scanned_ref[...]*(sg*(1.0+gt*(1.0-sg)))).astype(bf16)
    dy=dg*(gt*sg)
    act=act_ref[...]
    sp,sigd=soft_parts(xlin_ref[...])
    dscr[...]=sp.reshape(NCH,SUBT,C)
    uscr[...]=(sp*act).reshape(NCH,SUBT,C)
    dyscr[...]=dy.reshape(NCH,SUBT,C)
    split_states(sel_ref,bts,cts,T)
    rate=jnp.exp(chan_ref[CONV+3:CONV+3+NST,:]); nrate=-LOG2E*rate
    mask=block_mask()
    eb=spread(DT_RANK,sel_ref.shape[1])
    ones=mask.astype(bf16)
    lane=lax.broadcasted_iota(jnp.int32,(NST,SUBT),1)
    first=jnp.where(step==g-1,0.0,1.0)*before_ref[0,SUBT*NST-NST:SUBT*NST,:].astype(f32)
    def chunk(j,carry):
        q,acc=carry
        k=NCH-1-j
        bt=bts[k]; ct=cts[k]
        dbT=jnp.zeros((NST,SUBT),f32); dcT=dbT
        s_t=s_ref[k,SUBT*NST-NST:SUBT*NST,:].astype(f32)
        s_before=jnp.where(k==0,first,s_ref[jnp.maximum(k-1,0),SUBT*NST-NST:SUBT*NST,:].astype(f32))
        for t in range(SUBT-1,-1,-1):
            d=row8(dscr,k,t); u=row8(uscr,k,t); dyr=row8(dyscr,k,t)
            lam=jnp.broadcast_to(ct[:,t:t+1],(NST,C))*dyr+q
            lA[t*NST:t*NST+NST,:]=lam.astype(bf16)
            q=jnp.exp2(d*nrate)*lam
            dcT=jnp.where(lane==t,jnp.sum(s_t*dyr,axis=1,keepdims=True),dcT)
            dbT=jnp.where(lane==t,jnp.sum(lam*u,axis=1,keepdims=True),dbT)
            s_p=s_ref[k,t*NST-NST:t*NST,:].astype(f32) if t>0 else s_before
            wr=q*s_p*rate
            wA[t*NST:t*NST+NST,:]=wr.astype(bf16)
            acc=acc+wr*d
            s_t=s_p
        dbs[k]=dbT; dcs[k]=dcT
        lbscr[k]=dotf(blocked(sel_ref,k,eb,mask),lA[...])
        wsscr[k]=dotf(ones,wA[...])
        return q,acc
    q,acc=lax.fori_loop(0,NCH,chunk,(qscr[...],jnp.zeros((NST,C),f32)))
    qscr[...]=q
    gch_ref[CONV+3:CONV+3+NST,:]+=-acc
    lamB=lbscr[...].reshape(T,C); ws=wsscr[...].reshape(T,C)
    dyf=dyscr[...].reshape(T,C); spf=dscr[...].reshape(T,C)
    dact_ref[...]=chan_ref[CONV+2:CONV+3,:]*dyf+spf*lamB
    ddl=(act*lamB-ws)*sigd
    ddl_ref[...]=ddl.astype(bf16)
    gch_ref[CONV+1:CONV+2,:]+=jnp.sum(ddl,axis=0,keepdims=True)
    gch_ref[CONV+2:CONV+3,:]+=jnp.sum(dyf*act,axis=0,keepdims=True)
    for k in range(NCH):
        dselT[DT_RANK:DT_RANK+NST,SUBT*k:SUBT*k+SUBT]=dbs[k]
        dselT[DT_RANK+NST:DT_RANK+2*NST,SUBT*k:SUBT*k+SUBT]=dcs[k]
    dsel=dotf(ddl_ref[...],delta_w_ref[...],((1,),(1,)))+dselT[...].T
    dsel_ref[...]=dsel[:,:dsel_ref.shape[1]].astype(bf16)

def scan_bwd(dmix, out_w, s_all, act, gate, xlin, scanned, sel, chan, delta_w, T=256):
    N,C=act.shape; g=N//T; nch=T//SUBT; XW=sel.shape[1]
    row=lambda w: row_spec(T,w,g); full=full_spec
    vm=pltpu.VMEM
    return pl.pallas_call(
        functools.partial(scan_bwd_kernel,T=T,g=g),
        grid=(g,),
        in_specs=[row(dmix.shape[1]),full(out_w),pl.BlockSpec((nch,SUBT*NST,C),lambda i:(g-1-i,0,0)),
                  pl.BlockSpec((1,SUBT*NST,C),lambda i:(jnp.maximum((g-1-i)*nch-1,0),0,0)),
                  row(C),row(C),row(C),row(C),row(XW),full(chan),full(delta_w)],
        out_specs=[row(C),row(C),row(C),row(XW),pl.BlockSpec((24,C),lambda i:(0,0))],
        out_shape=[jax.ShapeDtypeStruct((N,C),bf16),jax.ShapeDtypeStruct((N,C),f32),jax.ShapeDtypeStruct((N,C),bf16),
                   jax.ShapeDtypeStruct((N,XW),bf16),jax.ShapeDtypeStruct((24,C),f32)],
        scratch_shapes=[vm((NST,C),f32)]+[vm((nch,SUBT,C),f32)]*5+[vm((nch,NST,SUBT),f32)]*4+[vm((128,T),f32)]+[vm((SUBT*NST,C),bf16)]*2,
        compiler_params=pltpu.CompilerParams(vmem_limit_bytes=56*2**20),
        cost_estimate=pl.CostEstimate(flops=2*N*C*dmix.shape[1],bytes_accessed=N*C*60,transcendentals=N*C*NST),
    )(dmix,out_w,s_all,s_all,act,gate,xlin,scanned,sel,chan,delta_w)

CAP = 192
EPSILON = 1e-05
MOMENT = 0.9
SMOOTH = 0.6
LEARNING = (0.02, 0.03, 0.4, 0.3, 0.04, 0.07, 0.3, 0.3, 0.01)
HIGHEST = lax.Precision.HIGHEST
LANES = 128


def conv_fwd_kernel(seq_ref, w_ref, chan_ref, selw_ref, conv_ref, gate_ref, pre_ref, act_ref, actb_ref, sel_ref, buf, *, T):
    C = conv_ref.shape[1]

    @pl.when(pl.program_id(0) == 0)
    def _():
        buf[0:8, :] = jnp.zeros((8, C), f32)

    seq = seq_ref[...]
    conv = dotf(seq, w_ref[0:C, :], ((1,), (1,)))
    gate_ref[...] = dotf(seq, w_ref[C : 2 * C, :], ((1,), (1,)))
    conv_ref[...] = conv
    buf[8 : 8 + T, :] = conv
    pre = chan_ref[CONV : CONV + 1, :] + chan_ref[CONV - 1 : CONV, :] * conv
    for tap in range(CONV - 1):
        pre = pre + chan_ref[tap : tap + 1, :] * buf[8 - CONV + 1 + tap : 8 - CONV + 1 + tap + T, :]
    buf[0:8, :] = buf[T : T + 8, :]
    pre_ref[...] = pre
    act = pre / (1.0 + jnp.exp(-pre))
    act_ref[...] = act
    actb = act.astype(bf16)
    actb_ref[...] = actb
    sel_ref[...] = dotf(actb, selw_ref[...])


def conv_fwd(seq, w_in, chan, selw, T=256):
    N = seq.shape[0]
    C = chan.shape[1]
    row, full = functools.partial(row_spec, T), full_spec
    XW = selw.shape[1]
    shape = jax.ShapeDtypeStruct
    return pl.pallas_call(
        functools.partial(conv_fwd_kernel, T=T),
        grid=(N // T,),
        in_specs=[row(seq.shape[1]), full(w_in), full(chan), full(selw)],
        out_specs=[row(C), row(C), row(C), row(C), row(C), row(XW)],
        out_shape=[shape((N, C), f32)] * 4 + [shape((N, C), bf16), shape((N, XW), f32)],
        scratch_shapes=[pltpu.VMEM((T + 8, C), f32)],
        compiler_params=pltpu.CompilerParams(vmem_limit_bytes=48 * 2**20),
        cost_estimate=pl.CostEstimate(
            flops=4 * N * C * seq.shape[1], bytes_accessed=N * C * 20, transcendentals=N * C
        ),
    )(seq, w_in, chan, selw)


def conv_bwd_kernel(
    dact_ref, dsel_ref, selw_ref, pre_ref, conv_ref, dgate_ref, w_ref, seq_ref, chan_ref,
    dconv_ref, dnorm_ref, gch_ref, gain_ref, buf, *, T
):
    C = conv_ref.shape[1]

    @pl.when(pl.program_id(0) == 0)
    def _():
        buf[T : T + 8, :] = jnp.zeros((8, C), f32)
        gch_ref[...] = jnp.zeros_like(gch_ref)
        gain_ref[...] = jnp.zeros_like(gain_ref)

    pre = pre_ref[...]
    sig = 1.0 / (1.0 + jnp.exp(-pre))
    dact = dact_ref[...] + dotf(dsel_ref[...], selw_ref[...], ((1,), (1,)))
    dpre = dact * (sig * (1.0 + pre * (1.0 - sig)))
    buf[0:T, :] = dpre
    conv = conv_ref[...]
    total = chan_ref[CONV - 1 : CONV, :] * dpre
    gch_ref[CONV - 1 : CONV, :] += jnp.sum(conv * dpre, axis=0, keepdims=True)
    for tap in range(CONV - 1):
        later = buf[CONV - 1 - tap : CONV - 1 - tap + T, :]
        total = total + chan_ref[tap : tap + 1, :] * later
        gch_ref[tap : tap + 1, :] += jnp.sum(conv * later, axis=0, keepdims=True)
    gch_ref[CONV : CONV + 1, :] += jnp.sum(dpre, axis=0, keepdims=True)
    buf[T : T + 8, :] = buf[0:8, :]
    dconv = total.astype(bf16)
    dconv_ref[...] = dconv
    dnorm = dotf(dconv, w_ref[0:C, :]) + dotf(dgate_ref[...], w_ref[C : 2 * C, :])
    dnorm_ref[...] = dnorm.astype(bf16)
    gain_ref[0:1, :] += jnp.sum(dnorm * seq_ref[...].astype(f32), axis=0, keepdims=True)


def conv_bwd(dact, dsel, selw, pre, conv, dgate, w_in, seq, chan, T=256):
    N, C = conv.shape
    D = seq.shape[1]
    g = N // T
    row, full = lambda w: row_spec(T, w, g), full_spec
    shape = jax.ShapeDtypeStruct
    return pl.pallas_call(
        functools.partial(conv_bwd_kernel, T=T),
        grid=(g,),
        in_specs=[row(C), row(dsel.shape[1]), full(selw), row(C), row(C), row(C), full(w_in), row(D), full(chan)],
        out_specs=[row(C), row(D), pl.BlockSpec((8, C), lambda i: (0, 0)), pl.BlockSpec((8, D), lambda i: (0, 0))],
        out_shape=[shape((N, C), bf16), shape((N, D), bf16), shape((8, C), f32), shape((8, D), f32)],
        scratch_shapes=[pltpu.VMEM((T + 8, C), f32)],
        compiler_params=pltpu.CompilerParams(vmem_limit_bytes=48 * 2**20),
        cost_estimate=pl.CostEstimate(flops=4 * N * C * D, bytes_accessed=N * C * 20, transcendentals=N * C),
    )(dact, dsel, selw, pre, conv, dgate, w_in, seq, chan)


def experts_kernel(x_ref, dz_ref, up_ref, down_ref, out_ref, drow_ref, gup_ref, gdown_ref, acc_out, acc_row, *, steps):
    @pl.when(pl.program_id(0) == 0)
    def _():
        acc_out[...] = jnp.zeros_like(acc_out)
        acc_row[...] = jnp.zeros_like(acc_row)

    x, dz, up, down = x_ref[...], dz_ref[...], up_ref[...], down_ref[...]
    lin = dotf(x, up, ((1,), (1,)))
    cdf = 0.5 * (1.0 + lax.erf(lin * math.sqrt(0.5)))
    act = (lin * cdf).astype(bf16)
    slope = cdf + lin * jnp.exp(-0.5 * lin * lin) * (1.0 / math.sqrt(2.0 * math.pi))
    acc_out[...] += dotf(act, down)
    dlin = (dotf(dz, down, ((1,), (1,))) * slope).astype(bf16)
    acc_row[...] += dotf(dlin, up)
    gdown_ref[...] = dotf(act, dz, ((0,), (0,))).astype(bf16)
    gup_ref[...] = dotf(dlin, x, ((0,), (0,))).astype(bf16)

    @pl.when(pl.program_id(0) == steps - 1)
    def _():
        out_ref[...] = acc_out[...].astype(bf16)
        drow_ref[...] = acc_row[...].astype(bf16)


def experts(x, dz, up, down, block=384):
    R, D = x.shape
    H = up.shape[0]
    steps = H // block
    fix = pl.BlockSpec((R, D), lambda i: (0, 0))
    mov = pl.BlockSpec((block, D), lambda i: (i, 0))
    shape = jax.ShapeDtypeStruct
    return pl.pallas_call(
        functools.partial(experts_kernel, steps=steps),
        grid=(steps,),
        in_specs=[fix, fix, mov, mov],
        out_specs=[fix, fix, mov, mov],
        out_shape=[shape((R, D), bf16)] * 2 + [shape((H, D), bf16)] * 2,
        scratch_shapes=[pltpu.VMEM((R, D), f32)] * 2,
        compiler_params=pltpu.CompilerParams(vmem_limit_bytes=56 * 2**20),
        cost_estimate=pl.CostEstimate(flops=12 * R * D * H, bytes_accessed=8 * H * D, transcendentals=R * H),
    )(x, dz, up, down)


def contract_rows(left, right):
    return dotf(left, right, ((0,), (0,)))


def ring_pairs(n):
    order = list(range(0, n, 2)) + list(range(n - 1, 0, -2))
    ahead = [(order[i], order[(i + 1) % n]) for i in range(n)]
    return ahead, [(b, a) for a, b in ahead]


def ring_gather(ahead_part, back_part, axis):
    n = lax.axis_size(axis)
    ahead, back = ring_pairs(n)
    first, second = [ahead_part], [back_part]
    for _ in range(n - 1):
        first.append(lax.ppermute(first[-1], axis, ahead))
        second.append(lax.ppermute(second[-1], axis, back))
    return first, [second[-r % n] for r in range(n)]


def ring_scatter(ahead_parts, back_parts, axis):
    n = lax.axis_size(axis)
    ahead, back = ring_pairs(n)
    one, two = ahead_parts[1], back_parts[n - 1]
    for s in range(n - 1):
        one = add_up(lax.ppermute(one, axis, ahead), ahead_parts[(s + 2) % n])
        two = add_up(lax.ppermute(two, axis, back), back_parts[(n - 2 - s) % n])
    return one, two


def add_up(a, b):
    return (a.astype(f32) + b.astype(f32)).astype(a.dtype)


def swap(value, j):
    n = lax.axis_size("mp")
    return lax.ppermute(value, "mp", [(i, i ^ j) for i in range(n)])


def gather_mp(rows):
    near = swap(rows, 1)
    across = swap(rows, 2)
    return [rows, near, across, swap(across, 1)]


def sum_mp(value):
    value = value + swap(value, 1)
    return value + swap(value, 2)


def scatter_mp(value):
    me = lax.axis_index("mp")
    block = lambda j: lax.dynamic_index_in_dim(value, me ^ j, 0, keepdims=False).astype(f32)
    near = swap(jnp.stack([block(1), block(3)]).astype(bf16), 1).astype(f32)
    far = (block(2) + near[1]).astype(bf16)
    return block(0) + near[0] + swap(far, 2).astype(f32)


def butterfly(value):
    for j in (1, 2):
        value = value + swap(value, j)
    n = lax.axis_size("dp")
    step = 1
    while step < n:
        value = value + lax.ppermute(value, "dp", [(i, i ^ step) for i in range(n)])
        step *= 2
    return value


def nesterov(weight, velocity, average, step_grad, rate):
    momentum = MOMENT * velocity + step_grad
    new_weight = weight - rate * (step_grad + MOMENT * momentum)
    smoothed = SMOOTH * average + (1.0 - SMOOTH) * new_weight
    return [new_weight, momentum, smoothed, new_weight.astype(jnp.bfloat16)]


def scale_of(values):
    return lax.rsqrt(jnp.mean(values * values, axis=-1, keepdims=True) + EPSILON)


def after(value, *others):
    return lax.optimization_barrier((value,) + others)[0]


def body(
    block_input, cotangent, expert_ids, slot_ids,
    inward_proj, select_proj, delta_proj, channel_params, outward_proj, expert_up, expert_down, norm_gains, router_weight,
    inward_velocity, select_velocity, delta_velocity, channel_velocity, outward_velocity, upward_velocity,
    downward_velocity, gains_velocity, router_velocity,
    inward_average, select_average, delta_average, channel_average, outward_average, upward_average,
    downward_average, gains_average, router_average,
):
    tok_rows, width = block_input.shape
    ring = lax.axis_size("dp")
    peers = lax.axis_size("mp")
    me = lax.axis_index("mp")
    own = inward_proj.shape[2]
    inner = own * ring
    wide = -(-inner // LANES) * LANES
    spare = wide - inner
    xw = select_proj.shape[1]
    vrows = channel_params.shape[0]

    first_a = jnp.concatenate(
        [
            inward_proj[0].T,
            select_proj,
            delta_proj.T,
            channel_params.T,
            jnp.zeros((own, 1), f32),
        ],
        axis=1,
    ).astype(bf16)
    first_b = inward_proj[1].T.astype(bf16)
    half = 5 * LANES
    in_a, in_b = ring_gather(first_a, first_b, "dp")
    out_a, out_b = ring_gather(
        after(outward_proj[:, :half].astype(bf16), in_a[-1], in_b[1]),
        after(outward_proj[:, half:].astype(bf16), in_a[-1], in_b[1]),
        "dp",
    )
    up_t = expert_up[0].T.astype(bf16)
    down_b = expert_down[0].astype(bf16)
    units = up_t.shape[0]
    mid = units // 2
    ex_a, ex_b = ring_gather(
        after(jnp.concatenate([up_t[:mid], down_b[:mid]]), out_a[-1], out_b[1]),
        after(jnp.concatenate([up_t[mid:], down_b[mid:]]), out_a[-1], out_b[1]),
        "dp",
    )
    up_all = jnp.concatenate([p[:mid] for p in ex_a] + [p[:mid] for p in ex_b])
    down_all = jnp.concatenate([p[mid:] for p in ex_a] + [p[mid:] for p in ex_b])

    rows_a = jnp.concatenate(in_a + [jnp.zeros((spare, first_a.shape[1]), bf16)])
    zero_rows = jnp.zeros((spare, width), bf16)
    w_in = jnp.concatenate([rows_a[:, :width]] + in_b + [zero_rows])
    small = rows_a[:, width:]
    selw = small[:, :xw]
    delta_t = small[:, xw : xw + DT_RANK]
    chan = small[:, xw + DT_RANK : xw + DT_RANK + vrows].astype(f32).T
    delta_w = delta_t.T
    out_w = jnp.concatenate(
        [jnp.concatenate(out_a + [zero_rows[:, :half]]), jnp.concatenate(out_b + [zero_rows[:, half:]])], axis=1
    )

    slot_index = (expert_ids ^ me) * CAP + slot_ids
    dispatch = (
        lax.broadcasted_iota(jnp.int32, (peers * CAP, tok_rows), 0) == slot_index[None, :]
    ).astype(bf16)

    def route(rows):
        return jnp.dot(dispatch, rows, preferred_element_type=f32)

    def unroute(blocks):
        return contract_rows(dispatch, blocks)

    def exchange(blocks):
        parts = blocks.reshape(peers, CAP, -1)
        return jnp.concatenate([parts[0]] + [swap(parts[j], j) for j in range(1, peers)])

    cot_rows = exchange(route(cotangent).astype(bf16))

    source = block_input.astype(f32)
    scale1 = scale_of(source)
    normed_b = (source * scale1 * norm_gains[0]).astype(bf16)

    def in_order(blocks):
        stacked = jnp.stack(blocks)
        return jnp.concatenate(
            [lax.dynamic_index_in_dim(stacked, me ^ m, 0, keepdims=False) for m in range(peers)]
        )

    seq = in_order(gather_mp(normed_b))
    conv_in, gate_in, pre, act, act_b, sel_part = conv_fwd(seq, w_in, chan, selw)
    selected = sum_mp(sel_part)
    rank_b = selected[:, :DT_RANK].astype(bf16)
    s_all, xlin, scanned, gated_b, mix = scan_fwd(rank_b, delta_w, act, gate_in, selected, chan, out_w)
    residual = source + scatter_mp(mix.reshape(peers, tok_rows, width))
    scale2 = scale_of(residual)
    normed2 = residual * scale2 * norm_gains[1]
    logits = jnp.dot(normed2, router_weight, precision=HIGHEST, preferred_element_type=f32)
    probs = jax.nn.softmax(logits, axis=-1)
    choose = (
        expert_ids[:, None] == jnp.arange(router_weight.shape[1], dtype=jnp.int32)[None, :]
    ).astype(f32)
    gate_prob = jnp.sum(probs * choose, axis=1)
    arrived = exchange(route(normed2.astype(bf16)).astype(bf16))
    prob_slots = (
        jnp.zeros((peers * CAP,), f32).at[slot_index].set(gate_prob)
    )
    prob_rows = exchange(prob_slots).reshape(peers * CAP)
    d_buffer = (prob_rows[:, None] * cot_rows.astype(f32)).astype(bf16)
    expert_out, d_rows, grad_up, grad_down = experts(arrived, d_buffer, up_all, down_all)
    d_arrived = exchange(d_rows)
    returned = exchange(expert_out)
    grad_out = cotangent.astype(f32)
    tokens_out = unroute(returned)
    block_output = (residual + gate_prob[:, None] * tokens_out).astype(bf16)
    d_gate = jnp.sum(grad_out * tokens_out, axis=1)
    d_logits = (d_gate * gate_prob)[:, None] * (choose - probs)
    d_normed2 = unroute(d_arrived) + lax.dot_general(
        d_logits, router_weight, (((1,), (1,)), ((), ())), precision=HIGHEST, preferred_element_type=f32
    )
    grad_router = lax.dot_general(
        normed2, d_logits, (((0,), (0,)), ((), ())), precision=HIGHEST, preferred_element_type=f32
    )
    hat2 = residual * scale2
    grad_gain2 = jnp.sum(d_normed2 * hat2, axis=0)
    a2 = norm_gains[1] * d_normed2
    d_residual = grad_out + scale2 * (a2 - hat2 * jnp.mean(a2 * hat2, axis=-1, keepdims=True))
    portion = in_order(gather_mp(d_residual.astype(bf16)))
    delta_pad = jnp.pad(delta_w, ((0, LANES - DT_RANK), (0, 0)))
    d_gate_b, d_act, ddl_b, dsel_part, gch_tail = scan_bwd(
        portion, out_w, s_all, act, gate_in, xlin, scanned, selected, chan, delta_pad
    )
    d_selected = sum_mp(dsel_part)
    d_conv_b, dnorm_part, gch_conv, gain_part = conv_bwd(
        d_act, d_selected, selw, pre, conv_in, d_gate_b, w_in, seq, chan
    )

    gparts_a = [grad_up[r * mid : (r + 1) * mid] for r in range(ring)]
    dparts_a = [grad_down[r * mid : (r + 1) * mid] for r in range(ring)]
    gparts_b = [grad_up[(ring + r) * mid : (ring + r + 1) * mid] for r in range(ring)]
    dparts_b = [grad_down[(ring + r) * mid : (ring + r + 1) * mid] for r in range(ring)]
    gu_a, gu_b = ring_scatter(gparts_a, gparts_b, "dp")
    gd_a, gd_b = ring_scatter(dparts_a, dparts_b, "dp")
    up_grad = jnp.concatenate([gu_a, gu_b]).astype(f32).T[None]
    down_grad = jnp.concatenate([gd_a, gd_b]).astype(f32)[None]

    grad_out_w = contract_rows(gated_b, portion)
    grad_delta = contract_rows(ddl_b, rank_b)
    grad_sel = contract_rows(act_b, d_selected)
    grad_in0 = contract_rows(d_conv_b, seq)
    grad_in1 = contract_rows(d_gate_b, seq)
    grad_chan = jnp.concatenate([gch_conv[: CONV + 1], gch_tail[CONV + 1 : CONV + 3 + NST], jnp.zeros((1, wide), f32)]).T
    pack_a = jnp.concatenate(
        [grad_in0, grad_sel, grad_delta, grad_chan, grad_out_w[:, :half]], axis=1
    ).astype(bf16)
    pack_b = jnp.concatenate([grad_in1, grad_out_w[:, half:]], axis=1).astype(bf16)
    split = lambda a: [a[r * own : (r + 1) * own] for r in range(ring)]
    sum_a, sum_b = ring_scatter(split(pack_a), split(pack_b), "dp")
    sum_a, sum_b = sum_a.astype(f32), sum_b.astype(f32)

    d_normed = scatter_mp(dnorm_part.reshape(peers, tok_rows, width))
    a1 = norm_gains[0] * d_normed
    hat1 = source * scale1
    block_grad = d_residual + scale1 * (a1 - hat1 * jnp.mean(a1 * hat1, axis=-1, keepdims=True))
    shared = butterfly(
        jnp.concatenate([(gain_part[:1] / norm_gains[:1]), grad_gain2[None], grad_router.T])
    )

    at = width + xw
    in_grad = jnp.stack([sum_a[:, :width].T, sum_b[:, :width].T])
    gradients = (
        in_grad,
        sum_a[:, width:at],
        sum_a[:, at : at + DT_RANK].T,
        sum_a[:, at + DT_RANK : at + DT_RANK + vrows].T,
        jnp.concatenate([sum_a[:, at + DT_RANK + vrows + 1 :], sum_b[:, width:]], axis=1),
        up_grad,
        down_grad,
        shared[:2],
        shared[2:].T,
    )
    masters = (
        inward_proj, select_proj, delta_proj, channel_params, outward_proj, expert_up, expert_down, norm_gains,
        router_weight,
    )
    velocities = (
        inward_velocity, select_velocity, delta_velocity, channel_velocity, outward_velocity, upward_velocity,
        downward_velocity, gains_velocity, router_velocity,
    )
    averages = (
        inward_average, select_average, delta_average, channel_average, outward_average, upward_average,
        downward_average, gains_average, router_average,
    )
    factor = 1.0 / math.sqrt(tok_rows * ring * peers)
    results = [block_output, block_grad]
    for position in range(9):
        results.extend(
            nesterov(
                masters[position],
                velocities[position],
                averages[position],
                gradients[position] * factor,
                LEARNING[position],
            )
        )
    return tuple(results)


def solution(mesh):
    in_specs = (
        P(("dp", "mp"), None),
        P(("dp", "mp"), None),
        P(("dp", "mp")),
        P(("dp", "mp")),
        P(None, None, ("dp", "mp")),
        P(("dp", "mp"), None),
        P(None, ("dp", "mp")),
        P(None, ("dp", "mp")),
        P(("dp", "mp"), None),
        P("mp", None, "dp"),
        P("mp", "dp", None),
        P(),
        P(),
        P(None, None, ("dp", "mp")),
        P(("dp", "mp"), None),
        P(None, ("dp", "mp")),
        P(None, ("dp", "mp")),
        P(("dp", "mp"), None),
        P("mp", None, "dp"),
        P("mp", "dp", None),
        P(),
        P(),
        P(None, None, ("dp", "mp")),
        P(("dp", "mp"), None),
        P(None, ("dp", "mp")),
        P(None, ("dp", "mp")),
        P(("dp", "mp"), None),
        P("mp", None, "dp"),
        P("mp", "dp", None),
        P(),
        P(),
    )
    out_specs = (
        P(("dp", "mp"), None),
        P(("dp", "mp"), None),
        P(None, None, ("dp", "mp")),
        P(None, None, ("dp", "mp")),
        P(None, None, ("dp", "mp")),
        P(None, None, ("dp", "mp")),
        P(("dp", "mp"), None),
        P(("dp", "mp"), None),
        P(("dp", "mp"), None),
        P(("dp", "mp"), None),
        P(None, ("dp", "mp")),
        P(None, ("dp", "mp")),
        P(None, ("dp", "mp")),
        P(None, ("dp", "mp")),
        P(None, ("dp", "mp")),
        P(None, ("dp", "mp")),
        P(None, ("dp", "mp")),
        P(None, ("dp", "mp")),
        P(("dp", "mp"), None),
        P(("dp", "mp"), None),
        P(("dp", "mp"), None),
        P(("dp", "mp"), None),
        P("mp", None, "dp"),
        P("mp", None, "dp"),
        P("mp", None, "dp"),
        P("mp", None, "dp"),
        P("mp", "dp", None),
        P("mp", "dp", None),
        P("mp", "dp", None),
        P("mp", "dp", None),
        P(),
        P(),
        P(),
        P(),
        P(),
        P(),
        P(),
        P(),
    )
    return jax.shard_map(body, mesh=mesh, in_specs=in_specs, out_specs=out_specs, check_vma=False)
```

```python
import functools
import math

import jax
import jax.numpy as jnp
from jax import lax
from jax.experimental import pallas as pl
from jax.experimental.pallas import tpu as pltpu
from jax.sharding import PartitionSpec as P

bf16, f32 = jnp.bfloat16, jnp.float32
CONV, DT_RANK, SUBT, NST = 4, 72, 16, 16
LOG2E = 1.0 / math.log(2.0)
LANES = 128
BLOCK = 256
CAP = 192
EPSILON = 1e-05
MOMENT = 0.9
SMOOTH = 0.6
LEARNING = (0.02, 0.03, 0.4, 0.3, 0.04, 0.07, 0.3, 0.3, 0.01)
HIGHEST = lax.Precision.HIGHEST
MIB = 2**20
SHAPE = jax.ShapeDtypeStruct


def dotf(a, b, dims=((1,), (0,))):
    return lax.dot_general(a, b, (dims, ((), ())), preferred_element_type=f32)


def block_mask():
    r = lax.broadcasted_iota(jnp.int32, (SUBT, SUBT * NST), 0)
    c = lax.broadcasted_iota(jnp.int32, (SUBT, SUBT * NST), 1)
    return (c // NST == r).astype(f32)


def spread(first, rows):
    r = lax.broadcasted_iota(jnp.int32, (rows, SUBT * NST), 0)
    c = lax.broadcasted_iota(jnp.int32, (rows, SUBT * NST), 1)
    return (c % NST + first == r).astype(bf16)


def soft_parts(x):
    e = jnp.exp(-jnp.abs(x))
    return jnp.maximum(x, 0.0) + jnp.log1p(e), jnp.where(x >= 0, 1.0, e) / (1.0 + e)


def row8(ref, k, t):
    d = ref[k, pl.ds(t, 8, stride=0), :]
    return jnp.concatenate([d, d], 0)


def split_states(sel_ref, bts, cts, T):
    selT = sel_ref[...].T
    for k in range(T // SUBT):
        bts[k] = selT[DT_RANK : DT_RANK + NST, SUBT * k : SUBT * k + SUBT]
        cts[k] = selT[DT_RANK + NST : DT_RANK + 2 * NST, SUBT * k : SUBT * k + SUBT]


def blocked(sel_ref, k, place, mask):
    sel = sel_ref[pl.ds(pl.multiple_of(k * SUBT, SUBT), SUBT), :]
    return (dotf(sel.astype(bf16), place) * mask).astype(bf16)


def blocked_all(sel_ref, place, T):
    r = lax.broadcasted_iota(jnp.int32, (T, SUBT * NST), 0)
    c = lax.broadcasted_iota(jnp.int32, (T, SUBT * NST), 1)
    flat = jnp.where(c // NST == r % SUBT, dotf(sel_ref[...].astype(bf16), place), 0.0)
    return flat.astype(bf16).reshape(T // SUBT, SUBT, SUBT * NST)


def rows_at(T, w, first=0):
    return pl.BlockSpec((T, w), lambda i: (first + i, 0))


def rows_back(T, w, last):
    return pl.BlockSpec((T, w), lambda i: (last - i, 0))


def whole(shape):
    shape = tuple(shape)
    return pl.BlockSpec(shape, lambda i: (0,) * len(shape))


def params(mib):
    return pltpu.CompilerParams(vmem_limit_bytes=mib * MIB)


def cost(flops=0, moved=1 << 20):
    return pl.CostEstimate(flops=flops, bytes_accessed=moved, transcendentals=0)


def turned(a):
    short = -a.shape[1] % LANES
    if short:
        a = jnp.concatenate([a, jnp.zeros((a.shape[0], short), f32)], axis=1)
    return a.T


def prep_kernel(in_ref, sel_ref, delta_ref, chan_ref, out_ref, a_ref, b_ref, *, half):
    own = sel_ref.shape[0]
    xw, vrows = sel_ref.shape[1], chan_ref.shape[0]
    width = in_ref.shape[2]
    a_ref[:, 0:width] = in_ref[0].astype(bf16)
    a_ref[:, width:] = out_ref[:, 0:half].astype(bf16)
    small = jnp.concatenate(
        [
            delta_ref[...],
            chan_ref[...],
            jnp.zeros((LANES - DT_RANK - vrows, own), f32),
        ],
        axis=0,
    )
    select = jnp.concatenate([sel_ref[...], jnp.zeros((own, LANES - xw), f32)], axis=1)
    b_ref[:, 0:width] = in_ref[1].astype(bf16)
    b_ref[:, width : width + LANES] = select.astype(bf16)
    b_ref[:, width + LANES : width + 2 * LANES] = turned(small)[0:own].astype(bf16)
    b_ref[:, width + 2 * LANES :] = out_ref[:, half:].astype(bf16)


def prep(inward, select, delta, channel, outward, half):
    own, width = outward.shape
    return pl.pallas_call(
        functools.partial(prep_kernel, half=half),
        out_shape=[SHAPE((own, width + half), bf16), SHAPE((own, 2 * width - half + 2 * LANES), bf16)],
        compiler_params=params(40),
        cost_estimate=cost(),
    )(inward, select, delta, channel, outward)


def prep_experts_kernel(up_ref, down_ref, both_ref):
    units = down_ref.shape[0]
    both_ref[0:units, :] = turned(up_ref[...])[0:units].astype(bf16)
    both_ref[units : 2 * units, :] = down_ref[...].astype(bf16)


def prep_experts(up, down):
    return pl.pallas_call(
        prep_experts_kernel,
        out_shape=SHAPE((2 * down.shape[0], down.shape[1]), bf16),
        compiler_params=params(40),
        cost_estimate=cost(),
    )(up, down)


def mixer_weights_kernel(owner_ref, *refs, ring, own, slot, width, half):
    a, b = refs[:ring], refs[ring : 2 * ring]
    w_ref, selw_ref, delta_ref, chan_ref, out_ref, small = refs[2 * ring :]
    wide = selw_ref.shape[0]
    if wide > ring * slot:
        for ref in (w_ref, selw_ref, out_ref, small):
            ref[...] = jnp.zeros_like(ref)

    def place(ref, at, value):
        if slot > own:
            value = jnp.concatenate([value, jnp.zeros((slot - own, value.shape[1]), value.dtype)], axis=0)
        ref[pl.ds(pl.multiple_of(at, 16), slot), :] = value

    for r in range(ring):
        at = owner_ref[r] * slot
        place(w_ref, at, a[r][:, 0:width])
        place(w_ref, wide + at, b[r][:, 0:width])
        place(selw_ref, at, b[r][:, width : width + LANES])
        place(small, at, b[r][:, width + LANES : width + 2 * LANES].astype(f32))
        place(out_ref, at, jnp.concatenate([a[r][:, width:], b[r][:, width + 2 * LANES :]], axis=1))
    flat = small[...].T
    delta_ref[0:DT_RANK, :] = flat[0:DT_RANK].astype(bf16)
    delta_ref[DT_RANK:LANES, :] = jnp.zeros((LANES - DT_RANK, wide), bf16)
    chan_ref[...] = flat[DT_RANK : DT_RANK + chan_ref.shape[0]]


def mixer_weights(owners, a, b, slot, wide, width, half):
    ring = len(a)
    own = b[0].shape[0]
    return pl.pallas_call(
        functools.partial(mixer_weights_kernel, ring=ring, own=own, slot=slot, width=width, half=half),
        in_specs=[pl.BlockSpec(memory_space=pltpu.SMEM)] + [pl.BlockSpec(memory_space=pltpu.VMEM)] * (2 * ring),
        out_shape=[
            SHAPE((2 * wide, width), bf16),
            SHAPE((wide, LANES), bf16),
            SHAPE((LANES, wide), bf16),
            SHAPE((24, wide), f32),
            SHAPE((wide, width), bf16),
        ],
        scratch_shapes=[pltpu.VMEM((wide, LANES), f32)],
        compiler_params=params(48),
        cost_estimate=cost(),
    )(owners, *a, *b)


def conv_fwd_kernel(seq_ref, w_ref, chan_ref, selw_ref, tail_ref, conv_ref, gate_ref, pre_ref, act_ref, actb_ref, sel_ref, end_ref, buf, *, T):
    C = conv_ref.shape[1]

    @pl.when(pl.program_id(0) == 0)
    def _():
        buf[0:8, :] = tail_ref[...]

    seq = seq_ref[...]
    conv = dotf(seq, w_ref[0:C, :], ((1,), (1,)))
    gate_ref[...] = dotf(seq, w_ref[C : 2 * C, :], ((1,), (1,)))
    conv_ref[...] = conv
    buf[8 : 8 + T, :] = conv
    pre = chan_ref[CONV : CONV + 1, :] + chan_ref[CONV - 1 : CONV, :] * conv
    for tap in range(CONV - 1):
        at = 8 - CONV + 1 + tap
        pre = pre + chan_ref[tap : tap + 1, :] * buf[at : at + T, :]
    buf[0:8, :] = buf[T : T + 8, :]
    end_ref[...] = buf[0:8, :]
    pre_ref[...] = pre
    act = pre / (1.0 + jnp.exp(-pre))
    act_ref[...] = act
    actb = act.astype(bf16)
    actb_ref[...] = actb
    sel_ref[...] = dotf(actb, selw_ref[...])


def conv_fwd(seq, first, count, w_in, chan, selw, tail, T=BLOCK):
    C, D = chan.shape[1], seq.shape[1]
    return pl.pallas_call(
        functools.partial(conv_fwd_kernel, T=T),
        grid=(count // T,),
        in_specs=[rows_at(T, D, first // T), whole(w_in.shape), whole(chan.shape), whole(selw.shape), whole(tail.shape)],
        out_specs=[rows_at(T, C)] * 5 + [rows_at(T, LANES), whole((8, C))],
        out_shape=[SHAPE((count, C), f32)] * 4 + [SHAPE((count, C), bf16), SHAPE((count, LANES), f32), SHAPE((8, C), f32)],
        scratch_shapes=[pltpu.VMEM((T + 8, C), f32)],
        compiler_params=params(48),
        cost_estimate=cost(),
    )(seq, w_in, chan, selw, tail)


def scan_fwd_kernel(
    sel_ref, delta_w_ref, act_ref, gate_ref, chan_ref, out_w_ref, start_ref,
    s_ref, xlin_ref, scanned_ref, gated_ref, mix_ref, rank_ref, end_ref,
    state, dscr, uscr, yscr, bts, cts, blocks, sA, sB, *, T
):
    C = act_ref.shape[1]
    NCH = T // SUBT

    @pl.when(pl.program_id(0) == 0)
    def _():
        state[...] = start_ref[...]

    rank = sel_ref[...].astype(bf16)
    rank_ref[...] = rank
    x = dotf(rank, delta_w_ref[...]) + chan_ref[CONV + 1 : CONV + 2, :]
    xlin_ref[...] = x
    sp, _ = soft_parts(x)
    dscr[...] = sp.reshape(NCH, SUBT, C)
    uscr[...] = (sp * act_ref[...]).reshape(NCH, SUBT, C)
    split_states(sel_ref, bts, cts, T)
    nrate = -LOG2E * jnp.exp(chan_ref[CONV + 3 : CONV + 3 + NST, :])
    blocks[...] = blocked_all(sel_ref, spread(DT_RANK + NST, LANES), T)

    def one(k, S, cur, prev):
        before = jnp.maximum(k - 1, 0)
        yv = dotf(blocks[before], prev[...])
        bt = bts[k]
        for t in range(SUBT):
            d = row8(dscr, k, t)
            u = row8(uscr, k, t)
            S = jnp.exp2(d * nrate) * S + u * jnp.broadcast_to(bt[:, t : t + 1], (NST, C))
            rounded = S.astype(bf16)
            cur[t * NST : t * NST + NST, :] = rounded
            s_ref[k, t * NST : t * NST + NST, :] = rounded
        yscr[before] = yv
        return S

    def pair(j, S):
        S = one(2 * j, S, sA, sB)
        return one(2 * j + 1, S, sB, sA)

    sB[...] = jnp.zeros_like(sB)
    state[...] = lax.fori_loop(0, NCH // 2, pair, state[...])
    end_ref[...] = state[...]
    yscr[NCH - 1] = dotf(blocks[NCH - 1], sB[...])
    scanned = yscr[...].reshape(T, C) + chan_ref[CONV + 2 : CONV + 3, :] * act_ref[...]
    scanned_ref[...] = scanned
    g = gate_ref[...]
    gated = (scanned * (g / (1.0 + jnp.exp(-g)))).astype(bf16)
    gated_ref[...] = gated
    mix_ref[...] = dotf(gated, out_w_ref[...]).astype(mix_ref.dtype)


def scan_fwd(sel, delta_w, act, gate, chan, out_w, start, T=BLOCK):
    N, C = act.shape
    W = out_w.shape[1]
    g, nch = N // T, T // SUBT
    vm = pltpu.VMEM
    return pl.pallas_call(
        functools.partial(scan_fwd_kernel, T=T),
        grid=(g,),
        in_specs=[rows_at(T, LANES), whole(delta_w.shape), rows_at(T, C), rows_at(T, C), whole(chan.shape), whole(out_w.shape), whole(start.shape)],
        out_specs=[pl.BlockSpec((nch, SUBT * NST, C), lambda i: (i, 0, 0))] + [rows_at(T, C)] * 3 + [rows_at(T, W), rows_at(T, LANES), whole((NST, C))],
        out_shape=[
            SHAPE((N // SUBT, SUBT * NST, C), bf16), SHAPE((N, C), f32), SHAPE((N, C), f32), SHAPE((N, C), bf16),
            SHAPE((N, W), bf16), SHAPE((N, LANES), bf16), SHAPE((NST, C), f32),
        ],
        scratch_shapes=[vm((NST, C), f32)] + [vm((nch, SUBT, C), f32)] * 3 + [vm((nch, NST, SUBT), f32)] * 2 + [vm((nch, SUBT, SUBT * NST), bf16)] + [vm((SUBT * NST, C), bf16)] * 2,
        compiler_params=params(48),
        cost_estimate=cost(),
    )(sel, delta_w, act, gate, chan, out_w, start)


def gather_states(first):
    r = lax.broadcasted_iota(jnp.int32, (SUBT * NST, LANES), 0)
    c = lax.broadcasted_iota(jnp.int32, (SUBT * NST, LANES), 1)
    return (r % NST + first == c).astype(bf16)


def fold(a):
    return sum(a[:, i : i + LANES] for i in range(LANES, a.shape[1], LANES)) + a[:, 0:LANES]


def scan_bwd_kernel(
    dmix_ref, out_w_ref, s_ref, before_ref, edge_ref, act_ref, gate_ref, xlin_ref, scanned_ref, sel_ref, chan_ref, delta_w_ref, q_ref,
    dgate_ref, dact_ref, ddl_ref, dsel_ref, gch_ref, qend_ref,
    qscr, dscr, uscr, dyscr, lbscr, wsscr, bts, cts, blocks, rows_b, rows_c, *bufs, T, g, opens
):
    C = act_ref.shape[1]
    NCH = T // SUBT
    step = pl.program_id(0)

    @pl.when(step == 0)
    def _():
        qscr[...] = q_ref[...]
        gch_ref[...] = jnp.zeros_like(gch_ref)

    dg = dotf(dmix_ref[...], out_w_ref[...], ((1,), (1,)))
    gt = gate_ref[...]
    sg = 1.0 / (1.0 + jnp.exp(-gt))
    dgate_ref[...] = (dg * scanned_ref[...] * (sg * (1.0 + gt * (1.0 - sg)))).astype(bf16)
    dy = dg * (gt * sg)
    act = act_ref[...]
    sp, sigd = soft_parts(xlin_ref[...])
    dscr[...] = sp.reshape(NCH, SUBT, C)
    uscr[...] = (sp * act).reshape(NCH, SUBT, C)
    dyscr[...] = dy.reshape(NCH, SUBT, C)
    split_states(sel_ref, bts, cts, T)
    nrate = -LOG2E * jnp.exp(chan_ref[CONV + 3 : CONV + 3 + NST, :])
    mask = block_mask()
    eb = spread(DT_RANK, LANES)
    half_rows = lax.broadcasted_iota(jnp.int32, (SUBT, SUBT * NST // 2), 0)
    half_cols = lax.broadcasted_iota(jnp.int32, (SUBT, SUBT * NST // 2), 1)
    halves = (half_cols // (NST // 2) == half_rows).astype(bf16)
    ones = jnp.ones((SUBT, LANES), bf16)
    last = slice(SUBT * NST - NST, SUBT * NST)
    first = before_ref[0, last, :].astype(f32)
    if opens:
        first = jnp.where(step == g - 1, edge_ref[...], first)

    def lanes_summed(partial):
        return (dotf(ones, partial[...].astype(bf16), ((1,), (1,))) * mask).astype(bf16)

    blocks[...] = blocked_all(sel_ref, eb, T)

    def one(k, q, acc, cur, prev):
        kp = jnp.minimum(k + 1, NCH - 1)
        lam_ref, w_ref, pb_ref, pc_ref = prev
        lamb = dotf(blocks[kp], lam_ref[...])
        wsum = dotf(halves, w_ref[...])
        sum_b, sum_c = lanes_summed(pb_ref), lanes_summed(pc_ref)
        lam_ref, w_ref, pb_ref, pc_ref = cur
        bt = bts[k]
        ct = cts[k]
        s_t = s_ref[k, last, :].astype(f32)
        s_before = jnp.where(k == 0, first, s_ref[jnp.maximum(k - 1, 0), last, :].astype(f32))
        held = None
        for t in range(SUBT - 1, -1, -1):
            d = row8(dscr, k, t)
            u = row8(uscr, k, t)
            dyr = row8(dyscr, k, t)
            lam = jnp.broadcast_to(ct[:, t : t + 1], (NST, C)) * dyr + q
            lam_ref[t * NST : t * NST + NST, :] = lam.astype(bf16)
            q = jnp.exp2(d * nrate) * lam
            pc_ref[t * NST : t * NST + NST, :] = fold(s_t * dyr)
            pb_ref[t * NST : t * NST + NST, :] = fold(lam * u)
            s_p = s_ref[k, t * NST - NST : t * NST, :].astype(f32) if t > 0 else s_before
            wr = q * s_p * nrate
            part = wr[0 : NST // 2] + wr[NST // 2 :]
            if t % 2:
                held = part
            else:
                w_ref[t * NST // 2 : t * NST // 2 + NST, :] = jnp.concatenate([part, held], axis=0).astype(bf16)
            acc = acc + wr * d
            s_t = s_p
        lbscr[kp] = lamb
        wsscr[kp] = wsum
        rows_b[kp] = sum_b
        rows_c[kp] = sum_c
        return q, acc

    def pair(j, carry):
        k = NCH - 1 - 2 * j
        carry = one(k, *carry, bufs[0:4], bufs[4:8])
        return one(k - 1, *carry, bufs[4:8], bufs[0:4])

    for ref in bufs[4:8]:
        ref[...] = jnp.zeros_like(ref)
    q, acc = lax.fori_loop(0, NCH // 2, pair, (qscr[...], jnp.zeros((NST, C), f32)))
    lam_ref, w_ref, pb_ref, pc_ref = bufs[4:8]
    lbscr[0] = dotf(blocks[0], lam_ref[...])
    wsscr[0] = dotf(halves, w_ref[...])
    rows_b[0] = lanes_summed(pb_ref)
    rows_c[0] = lanes_summed(pc_ref)
    qscr[...] = q
    qend_ref[...] = q
    gch_ref[CONV + 3 : CONV + 3 + NST, :] += acc * (1.0 / LOG2E)
    lamB = lbscr[...].reshape(T, C)
    ws = wsscr[...].reshape(T, C) * (-1.0 / LOG2E)
    dyf = dyscr[...].reshape(T, C)
    spf = dscr[...].reshape(T, C)
    dact_ref[...] = chan_ref[CONV + 2 : CONV + 3, :] * dyf + spf * lamB
    ddl = (act * lamB - ws) * sigd
    ddl_ref[...] = ddl.astype(bf16)
    gch_ref[CONV + 1 : CONV + 2, :] += jnp.sum(ddl, axis=0, keepdims=True)
    gch_ref[CONV + 2 : CONV + 3, :] += jnp.sum(dyf * act, axis=0, keepdims=True)
    flat = lambda ref: ref[...].reshape(T, SUBT * NST)
    dsel = dotf(ddl_ref[...], delta_w_ref[...], ((1,), (1,)))
    dsel = dsel + dotf(flat(rows_b), gather_states(DT_RANK)) + dotf(flat(rows_c), gather_states(DT_RANK + NST))
    dsel_ref[...] = dsel.astype(bf16)


def scan_bwd(dmix, at, half, kept, edge, q, count, out_w, sel, chan, delta_w, T=BLOCK):
    s_all, act, gate, xlin, scanned = kept
    C = act.shape[1]
    g, nch = count // T, T // SUBT
    low = half // T
    row = lambda w: rows_back(T, w, low + g - 1)
    out = lambda w: rows_back(T, w, g - 1)
    vm = pltpu.VMEM
    return pl.pallas_call(
        functools.partial(scan_bwd_kernel, T=T, g=g, opens=low == 0),
        grid=(g,),
        in_specs=[
            rows_back(T, dmix.shape[1], at // T + g - 1), whole(out_w.shape),
            pl.BlockSpec((nch, SUBT * NST, C), lambda i: (low + g - 1 - i, 0, 0)),
            pl.BlockSpec((1, SUBT * NST, C), lambda i: (jnp.maximum((low + g - 1 - i) * nch - 1, 0), 0, 0)),
            whole(edge.shape),
            row(C), row(C), row(C), row(C), row(LANES), whole(chan.shape), whole(delta_w.shape), whole(q.shape),
        ],
        out_specs=[out(C), out(C), out(C), out(LANES), whole((24, C)), whole((NST, C))],
        out_shape=[
            SHAPE((count, C), bf16), SHAPE((count, C), f32), SHAPE((count, C), bf16), SHAPE((count, LANES), bf16),
            SHAPE((24, C), f32), SHAPE((NST, C), f32),
        ],
        scratch_shapes=[vm((NST, C), f32)] + [vm((nch, SUBT, C), f32)] * 5 + [vm((nch, NST, SUBT), f32)] * 2 + [vm((nch, SUBT, SUBT * NST), bf16)] * 3
        + [vm((SUBT * NST, C), bf16), vm((SUBT * NST // 2, C), bf16), vm((SUBT * NST, LANES), f32), vm((SUBT * NST, LANES), f32)] * 2,
        compiler_params=params(56),
        cost_estimate=cost(),
    )(dmix, out_w, s_all, s_all, edge, act, gate, xlin, scanned, sel, chan, delta_w, q)


def conv_bwd_kernel(
    dact_ref, dsel_ref, selw_ref, pre_ref, conv_ref, dgate_ref, w_ref, seq_ref, chan_ref, next_ref,
    actb_ref, ddl_ref, rank_ref, before_ref, gchin_ref, tail_ref,
    dnorm_ref, gain_ref, head_ref, gch_ref, grad_ref, buf, acc, *, T, g, final
):
    C, D = conv_ref.shape[1], seq_ref.shape[1]
    step = pl.program_id(0)

    @pl.when(step == 0)
    def _():
        buf[T : T + 8, :] = next_ref[...]
        gch_ref[...] = gchin_ref[...]
        gain_ref[...] = jnp.zeros_like(gain_ref)
        acc[...] = before_ref[...]

    pre = pre_ref[...]
    sig = 1.0 / (1.0 + jnp.exp(-pre))
    dsel = dsel_ref[...]
    dact = dact_ref[...] + dotf(dsel, selw_ref[...], ((1,), (1,)))
    dpre = dact * (sig * (1.0 + pre * (1.0 - sig)))
    buf[0:T, :] = dpre
    conv = conv_ref[...]
    total = chan_ref[CONV - 1 : CONV, :] * dpre
    gch_ref[CONV - 1 : CONV, :] += jnp.sum(conv * dpre, axis=0, keepdims=True)
    for tap in range(CONV - 1):
        later = buf[CONV - 1 - tap : CONV - 1 - tap + T, :]
        total = total + chan_ref[tap : tap + 1, :] * later
        gch_ref[tap : tap + 1, :] += jnp.sum(conv * later, axis=0, keepdims=True)
    gch_ref[CONV : CONV + 1, :] += jnp.sum(dpre, axis=0, keepdims=True)
    buf[T : T + 8, :] = buf[0:8, :]
    head_ref[...] = buf[0:8, :]
    dconv = total.astype(bf16)
    seq = seq_ref[...]
    rows = ((0,), (0,))
    acc[:, 0:D] += dotf(dconv, seq, rows)
    acc[:, D : D + LANES] += dotf(actb_ref[...], dsel, rows)
    keep = lax.broadcasted_iota(jnp.int32, (T, LANES), 1) < DT_RANK
    rank = jnp.where(keep, rank_ref[...].astype(f32), 0.0).astype(bf16)
    acc[:, D + LANES :] += dotf(ddl_ref[...], rank, rows)
    dnorm = dotf(dconv, w_ref[0:C, :]) + dotf(dgate_ref[...], w_ref[C : 2 * C, :])
    dnorm_ref[...] = dnorm.astype(bf16)
    gain_ref[0:1, :] += jnp.sum(dnorm * seq.astype(f32), axis=0, keepdims=True)

    @pl.when(step == g - 1)
    def _():
        if final:
            taps = jnp.where(lax.broadcasted_iota(jnp.int32, (8, C), 0) <= CONV, gch_ref[...], tail_ref[0:8, :])
            side = jnp.concatenate(
                [jnp.zeros((DT_RANK, C), f32), taps, tail_ref[8:, :], jnp.zeros((LANES - DT_RANK - 24, C), f32)], axis=0
            )
            acc[:, D + LANES :] += side.T
        grad_ref[...] = acc[...].astype(grad_ref.dtype)


def conv_bwd(at, count, final, dact, dsel, selw, pre, conv, dgate, w_in, seq, chan, later, actb, ddl, rank, before, gch, tail, T=BLOCK):
    C, D = conv.shape[1], seq.shape[1]
    g = count // T
    own = lambda w: rows_back(T, w, g - 1)
    packed = SHAPE((C, D + 2 * LANES), bf16 if final else f32)
    return pl.pallas_call(
        functools.partial(conv_bwd_kernel, T=T, g=g, final=final),
        grid=(g,),
        in_specs=[
            own(C), own(LANES), whole(selw.shape), own(C), own(C), own(C), whole(w_in.shape),
            rows_back(T, D, at // T + g - 1), whole(chan.shape), whole(later.shape),
            own(C), own(C), own(LANES), whole(before.shape), whole(gch.shape), whole(tail.shape),
        ],
        out_specs=[own(D), whole((8, D)), whole((8, C)), whole((8, C)), whole(packed.shape)],
        out_shape=[SHAPE((count, D), bf16), SHAPE((8, D), f32), SHAPE((8, C), f32), SHAPE((8, C), f32), packed],
        scratch_shapes=[pltpu.VMEM((T + 8, C), f32), pltpu.VMEM(packed.shape, f32)],
        compiler_params=params(56),
        cost_estimate=cost(),
    )(dact, dsel, selw, pre, conv, dgate, w_in, seq, chan, later, actb, ddl, rank, before, gch, tail)


def as_column(row, count):
    return jnp.broadcast_to(row[0:1, :], (LANES, count)).T[:, 0:1]


def as_rows(column, count):
    return jnp.broadcast_to(column, (count, LANES)).T[0:8, :]


def experts_kernel(x_ref, cot_ref, prob_ref, w_ref, out_ref, drow_ref, dot_ref, g_ref, acc_out, acc_row, dz_ref, *, steps, per, units):
    R = x_ref.shape[0]

    @pl.when(pl.program_id(0) == 0)
    def _():
        acc_out[...] = jnp.zeros_like(acc_out)
        acc_row[...] = jnp.zeros_like(acc_row)
        dz_ref[...] = (as_column(prob_ref[...], R) * cot_ref[...].astype(f32)).astype(bf16)

    x, dz = x_ref[...], dz_ref[...]
    up = jnp.concatenate([w_ref[2 * r * units : (2 * r + 1) * units, :] for r in range(per)], axis=0)
    down = jnp.concatenate([w_ref[(2 * r + 1) * units : (2 * r + 2) * units, :] for r in range(per)], axis=0)
    lin = dotf(x, up, ((1,), (1,)))
    cdf = 0.5 * (1.0 + lax.erf(lin * math.sqrt(0.5)))
    act = (lin * cdf).astype(bf16)
    slope = cdf + lin * jnp.exp(-0.5 * lin * lin) * (1.0 / math.sqrt(2.0 * math.pi))
    acc_out[...] += dotf(act, down)
    dlin = (dotf(dz, down, ((1,), (1,))) * slope).astype(bf16)
    acc_row[...] += dotf(dlin, up)
    gdown = dotf(act, dz, ((0,), (0,))).astype(bf16)
    gup = dotf(dlin, x, ((0,), (0,))).astype(bf16)
    for r in range(per):
        g_ref[2 * r * units : (2 * r + 1) * units, :] = gup[r * units : (r + 1) * units]
        g_ref[(2 * r + 1) * units : (2 * r + 2) * units, :] = gdown[r * units : (r + 1) * units]

    @pl.when(pl.program_id(0) == steps - 1)
    def _():
        out = acc_out[...].astype(bf16)
        out_ref[...] = out
        drow_ref[...] = acc_row[...].astype(bf16)
        dot_ref[...] = as_rows(jnp.sum(out.astype(f32) * dz.astype(f32), axis=1, keepdims=True), R)


def experts(x, cot, prob, w, units, per=2):
    R, D = x.shape
    block = 2 * units * per
    steps = w.shape[0] // block
    fix = whole((R, D))
    mov = rows_at(block, D)
    return pl.pallas_call(
        functools.partial(experts_kernel, steps=steps, per=per, units=units),
        grid=(steps,),
        in_specs=[fix, fix, whole(prob.shape), mov],
        out_specs=[fix, fix, whole((8, R)), mov],
        out_shape=[SHAPE((R, D), bf16)] * 2 + [SHAPE((8, R), f32), SHAPE(w.shape, bf16)],
        scratch_shapes=[pltpu.VMEM((R, D), f32)] * 2 + [pltpu.VMEM((R, D), bf16)],
        compiler_params=params(60),
        cost_estimate=cost(),
    )(x, cot, prob, w)


def mean_scale(values):
    return lax.rsqrt(jnp.mean(values * values, axis=-1, keepdims=True) + EPSILON)


def dot32(a, b, dims):
    return lax.dot_general(a, b, (dims, ((), ())), precision=HIGHEST, preferred_element_type=f32)


def route_kernel(src_ref, near_ref, far_ref, gain_ref, router_ref, ids_ref, row_ref, col_ref, res_ref, prob_ref, gate_ref, out_ref, slotp_ref, *, count):
    res = src_ref[...].astype(f32) + near_ref[...] + far_ref[...].astype(f32)
    res_ref[...] = res
    normed = res * mean_scale(res) * gain_ref[1:2, :]
    T, S = res.shape[0], out_ref.shape[0]
    logits = dot32(normed, router_ref[...], ((1,), (0,)))
    lane = lax.broadcasted_iota(jnp.int32, (T, LANES), 1)
    logits = jnp.where(lane < count, logits, -jnp.inf)
    e = jnp.exp(logits - jnp.max(logits, axis=1, keepdims=True))
    probs = e / jnp.sum(e, axis=1, keepdims=True)
    prob_ref[...] = probs
    gate = jnp.sum(jnp.where(lane == ids_ref[...], probs, 0.0), axis=1, keepdims=True)
    gate_ref[...] = jnp.broadcast_to(gate, (T, LANES))
    take = (lax.broadcasted_iota(jnp.int32, (S, T), 0) == row_ref[...]).astype(bf16)
    out_ref[...] = dotf(take, normed.astype(bf16)).astype(bf16)
    put = lax.broadcasted_iota(jnp.int32, (T, S), 1) == col_ref[...]
    slotp_ref[...] = jnp.broadcast_to(jnp.sum(jnp.where(put, gate, 0.0), axis=0, keepdims=True), (8, S))


def route_tokens(source, near, far, gains, router, ids, row, col, slots, count):
    T, D = source.shape
    return pl.pallas_call(
        functools.partial(route_kernel, count=count),
        out_shape=[SHAPE((T, D), f32), SHAPE((T, LANES), f32), SHAPE((T, LANES), f32), SHAPE((slots, D), bf16), SHAPE((8, slots), f32)],
        compiler_params=params(48),
        cost_estimate=cost(),
    )(source, near, far, gains, router, ids, row, col)


def back_kernel(rows_ref, dot_ref, col_ref, ids_ref, prob_ref, router_ref, res_ref, cot_ref, gain_ref, dres_ref, dmix_ref, part_ref, *, count):
    res = res_ref[...]
    T, S = res.shape[0], rows_ref.shape[0]
    put = lax.broadcasted_iota(jnp.int32, (T, S), 1) == col_ref[...]
    lane = lax.broadcasted_iota(jnp.int32, (T, LANES), 1)
    weighted = jnp.sum(jnp.where(put, dot_ref[0:1, :], 0.0), axis=1, keepdims=True)
    dlog = weighted * (jnp.where(lane == ids_ref[...], 1.0, 0.0) - prob_ref[...])
    dnorm = dotf(put.astype(bf16), rows_ref[...]) + dot32(dlog, router_ref[...], ((1,), (1,)))
    scale = mean_scale(res)
    hat = res * scale
    part_ref[0:8, :] = jnp.broadcast_to(jnp.sum(dnorm * hat, axis=0, keepdims=True), (8, res.shape[1]))
    part_ref[8:, :] = dot32(dlog, hat * gain_ref[1:2, :], ((0,), (0,)))[0 : part_ref.shape[0] - 8]
    a = gain_ref[1:2, :] * dnorm
    dres = cot_ref[...].astype(f32) + scale * (a - hat * jnp.mean(a * hat, axis=-1, keepdims=True))
    dres_ref[...] = dres
    dmix_ref[...] = dres.astype(bf16)


def back_tokens(rows, dots, col, ids, probs, router, res, cot, gains, count):
    T, D = res.shape
    return pl.pallas_call(
        functools.partial(back_kernel, count=count),
        out_shape=[SHAPE((T, D), f32), SHAPE((T, D), bf16), SHAPE((16, D), f32)],
        compiler_params=params(48),
        cost_estimate=cost(),
    )(rows, dots, col, ids, probs, router, res, cot, gains)


def step_of(refs, outs, grad, rate, factor, at=Ellipsis):
    weight, velocity, average = (ref[at] for ref in refs)
    g = grad * factor
    momentum = MOMENT * velocity + g
    new = weight - rate * (g + MOMENT * momentum)
    outs[0][at] = new
    outs[1][at] = momentum
    outs[2][at] = SMOOTH * average + (1.0 - SMOOTH) * new
    outs[3][at] = new.astype(bf16)


def upright(a, rows, columns):
    a = a.astype(f32)
    short = -a.shape[0] % LANES
    if short:
        a = jnp.concatenate([a, jnp.zeros((short, a.shape[1]), f32)], axis=0)
    return a.T[0:rows, 0:columns]


def mixer_step_kernel(*refs, factor, own, width, xw, vrows):
    conv_ref, early_ref = refs[:2]
    ins = [refs[2 + 3 * p : 5 + 3 * p] for p in range(5)]
    outs = [refs[17 + 4 * p : 21 + 4 * p] for p in range(5)]
    inward, select, delta, channel, outward = range(5)
    step_of(ins[inward], outs[inward], conv_ref[0:own, 0:width].astype(f32), LEARNING[0], factor, 0)
    step_of(ins[inward], outs[inward], early_ref[0:own, 0:width].astype(f32), LEARNING[0], factor, 1)
    at = width
    step_of(ins[select], outs[select], conv_ref[0:own, at : at + LANES].astype(f32)[:, 0:xw], LEARNING[1], factor)
    rest = upright(conv_ref[:, at + LANES : at + 2 * LANES], LANES, own)
    step_of(ins[delta], outs[delta], rest[0:DT_RANK], LEARNING[2], factor)
    step_of(ins[channel], outs[channel], rest[DT_RANK : DT_RANK + vrows], LEARNING[3], factor)
    step_of(ins[outward], outs[outward], early_ref[0:own, width:].astype(f32), LEARNING[4], factor)


def mixer_step(conv, early, triples, factor):
    own, width = triples[4][0].shape
    xw, vrows = triples[1][0].shape[1], triples[3][0].shape[0]
    shapes = []
    for triple in triples:
        shapes += [SHAPE(triple[0].shape, f32)] * 3 + [SHAPE(triple[0].shape, bf16)]
    flat = pl.pallas_call(
        functools.partial(mixer_step_kernel, factor=factor, own=own, width=width, xw=xw, vrows=vrows),
        out_shape=shapes,
        compiler_params=params(56),
        cost_estimate=cost(),
    )(conv, early, *[a for triple in triples for a in triple])
    return [flat[4 * p : 4 * p + 4] for p in range(5)]


def experts_step_kernel(gup_ref, gdown_ref, *refs, factor):
    ups, downs = refs[0:3], refs[3:6]
    rows, columns = ups[0].shape[1:]
    step_of(ups, refs[6:10], upright(gup_ref[...], rows, columns), LEARNING[5], factor, 0)
    step_of(downs, refs[10:14], gdown_ref[...].astype(f32), LEARNING[6], factor, 0)


def experts_step(grads, ups, downs, factor):
    _, D, units = ups[0].shape
    block = LANES if units % LANES == 0 else units
    n = units // block
    up = pl.BlockSpec((1, D, block), lambda i: (0, 0, i))
    down = pl.BlockSpec((1, block, D), lambda i: (0, i, 0))
    shapes = lambda a: [SHAPE(a.shape, f32)] * 3 + [SHAPE(a.shape, bf16)]
    flat = pl.pallas_call(
        functools.partial(experts_step_kernel, factor=factor),
        grid=(n,),
        in_specs=[rows_at(block, D), rows_at(block, D, n)] + [up] * 3 + [down] * 3,
        out_specs=[up] * 4 + [down] * 4,
        out_shape=shapes(ups[0]) + shapes(downs[0]),
        compiler_params=params(48),
        cost_estimate=cost(),
    )(grads, grads, *ups, *downs)
    return flat[:4], flat[4:]


def contract_rows(left, right):
    return dotf(left, right, ((0,), (0,)))


def tie(*values):
    return lax.optimization_barrier(values)


def ring_order(n):
    return list(range(0, n, 2)) + list(range(n - 1, 0, -2))


def ring_gather(ahead_part, back_part, axis):
    n = lax.axis_size(axis)
    order = ring_order(n)
    ahead = [(order[i], order[(i + 1) % n]) for i in range(n)]
    back = [(b, a) for a, b in ahead]
    first, second = [ahead_part], [back_part]
    for _ in range(n - 1):
        first.append(lax.ppermute(first[-1], axis, ahead))
        second.append(lax.ppermute(second[-1], axis, back))
    place = [order.index(i) for i in range(n)]
    owners = jnp.array([[order[(place[i] - r) % n] for r in range(n)] for i in range(n)], jnp.int32)
    return owners[lax.axis_index(axis)], first, [second[-r % n] for r in range(n)]


def halving_sum(value, axis, fills=()):
    n = lax.axis_size(axis)
    me = lax.axis_index(axis)
    bit, out = 1, []
    rows = value.shape[1:]
    value = value.reshape((n,) + rows)
    while bit < n:
        mine = (me // bit) % 2
        pairs = value.reshape((value.shape[0] // 2, 2) + rows)
        keep = lax.dynamic_index_in_dim(pairs, mine, 1, keepdims=False)
        send = lax.dynamic_index_in_dim(pairs, 1 - mine, 1, keepdims=False)
        got = lax.ppermute(send, axis, [(i, i ^ bit) for i in range(n)])
        if fills:
            keep, *done = tie(keep, *fills[0]())
            fills, out = fills[1:], out + [done]
        value = (keep.astype(f32) + got.astype(f32)).astype(bf16)
        bit *= 2
    return value[0], out + [fill() for fill in fills]


def swap(value, j):
    n = lax.axis_size("mp")
    return lax.ppermute(value, "mp", [(i, i ^ j) for i in range(n)])


def gather_mp(rows):
    me, n = lax.axis_index("mp"), lax.axis_size("mp")
    near = swap(rows, 1)
    across = swap(rows, 2)
    total = jnp.zeros((n,) + rows.shape, rows.dtype)
    for j, block in enumerate([rows, near, across, swap(across, 1)]):
        total = lax.dynamic_update_index_in_dim(total, block, me ^ j, 0)
    return total.reshape(n * rows.shape[0], rows.shape[1])


def sum_mp(value):
    value = value + swap(value, 1)
    return value + swap(value, 2)


def scatter_mp(halves):
    me = lax.axis_index("mp")

    def pick(j):
        k = (me ^ j) % 2
        one = lax.dynamic_index_in_dim(halves[0], k, 0, keepdims=False)
        two = lax.dynamic_index_in_dim(halves[1], k, 0, keepdims=False)
        return jnp.where((me ^ j) < 2, one, two)

    near = swap(jnp.stack([pick(3), pick(1)]), 1).astype(f32)
    far = (pick(2).astype(f32) + near[0]).astype(bf16)
    return pick(0).astype(f32) + near[1], swap(far, 2)


def butterfly(value):
    for j in (1, 2):
        value = value + swap(value, j)
    n = lax.axis_size("dp")
    step = 1
    while step < n:
        value = value + lax.ppermute(value, "dp", [(i, i ^ step) for i in range(n)])
        step *= 2
    return value


def nesterov(weight, velocity, average, step_grad, rate):
    momentum = MOMENT * velocity + step_grad
    new_weight = weight - rate * (step_grad + MOMENT * momentum)
    smoothed = SMOOTH * average + (1.0 - SMOOTH) * new_weight
    return [new_weight, momentum, smoothed, new_weight.astype(jnp.bfloat16)]


def body(
    block_input, cotangent, expert_ids, slot_ids,
    inward_proj, select_proj, delta_proj, channel_params, outward_proj, expert_up, expert_down, norm_gains, router_weight,
    inward_velocity, select_velocity, delta_velocity, channel_velocity, outward_velocity, upward_velocity,
    downward_velocity, gains_velocity, router_velocity,
    inward_average, select_average, delta_average, channel_average, outward_average, upward_average,
    downward_average, gains_average, router_average,
):
    tok_rows, width = block_input.shape
    ring, peers = lax.axis_size("dp"), lax.axis_size("mp")
    me = lax.axis_index("mp")
    own = inward_proj.shape[2]
    slot = -(-own // 16) * 16
    wide = -(-slot * ring // LANES) * LANES
    experts_all = router_weight.shape[1]
    slots = peers * CAP

    half = 5 * LANES
    owners, mix_a, mix_b = ring_gather(
        *prep(jnp.swapaxes(inward_proj, 1, 2), select_proj, delta_proj, channel_params, outward_proj, half), "dp"
    )
    units = expert_down.shape[1]
    mix_a[3], mix_b[-3], up_own = tie(mix_a[3], mix_b[-3], expert_up[0])
    expert_w = lax.all_gather(prep_experts(up_own, expert_down[0]), "dp", axis=0, tiled=True)
    w_in, selw, delta_w, chan, out_w = mixer_weights(owners, mix_a, mix_b, slot, wide, width, half)

    slot_index = (expert_ids ^ me) * CAP + slot_ids
    slot_row, slot_col, ids_col = slot_index[None, :], slot_index[:, None], expert_ids[:, None]
    dispatch = (lax.broadcasted_iota(jnp.int32, (slots, tok_rows), 0) == slot_row).astype(bf16)
    router_pad = jnp.pad(router_weight, ((0, 0), (0, LANES - experts_all)))

    def exchange(blocks):
        parts = blocks.reshape(peers, CAP, -1)
        return jnp.concatenate([parts[0]] + [swap(parts[j], j) for j in range(1, peers)])

    def exchange_row(rows):
        parts = rows[0].reshape(peers, CAP)
        row = jnp.concatenate([parts[0]] + [swap(parts[j], j) for j in range(1, peers)])
        return jnp.broadcast_to(row[None], (8, slots))

    source = block_input.astype(f32)
    scale1 = mean_scale(source)
    normed_b = (source * scale1 * norm_gains[0]).astype(bf16)
    seq = gather_mp(normed_b)
    cot_out = jnp.dot(dispatch, cotangent, preferred_element_type=f32).astype(bf16)
    cot_out, seq = tie(cot_out, seq)
    cot_rows = exchange(cot_out)

    count = seq.shape[0] // 2
    conv_tail, state = jnp.zeros((8, wide), f32), jnp.zeros((NST, wide), f32)
    convs, scans, selections = [], [], []
    for h in range(2):
        convs.append(conv_fwd(seq, h * count, count, w_in, chan, selw, conv_tail))
        conv_tail = convs[-1][6]
        selections.append(sum_mp(convs[-1][5]))
    edges = [state]
    for h in range(2):
        conv_in, gate_in, pre, act, act_b, _, _ = convs[h]
        scans.append(scan_fwd(selections[h], delta_w, act, gate_in, chan, out_w, state))
        state = scans[-1][6]
        edges.append(state)
    near, far = scatter_mp([s[4].reshape(2, tok_rows, width) for s in scans])
    residual, probs, gate_prob, outgoing, prob_slots = route_tokens(
        block_input, near, far, norm_gains, router_pad, ids_col, slot_row, slot_col, slots, experts_all
    )
    arrived = exchange(outgoing)
    expert_out, d_rows, dots, grad_experts = experts(arrived, cot_rows, exchange_row(prob_slots), expert_w, units)
    experts_grad = lax.psum_scatter(grad_experts, "dp", scatter_dimension=0, tiled=True)

    d_residual, d_mixer, parts = back_tokens(
        exchange(d_rows), exchange_row(dots), slot_col, ids_col, probs, router_pad, residual, cotangent, norm_gains,
        experts_all,
    )
    portion = gather_mp(d_mixer)
    expert_out, portion = tie(expert_out, portion)
    returned = exchange(expert_out)

    def both(left, right):
        return contract_rows(left[0], right[:count]) + contract_rows(left[1], right[count:])

    def cut(a):
        return a[: slot * ring]

    out_grad = both([s[3] for s in scans], portion).astype(bf16)
    q, later = jnp.zeros((NST, wide), f32), jnp.zeros((8, wide), f32)
    tails, sums = [None] * 2, [None] * 2
    for h in (1, 0):
        kept = scans[h][0], convs[h][3], convs[h][1], scans[h][1], scans[h][2]
        tails[h] = scan_bwd(portion, h * count, 0, kept, edges[h], q, count, out_w, selections[h], chan, delta_w)
        q = tails[h][5]
        sums[h] = sum_mp(tails[h][3])
    gate_grad = both([t[0] for t in tails], seq).astype(bf16)
    early = jnp.concatenate([cut(gate_grad), cut(out_grad)], axis=1)
    early, experts_grad = tie(early, experts_grad)
    early = lax.psum_scatter(early, "dp", scatter_dimension=0, tiled=True)
    grads, gch = jnp.zeros((wide, width + 2 * LANES), f32), jnp.zeros((8, wide), f32)
    tail_sum = tails[0][4] + tails[1][4]
    dnorms, gains = [None] * 2, [None] * 2
    for h in (1, 0):
        dnorms[h], gains[h], later, gch, grads = conv_bwd(
            h * count, count, h == 0, tails[h][1], sums[h], selw, convs[h][2], convs[h][0], tails[h][0], w_in, seq,
            chan, later, convs[h][4], tails[h][2], scans[h][5], grads, gch, tail_sum,
        )
    near, far = scatter_mp([d.reshape(2, tok_rows, width) for d in dnorms])
    factor = 1.0 / math.sqrt(tok_rows * ring * peers)
    gain_part = (gains[0][:1] + gains[1][:1]) / norm_gains[:1]
    small = jnp.concatenate([gain_part, parts[:1], parts[8 : 8 + experts_all]])

    def expert_update():
        up_new, down_new = experts_step(
            experts_grad,
            (expert_up, upward_velocity, upward_average),
            (expert_down, downward_velocity, downward_average),
            factor,
        )
        return list(up_new) + list(down_new)

    def token_results():
        d_normed = near + far.astype(f32)
        a1 = norm_gains[0] * d_normed
        hat1 = source * scale1
        block_grad = d_residual + scale1 * (a1 - hat1 * jnp.mean(a1 * hat1, axis=-1, keepdims=True))
        tokens_out = contract_rows(dispatch, returned)
        return (residual + gate_prob[:, :1] * tokens_out).astype(bf16), block_grad

    conv_grad, filled = halving_sum(
        cut(grads).reshape(ring, slot, -1), "dp", [expert_update, token_results, lambda: [butterfly(small)]]
    )
    expert_new, (block_output, block_grad), (shared,) = filled[:3]
    mixer_new = mixer_step(
        conv_grad,
        early,
        (
            tuple(jnp.swapaxes(a, 1, 2) for a in (inward_proj, inward_velocity, inward_average)),
            (select_proj, select_velocity, select_average),
            (delta_proj, delta_velocity, delta_average),
            (channel_params, channel_velocity, channel_average),
            (outward_proj, outward_velocity, outward_average),
        ),
        factor,
    )
    results = [block_output, block_grad]
    mixer_new[0] = [jnp.swapaxes(a, 1, 2) for a in mixer_new[0]]
    for new in mixer_new:
        results.extend(new)
    results.extend(expert_new)
    results.extend(nesterov(norm_gains, gains_velocity, gains_average, shared[:2] * factor, LEARNING[7]))
    results.extend(nesterov(router_weight, router_velocity, router_average, shared[2:].T * factor, LEARNING[8]))
    return tuple(results)


def solution(mesh):
    in_specs = (
        P(("dp", "mp"), None),
        P(("dp", "mp"), None),
        P(("dp", "mp")),
        P(("dp", "mp")),
        P(None, None, ("dp", "mp")),
        P(("dp", "mp"), None),
        P(None, ("dp", "mp")),
        P(None, ("dp", "mp")),
        P(("dp", "mp"), None),
        P("mp", None, "dp"),
        P("mp", "dp", None),
        P(),
        P(),
        P(None, None, ("dp", "mp")),
        P(("dp", "mp"), None),
        P(None, ("dp", "mp")),
        P(None, ("dp", "mp")),
        P(("dp", "mp"), None),
        P("mp", None, "dp"),
        P("mp", "dp", None),
        P(),
        P(),
        P(None, None, ("dp", "mp")),
        P(("dp", "mp"), None),
        P(None, ("dp", "mp")),
        P(None, ("dp", "mp")),
        P(("dp", "mp"), None),
        P("mp", None, "dp"),
        P("mp", "dp", None),
        P(),
        P(),
    )
    out_specs = (
        P(("dp", "mp"), None),
        P(("dp", "mp"), None),
        P(None, None, ("dp", "mp")),
        P(None, None, ("dp", "mp")),
        P(None, None, ("dp", "mp")),
        P(None, None, ("dp", "mp")),
        P(("dp", "mp"), None),
        P(("dp", "mp"), None),
        P(("dp", "mp"), None),
        P(("dp", "mp"), None),
        P(None, ("dp", "mp")),
        P(None, ("dp", "mp")),
        P(None, ("dp", "mp")),
        P(None, ("dp", "mp")),
        P(None, ("dp", "mp")),
        P(None, ("dp", "mp")),
        P(None, ("dp", "mp")),
        P(None, ("dp", "mp")),
        P(("dp", "mp"), None),
        P(("dp", "mp"), None),
        P(("dp", "mp"), None),
        P(("dp", "mp"), None),
        P("mp", None, "dp"),
        P("mp", None, "dp"),
        P("mp", None, "dp"),
        P("mp", None, "dp"),
        P("mp", "dp", None),
        P("mp", "dp", None),
        P("mp", "dp", None),
        P("mp", "dp", None),
        P(),
        P(),
        P(),
        P(),
        P(),
        P(),
        P(),
        P(),
    )
    return jax.shard_map(body, mesh=mesh, in_specs=in_specs, out_specs=out_specs, check_vma=False)
```

```python
import functools
import math

import jax
import jax.numpy as jnp
from jax import lax
from jax.experimental import pallas as pl
from jax.experimental.pallas import tpu as pltpu
from jax.sharding import PartitionSpec as P

bf16, f32 = jnp.bfloat16, jnp.float32
CONV, DT_RANK, SUBT, NST = 4, 72, 16, 16
LOG2E = 1.0 / math.log(2.0)
LANES = 128
BLOCK = 256
CAP = 192
EPSILON = 1e-05
MOMENT = 0.9
SMOOTH = 0.6
LEARNING = (0.02, 0.03, 0.4, 0.3, 0.04, 0.07, 0.3, 0.3, 0.01)
HIGHEST = lax.Precision.HIGHEST
MIB = 2**20
SHAPE = jax.ShapeDtypeStruct


def dotf(a, b, dims=((1,), (0,))):
    return lax.dot_general(a, b, (dims, ((), ())), preferred_element_type=f32)


def block_mask():
    r = lax.broadcasted_iota(jnp.int32, (SUBT, SUBT * NST), 0)
    c = lax.broadcasted_iota(jnp.int32, (SUBT, SUBT * NST), 1)
    return (c // NST == r).astype(f32)


def spread(first, rows):
    r = lax.broadcasted_iota(jnp.int32, (rows, SUBT * NST), 0)
    c = lax.broadcasted_iota(jnp.int32, (rows, SUBT * NST), 1)
    return (c % NST + first == r).astype(bf16)


def soft_parts(x):
    e = jnp.exp(-jnp.abs(x))
    return jnp.maximum(x, 0.0) + jnp.log1p(e), jnp.where(x >= 0, 1.0, e) / (1.0 + e)


def row8(ref, k, t):
    d = ref[k, pl.ds(t, 8, stride=0), :]
    return jnp.concatenate([d, d], 0)


def split_states(sel_ref, bts, cts, T):
    selT = sel_ref[...].T
    for k in range(T // SUBT):
        bts[k] = selT[DT_RANK : DT_RANK + NST, SUBT * k : SUBT * k + SUBT]
        cts[k] = selT[DT_RANK + NST : DT_RANK + 2 * NST, SUBT * k : SUBT * k + SUBT]


def blocked(sel_ref, k, place, mask):
    sel = sel_ref[pl.ds(pl.multiple_of(k * SUBT, SUBT), SUBT), :]
    return (dotf(sel.astype(bf16), place) * mask).astype(bf16)


def blocked_all(sel_ref, place, T):
    r = lax.broadcasted_iota(jnp.int32, (T, SUBT * NST), 0)
    c = lax.broadcasted_iota(jnp.int32, (T, SUBT * NST), 1)
    flat = jnp.where(c // NST == r % SUBT, dotf(sel_ref[...].astype(bf16), place), 0.0)
    return flat.astype(bf16).reshape(T // SUBT, SUBT, SUBT * NST)


def rows_at(T, w, first=0):
    return pl.BlockSpec((T, w), lambda i: (first + i, 0))


def rows_back(T, w, last):
    return pl.BlockSpec((T, w), lambda i: (last - i, 0))


def whole(shape):
    shape = tuple(shape)
    return pl.BlockSpec(shape, lambda i: (0,) * len(shape))


def params(mib):
    return pltpu.CompilerParams(vmem_limit_bytes=mib * MIB)


def cost(flops=0, moved=1 << 20):
    return pl.CostEstimate(flops=flops, bytes_accessed=moved, transcendentals=0)


def turned(a):
    short = -a.shape[1] % LANES
    if short:
        a = jnp.concatenate([a, jnp.zeros((a.shape[0], short), f32)], axis=1)
    return a.T


def prep_kernel(in_ref, sel_ref, delta_ref, chan_ref, out_ref, a_ref, b_ref, *, half):
    own = sel_ref.shape[0]
    xw, vrows = sel_ref.shape[1], chan_ref.shape[0]
    width = in_ref.shape[2]
    a_ref[:, 0:width] = in_ref[0].astype(bf16)
    a_ref[:, width:] = out_ref[:, 0:half].astype(bf16)
    small = jnp.concatenate(
        [
            delta_ref[...],
            chan_ref[...],
            jnp.zeros((LANES - DT_RANK - vrows, own), f32),
        ],
        axis=0,
    )
    select = jnp.concatenate([sel_ref[...], jnp.zeros((own, LANES - xw), f32)], axis=1)
    b_ref[:, 0:width] = in_ref[1].astype(bf16)
    b_ref[:, width : width + LANES] = select.astype(bf16)
    b_ref[:, width + LANES : width + 2 * LANES] = turned(small)[0:own].astype(bf16)
    b_ref[:, width + 2 * LANES :] = out_ref[:, half:].astype(bf16)


def prep(inward, select, delta, channel, outward, half):
    own, width = outward.shape
    return pl.pallas_call(
        functools.partial(prep_kernel, half=half),
        out_shape=[SHAPE((own, width + half), bf16), SHAPE((own, 2 * width - half + 2 * LANES), bf16)],
        compiler_params=params(40),
        cost_estimate=cost(),
    )(inward, select, delta, channel, outward)


def prep_experts_kernel(up_ref, down_ref, both_ref):
    units = down_ref.shape[0]
    both_ref[0:units, :] = turned(up_ref[...])[0:units].astype(bf16)
    both_ref[units : 2 * units, :] = down_ref[...].astype(bf16)


def prep_experts(up, down):
    return pl.pallas_call(
        prep_experts_kernel,
        out_shape=SHAPE((2 * down.shape[0], down.shape[1]), bf16),
        compiler_params=params(40),
        cost_estimate=cost(),
    )(up, down)


def mixer_weights_kernel(owner_ref, *refs, ring, own, slot, width, half):
    a, b = refs[:ring], refs[ring : 2 * ring]
    w_ref, selw_ref, delta_ref, chan_ref, out_ref, small = refs[2 * ring :]
    wide = selw_ref.shape[0]
    if wide > ring * slot:
        for ref in (w_ref, selw_ref, out_ref, small):
            ref[...] = jnp.zeros_like(ref)

    def place(ref, at, value):
        if slot > own:
            value = jnp.concatenate([value, jnp.zeros((slot - own, value.shape[1]), value.dtype)], axis=0)
        ref[pl.ds(pl.multiple_of(at, 16), slot), :] = value

    for r in range(ring):
        at = owner_ref[r] * slot
        place(w_ref, at, a[r][:, 0:width])
        place(w_ref, wide + at, b[r][:, 0:width])
        place(selw_ref, at, b[r][:, width : width + LANES])
        place(small, at, b[r][:, width + LANES : width + 2 * LANES].astype(f32))
        place(out_ref, at, jnp.concatenate([a[r][:, width:], b[r][:, width + 2 * LANES :]], axis=1))
    flat = small[...].T
    delta_ref[0:DT_RANK, :] = flat[0:DT_RANK].astype(bf16)
    delta_ref[DT_RANK:LANES, :] = jnp.zeros((LANES - DT_RANK, wide), bf16)
    chan_ref[...] = flat[DT_RANK : DT_RANK + chan_ref.shape[0]]


def mixer_weights(owners, a, b, slot, wide, width, half):
    ring = len(a)
    own = b[0].shape[0]
    return pl.pallas_call(
        functools.partial(mixer_weights_kernel, ring=ring, own=own, slot=slot, width=width, half=half),
        in_specs=[pl.BlockSpec(memory_space=pltpu.SMEM)] + [pl.BlockSpec(memory_space=pltpu.VMEM)] * (2 * ring),
        out_shape=[
            SHAPE((2 * wide, width), bf16),
            SHAPE((wide, LANES), bf16),
            SHAPE((LANES, wide), bf16),
            SHAPE((24, wide), f32),
            SHAPE((wide, width), bf16),
        ],
        scratch_shapes=[pltpu.VMEM((wide, LANES), f32)],
        compiler_params=params(48),
        cost_estimate=cost(),
    )(owners, *a, *b)


def conv_fwd_kernel(seq_ref, w_ref, chan_ref, selw_ref, tail_ref, conv_ref, gate_ref, pre_ref, act_ref, actb_ref, sel_ref, end_ref, buf, *, T):
    C = conv_ref.shape[1]

    @pl.when(pl.program_id(0) == 0)
    def _():
        buf[0:8, :] = tail_ref[...]

    seq = seq_ref[...]
    conv = dotf(seq, w_ref[0:C, :], ((1,), (1,)))
    gate_ref[...] = dotf(seq, w_ref[C : 2 * C, :], ((1,), (1,)))
    conv_ref[...] = conv
    buf[8 : 8 + T, :] = conv
    pre = chan_ref[CONV : CONV + 1, :] + chan_ref[CONV - 1 : CONV, :] * conv
    for tap in range(CONV - 1):
        at = 8 - CONV + 1 + tap
        pre = pre + chan_ref[tap : tap + 1, :] * buf[at : at + T, :]
    buf[0:8, :] = buf[T : T + 8, :]
    end_ref[...] = buf[0:8, :]
    pre_ref[...] = pre
    act = pre / (1.0 + jnp.exp(-pre))
    act_ref[...] = act
    actb = act.astype(bf16)
    actb_ref[...] = actb
    sel_ref[...] = dotf(actb, selw_ref[...])


def conv_fwd(seq, first, count, w_in, chan, selw, tail, T=BLOCK):
    C, D = chan.shape[1], seq.shape[1]
    return pl.pallas_call(
        functools.partial(conv_fwd_kernel, T=T),
        grid=(count // T,),
        in_specs=[rows_at(T, D, first // T), whole(w_in.shape), whole(chan.shape), whole(selw.shape), whole(tail.shape)],
        out_specs=[rows_at(T, C)] * 5 + [rows_at(T, LANES), whole((8, C))],
        out_shape=[SHAPE((count, C), f32)] * 4 + [SHAPE((count, C), bf16), SHAPE((count, LANES), f32), SHAPE((8, C), f32)],
        scratch_shapes=[pltpu.VMEM((T + 8, C), f32)],
        compiler_params=params(48),
        cost_estimate=cost(),
    )(seq, w_in, chan, selw, tail)


def scan_fwd_kernel(
    sel_ref, delta_w_ref, act_ref, gate_ref, chan_ref, out_w_ref, start_ref,
    s_ref, xlin_ref, scanned_ref, gated_ref, mix_ref, rank_ref, end_ref,
    state, dscr, uscr, yscr, bts, cts, blocks, sA, sB, *, T
):
    C = act_ref.shape[1]
    NCH = T // SUBT

    @pl.when(pl.program_id(0) == 0)
    def _():
        state[...] = start_ref[...]

    rank = sel_ref[...].astype(bf16)
    rank_ref[...] = rank
    x = dotf(rank, delta_w_ref[...]) + chan_ref[CONV + 1 : CONV + 2, :]
    xlin_ref[...] = x
    sp, _ = soft_parts(x)
    dscr[...] = sp.reshape(NCH, SUBT, C)
    uscr[...] = (sp * act_ref[...]).reshape(NCH, SUBT, C)
    split_states(sel_ref, bts, cts, T)
    nrate = -LOG2E * jnp.exp(chan_ref[CONV + 3 : CONV + 3 + NST, :])
    blocks[...] = blocked_all(sel_ref, spread(DT_RANK + NST, LANES), T)

    def one(k, S, cur, prev):
        before = jnp.maximum(k - 1, 0)
        yv = dotf(blocks[before], prev[...])
        bt = bts[k]
        for t in range(SUBT):
            d = row8(dscr, k, t)
            u = row8(uscr, k, t)
            S = jnp.exp2(d * nrate) * S + u * jnp.broadcast_to(bt[:, t : t + 1], (NST, C))
            rounded = S.astype(bf16)
            cur[t * NST : t * NST + NST, :] = rounded
            s_ref[k, t * NST : t * NST + NST, :] = rounded
        yscr[before] = yv
        return S

    def pair(j, S):
        S = one(2 * j, S, sA, sB)
        return one(2 * j + 1, S, sB, sA)

    sB[...] = jnp.zeros_like(sB)
    state[...] = lax.fori_loop(0, NCH // 2, pair, state[...])
    end_ref[...] = state[...]
    yscr[NCH - 1] = dotf(blocks[NCH - 1], sB[...])
    scanned = yscr[...].reshape(T, C) + chan_ref[CONV + 2 : CONV + 3, :] * act_ref[...]
    scanned_ref[...] = scanned
    g = gate_ref[...]
    gated = (scanned * (g / (1.0 + jnp.exp(-g)))).astype(bf16)
    gated_ref[...] = gated
    mix_ref[...] = dotf(gated, out_w_ref[...]).astype(mix_ref.dtype)


def scan_fwd(sel, delta_w, act, gate, chan, out_w, start, T=BLOCK):
    N, C = act.shape
    W = out_w.shape[1]
    g, nch = N // T, T // SUBT
    vm = pltpu.VMEM
    return pl.pallas_call(
        functools.partial(scan_fwd_kernel, T=T),
        grid=(g,),
        in_specs=[rows_at(T, LANES), whole(delta_w.shape), rows_at(T, C), rows_at(T, C), whole(chan.shape), whole(out_w.shape), whole(start.shape)],
        out_specs=[pl.BlockSpec((nch, SUBT * NST, C), lambda i: (i, 0, 0))] + [rows_at(T, C)] * 3 + [rows_at(T, W), rows_at(T, LANES), whole((NST, C))],
        out_shape=[
            SHAPE((N // SUBT, SUBT * NST, C), bf16), SHAPE((N, C), f32), SHAPE((N, C), f32), SHAPE((N, C), bf16),
            SHAPE((N, W), bf16), SHAPE((N, LANES), bf16), SHAPE((NST, C), f32),
        ],
        scratch_shapes=[vm((NST, C), f32)] + [vm((nch, SUBT, C), f32)] * 3 + [vm((nch, NST, SUBT), f32)] * 2 + [vm((nch, SUBT, SUBT * NST), bf16)] + [vm((SUBT * NST, C), bf16)] * 2,
        compiler_params=params(48),
        cost_estimate=cost(),
    )(sel, delta_w, act, gate, chan, out_w, start)


def gather_states(first):
    r = lax.broadcasted_iota(jnp.int32, (SUBT * NST, LANES), 0)
    c = lax.broadcasted_iota(jnp.int32, (SUBT * NST, LANES), 1)
    return (r % NST + first == c).astype(bf16)


def fold(a):
    return sum(a[:, i : i + LANES] for i in range(LANES, a.shape[1], LANES)) + a[:, 0:LANES]


def scan_bwd_kernel(
    dmix_ref, out_w_ref, s_ref, before_ref, edge_ref, act_ref, gate_ref, xlin_ref, scanned_ref, sel_ref, chan_ref, delta_w_ref, q_ref,
    dgate_ref, dact_ref, ddl_ref, dsel_ref, gch_ref, qend_ref,
    qscr, dscr, uscr, dyscr, lbscr, wsscr, bts, cts, blocks, rows_b, rows_c, *bufs, T, g, opens
):
    C = act_ref.shape[1]
    NCH = T // SUBT
    step = pl.program_id(0)

    @pl.when(step == 0)
    def _():
        qscr[...] = q_ref[...]
        gch_ref[...] = jnp.zeros_like(gch_ref)

    dg = dotf(dmix_ref[...], out_w_ref[...], ((1,), (1,)))
    gt = gate_ref[...]
    sg = 1.0 / (1.0 + jnp.exp(-gt))
    dgate_ref[...] = (dg * scanned_ref[...] * (sg * (1.0 + gt * (1.0 - sg)))).astype(bf16)
    dy = dg * (gt * sg)
    act = act_ref[...]
    sp, sigd = soft_parts(xlin_ref[...])
    dscr[...] = sp.reshape(NCH, SUBT, C)
    uscr[...] = (sp * act).reshape(NCH, SUBT, C)
    dyscr[...] = dy.reshape(NCH, SUBT, C)
    split_states(sel_ref, bts, cts, T)
    nrate = -LOG2E * jnp.exp(chan_ref[CONV + 3 : CONV + 3 + NST, :])
    mask = block_mask()
    eb = spread(DT_RANK, LANES)
    half_rows = lax.broadcasted_iota(jnp.int32, (SUBT, SUBT * NST // 2), 0)
    half_cols = lax.broadcasted_iota(jnp.int32, (SUBT, SUBT * NST // 2), 1)
    halves = (half_cols // (NST // 2) == half_rows).astype(bf16)
    ones = jnp.ones((SUBT, LANES), bf16)
    last = slice(SUBT * NST - NST, SUBT * NST)
    first = before_ref[0, last, :].astype(f32)
    if opens:
        first = jnp.where(step == g - 1, edge_ref[...], first)

    def lanes_summed(partial):
        return (dotf(ones, partial[...].astype(bf16), ((1,), (1,))) * mask).astype(bf16)

    blocks[...] = blocked_all(sel_ref, eb, T)

    def one(k, q, acc, cur, prev):
        kp = jnp.minimum(k + 1, NCH - 1)
        lam_ref, w_ref, pb_ref, pc_ref = prev
        lamb = dotf(blocks[kp], lam_ref[...])
        wsum = dotf(halves, w_ref[...])
        sum_b, sum_c = lanes_summed(pb_ref), lanes_summed(pc_ref)
        lam_ref, w_ref, pb_ref, pc_ref = cur
        bt = bts[k]
        ct = cts[k]
        s_t = s_ref[k, last, :].astype(f32)
        s_before = jnp.where(k == 0, first, s_ref[jnp.maximum(k - 1, 0), last, :].astype(f32))
        held = None
        for t in range(SUBT - 1, -1, -1):
            d = row8(dscr, k, t)
            u = row8(uscr, k, t)
            dyr = row8(dyscr, k, t)
            lam = jnp.broadcast_to(ct[:, t : t + 1], (NST, C)) * dyr + q
            lam_ref[t * NST : t * NST + NST, :] = lam.astype(bf16)
            q = jnp.exp2(d * nrate) * lam
            pc_ref[t * NST : t * NST + NST, :] = fold(s_t * dyr)
            pb_ref[t * NST : t * NST + NST, :] = fold(lam * u)
            s_p = s_ref[k, t * NST - NST : t * NST, :].astype(f32) if t > 0 else s_before
            wr = q * s_p * nrate
            part = wr[0 : NST // 2] + wr[NST // 2 :]
            if t % 2:
                held = part
            else:
                w_ref[t * NST // 2 : t * NST // 2 + NST, :] = jnp.concatenate([part, held], axis=0).astype(bf16)
            acc = acc + wr * d
            s_t = s_p
        lbscr[kp] = lamb
        wsscr[kp] = wsum
        rows_b[kp] = sum_b
        rows_c[kp] = sum_c
        return q, acc

    def pair(j, carry):
        k = NCH - 1 - 2 * j
        carry = one(k, *carry, bufs[0:4], bufs[4:8])
        return one(k - 1, *carry, bufs[4:8], bufs[0:4])

    for ref in bufs[4:8]:
        ref[...] = jnp.zeros_like(ref)
    q, acc = lax.fori_loop(0, NCH // 2, pair, (qscr[...], jnp.zeros((NST, C), f32)))
    lam_ref, w_ref, pb_ref, pc_ref = bufs[4:8]
    lbscr[0] = dotf(blocks[0], lam_ref[...])
    wsscr[0] = dotf(halves, w_ref[...])
    rows_b[0] = lanes_summed(pb_ref)
    rows_c[0] = lanes_summed(pc_ref)
    qscr[...] = q
    qend_ref[...] = q
    gch_ref[CONV + 3 : CONV + 3 + NST, :] += acc * (1.0 / LOG2E)
    lamB = lbscr[...].reshape(T, C)
    ws = wsscr[...].reshape(T, C) * (-1.0 / LOG2E)
    dyf = dyscr[...].reshape(T, C)
    spf = dscr[...].reshape(T, C)
    dact_ref[...] = chan_ref[CONV + 2 : CONV + 3, :] * dyf + spf * lamB
    ddl = (act * lamB - ws) * sigd
    ddl_ref[...] = ddl.astype(bf16)
    gch_ref[CONV + 1 : CONV + 2, :] += jnp.sum(ddl, axis=0, keepdims=True)
    gch_ref[CONV + 2 : CONV + 3, :] += jnp.sum(dyf * act, axis=0, keepdims=True)
    flat = lambda ref: ref[...].reshape(T, SUBT * NST)
    dsel = dotf(ddl_ref[...], delta_w_ref[...], ((1,), (1,)))
    dsel = dsel + dotf(flat(rows_b), gather_states(DT_RANK)) + dotf(flat(rows_c), gather_states(DT_RANK + NST))
    dsel_ref[...] = dsel.astype(bf16)


def scan_bwd(dmix, at, half, kept, edge, q, count, out_w, sel, chan, delta_w, T=BLOCK):
    s_all, act, gate, xlin, scanned = kept
    C = act.shape[1]
    g, nch = count // T, T // SUBT
    low = half // T
    row = lambda w: rows_back(T, w, low + g - 1)
    out = lambda w: rows_back(T, w, g - 1)
    vm = pltpu.VMEM
    return pl.pallas_call(
        functools.partial(scan_bwd_kernel, T=T, g=g, opens=low == 0),
        grid=(g,),
        in_specs=[
            rows_back(T, dmix.shape[1], at // T + g - 1), whole(out_w.shape),
            pl.BlockSpec((nch, SUBT * NST, C), lambda i: (low + g - 1 - i, 0, 0)),
            pl.BlockSpec((1, SUBT * NST, C), lambda i: (jnp.maximum((low + g - 1 - i) * nch - 1, 0), 0, 0)),
            whole(edge.shape),
            row(C), row(C), row(C), row(C), row(LANES), whole(chan.shape), whole(delta_w.shape), whole(q.shape),
        ],
        out_specs=[out(C), out(C), out(C), out(LANES), whole((24, C)), whole((NST, C))],
        out_shape=[
            SHAPE((count, C), bf16), SHAPE((count, C), f32), SHAPE((count, C), bf16), SHAPE((count, LANES), bf16),
            SHAPE((24, C), f32), SHAPE((NST, C), f32),
        ],
        scratch_shapes=[vm((NST, C), f32)] + [vm((nch, SUBT, C), f32)] * 5 + [vm((nch, NST, SUBT), f32)] * 2 + [vm((nch, SUBT, SUBT * NST), bf16)] * 3
        + [vm((SUBT * NST, C), bf16), vm((SUBT * NST // 2, C), bf16), vm((SUBT * NST, LANES), f32), vm((SUBT * NST, LANES), f32)] * 2,
        compiler_params=params(56),
        cost_estimate=cost(),
    )(dmix, out_w, s_all, s_all, edge, act, gate, xlin, scanned, sel, chan, delta_w, q)


def conv_bwd_kernel(
    dact_ref, dsel_ref, selw_ref, pre_ref, conv_ref, dgate_ref, w_ref, seq_ref, chan_ref, next_ref,
    actb_ref, ddl_ref, rank_ref, before_ref, gchin_ref, tail_ref,
    dnorm_ref, gain_ref, head_ref, gch_ref, grad_ref, buf, acc, *, T, g, opens, final
):
    C, D = conv_ref.shape[1], seq_ref.shape[1]
    step = pl.program_id(0)

    @pl.when(step == 0)
    def _():
        buf[T : T + 8, :] = next_ref[...]
        gain_ref[...] = jnp.zeros_like(gain_ref)
        if opens:
            gch_ref[...] = jnp.zeros_like(gch_ref)
            acc[...] = jnp.zeros_like(acc)
        else:
            gch_ref[...] = gchin_ref[...]
            acc[...] = before_ref[...]

    pre = pre_ref[...]
    sig = 1.0 / (1.0 + jnp.exp(-pre))
    dsel = dsel_ref[...]
    dact = dact_ref[...] + dotf(dsel, selw_ref[...], ((1,), (1,)))
    dpre = dact * (sig * (1.0 + pre * (1.0 - sig)))
    buf[0:T, :] = dpre
    conv = conv_ref[...]
    total = chan_ref[CONV - 1 : CONV, :] * dpre
    gch_ref[CONV - 1 : CONV, :] += jnp.sum(conv * dpre, axis=0, keepdims=True)
    for tap in range(CONV - 1):
        later = buf[CONV - 1 - tap : CONV - 1 - tap + T, :]
        total = total + chan_ref[tap : tap + 1, :] * later
        gch_ref[tap : tap + 1, :] += jnp.sum(conv * later, axis=0, keepdims=True)
    gch_ref[CONV : CONV + 1, :] += jnp.sum(dpre, axis=0, keepdims=True)
    buf[T : T + 8, :] = buf[0:8, :]
    head_ref[...] = buf[0:8, :]
    dconv = total.astype(bf16)
    seq = seq_ref[...]
    rows = ((0,), (0,))
    acc[:, 0:D] += dotf(dconv, seq, rows)
    acc[:, D : D + LANES] += dotf(actb_ref[...], dsel, rows)
    keep = lax.broadcasted_iota(jnp.int32, (T, LANES), 1) < DT_RANK
    rank = jnp.where(keep, rank_ref[...].astype(f32), 0.0).astype(bf16)
    acc[:, D + LANES :] += dotf(ddl_ref[...], rank, rows)
    dnorm = dotf(dconv, w_ref[0:C, :]) + dotf(dgate_ref[...], w_ref[C : 2 * C, :])
    dnorm_ref[...] = dnorm.astype(bf16)
    gain_ref[0:1, :] += jnp.sum(dnorm * seq.astype(f32), axis=0, keepdims=True)

    @pl.when(step == g - 1)
    def _():
        if final:
            taps = jnp.where(lax.broadcasted_iota(jnp.int32, (8, C), 0) <= CONV, gch_ref[...], tail_ref[0:8, :])
            side = jnp.concatenate(
                [jnp.zeros((DT_RANK, C), f32), taps, tail_ref[8:, :], jnp.zeros((LANES - DT_RANK - 24, C), f32)], axis=0
            )
            acc[:, D + LANES :] += side.T
        grad_ref[...] = acc[...].astype(grad_ref.dtype)


def conv_bwd(at, count, final, dact, dsel, selw, pre, conv, dgate, w_in, seq, chan, later, actb, ddl, rank, before, gch, tail, T=BLOCK):
    C, D = conv.shape[1], seq.shape[1]
    g = count // T
    opens = before is None
    own = lambda w: rows_back(T, w, g - 1)
    packed = SHAPE((C, D + 2 * LANES), bf16 if final else f32)
    return pl.pallas_call(
        functools.partial(conv_bwd_kernel, T=T, g=g, opens=opens, final=final),
        grid=(g,),
        in_specs=[
            own(C), own(LANES), whole(selw.shape), own(C), own(C), own(C), whole(w_in.shape),
            rows_back(T, D, at // T + g - 1), whole(chan.shape), whole(later.shape),
            own(C), own(C), own(LANES), whole((8, LANES) if opens else before.shape), whole(gch.shape), whole(tail.shape),
        ],
        out_specs=[own(D), whole((8, D)), whole((8, C)), whole((8, C)), whole(packed.shape)],
        out_shape=[SHAPE((count, D), bf16), SHAPE((8, D), f32), SHAPE((8, C), f32), SHAPE((8, C), f32), packed],
        scratch_shapes=[pltpu.VMEM((T + 8, C), f32), pltpu.VMEM(packed.shape, f32)],
        compiler_params=params(56),
        cost_estimate=cost(),
    )(dact, dsel, selw, pre, conv, dgate, w_in, seq, chan, later, actb, ddl, rank, jnp.zeros((8, LANES), f32) if opens else before, gch, tail)


def as_column(row, count):
    return jnp.broadcast_to(row[0:1, :], (LANES, count)).T[:, 0:1]


def as_rows(column, count):
    return jnp.broadcast_to(column, (count, LANES)).T[0:8, :]


def experts_kernel(x0, x1, x2, x3, c0, c1, c2, c3, prob_ref, w_ref, out_ref, drow_ref, dot_ref, g_ref, acc_out, acc_row, x_ref, dz_ref, xt_ref, dzt_ref, *, steps, per, units):
    R = x_ref.shape[0]

    @pl.when(pl.program_id(0) == 0)
    def _():
        acc_out[...] = jnp.zeros_like(acc_out)
        acc_row[...] = jnp.zeros_like(acc_row)
        x_ref[...] = jnp.concatenate([x0[...], x1[...], x2[...], x3[...]], axis=0)
        cot = jnp.concatenate([c0[...], c1[...], c2[...], c3[...]], axis=0)
        dz = as_column(prob_ref[...], R) * cot.astype(f32)
        dz_ref[...] = dz.astype(bf16)
        dzt_ref[...] = dz.T.astype(bf16)
        xt_ref[...] = x_ref[...].astype(f32).T.astype(bf16)

    up = jnp.concatenate([w_ref[2 * r * units : (2 * r + 1) * units, :] for r in range(per)], axis=0)
    down = jnp.concatenate([w_ref[(2 * r + 1) * units : (2 * r + 2) * units, :] for r in range(per)], axis=0)
    lin = dotf(up, xt_ref[...])
    cdf = 0.5 * (1.0 + lax.erf(lin * math.sqrt(0.5)))
    act = (lin * cdf).astype(bf16)
    slope = cdf + lin * jnp.exp(-0.5 * lin * lin) * (1.0 / math.sqrt(2.0 * math.pi))
    dlin = (dotf(down, dzt_ref[...]) * slope).astype(bf16)
    gdown = dotf(act, dz_ref[...]).astype(bf16)
    gup = dotf(dlin, x_ref[...]).astype(bf16)
    acc_out[...] += dotf(act, down, ((0,), (0,)))
    acc_row[...] += dotf(dlin, up, ((0,), (0,)))
    for r in range(per):
        g_ref[2 * r * units : (2 * r + 1) * units, :] = gup[r * units : (r + 1) * units]
        g_ref[(2 * r + 1) * units : (2 * r + 2) * units, :] = gdown[r * units : (r + 1) * units]

    @pl.when(pl.program_id(0) == steps - 1)
    def _():
        out = acc_out[...].astype(bf16)
        out_ref[...] = out
        drow_ref[...] = acc_row[...].astype(bf16)
        dot_ref[...] = as_rows(jnp.sum(out.astype(f32) * dz_ref[...].astype(f32), axis=1, keepdims=True), R)


def experts(x, cot, prob, w, units, per=2):
    R, D = len(x) * x[0].shape[0], x[0].shape[1]
    block = 2 * units * per
    steps = w.shape[0] // block
    fix = whole((R, D))
    mov = rows_at(block, D)
    return pl.pallas_call(
        functools.partial(experts_kernel, steps=steps, per=per, units=units),
        grid=(steps,),
        in_specs=[whole(x[0].shape)] * 8 + [whole(prob.shape), mov],
        out_specs=[fix, fix, whole((8, R)), mov],
        out_shape=[SHAPE((R, D), bf16)] * 2 + [SHAPE((8, R), f32), SHAPE(w.shape, bf16)],
        scratch_shapes=[pltpu.VMEM((R, D), f32)] * 2 + [pltpu.VMEM((R, D), bf16)] * 2 + [pltpu.VMEM((D, R), bf16)] * 2,
        compiler_params=params(60),
        cost_estimate=cost(),
    )(*x, *cot, prob, w)


def mean_scale(values):
    return lax.rsqrt(jnp.mean(values * values, axis=-1, keepdims=True) + EPSILON)


def dot32(a, b, dims):
    return lax.dot_general(a, b, (dims, ((), ())), precision=HIGHEST, preferred_element_type=f32)


def route_kernel(src_ref, near_ref, far_ref, gain_ref, router_ref, ids_ref, row_ref, col_ref, res_ref, prob_ref, gate_ref, out_ref, slotp_ref, *, count):
    res = src_ref[...].astype(f32) + near_ref[...] + far_ref[...].astype(f32)
    res_ref[...] = res
    normed = res * mean_scale(res) * gain_ref[1:2, :]
    T, S = res.shape[0], out_ref.shape[0]
    logits = dot32(normed, router_ref[...], ((1,), (0,)))
    lane = lax.broadcasted_iota(jnp.int32, (T, LANES), 1)
    logits = jnp.where(lane < count, logits, -jnp.inf)
    e = jnp.exp(logits - jnp.max(logits, axis=1, keepdims=True))
    probs = e / jnp.sum(e, axis=1, keepdims=True)
    prob_ref[...] = probs
    gate = jnp.sum(jnp.where(lane == ids_ref[...], probs, 0.0), axis=1, keepdims=True)
    gate_ref[...] = jnp.broadcast_to(gate, (T, LANES))
    take = (lax.broadcasted_iota(jnp.int32, (S, T), 0) == row_ref[...]).astype(bf16)
    out_ref[...] = dotf(take, normed.astype(bf16)).astype(bf16)
    put = lax.broadcasted_iota(jnp.int32, (T, S), 1) == col_ref[...]
    slotp_ref[...] = jnp.broadcast_to(jnp.sum(jnp.where(put, gate, 0.0), axis=0, keepdims=True), (8, S))


def route_tokens(source, near, far, gains, router, ids, row, col, slots, count):
    T, D = source.shape
    return pl.pallas_call(
        functools.partial(route_kernel, count=count),
        out_shape=[SHAPE((T, D), f32), SHAPE((T, LANES), f32), SHAPE((T, LANES), f32), SHAPE((slots, D), bf16), SHAPE((8, slots), f32)],
        compiler_params=params(48),
        cost_estimate=cost(),
    )(source, near, far, gains, router, ids, row, col)


def back_kernel(r0, r1, r2, r3, dot_ref, col_ref, ids_ref, prob_ref, router_ref, res_ref, cot_ref, gain_ref, dres_ref, dmix_ref, part_ref, *, count):
    res = res_ref[...]
    T, S = res.shape[0], dot_ref.shape[1]
    rows = jnp.concatenate([r0[...], r1[...], r2[...], r3[...]], axis=0)
    put = lax.broadcasted_iota(jnp.int32, (T, S), 1) == col_ref[...]
    lane = lax.broadcasted_iota(jnp.int32, (T, LANES), 1)
    weighted = jnp.sum(jnp.where(put, dot_ref[0:1, :], 0.0), axis=1, keepdims=True)
    dlog = weighted * (jnp.where(lane == ids_ref[...], 1.0, 0.0) - prob_ref[...])
    dnorm = dotf(put.astype(bf16), rows) + dot32(dlog, router_ref[...], ((1,), (1,)))
    scale = mean_scale(res)
    hat = res * scale
    part_ref[0:8, :] = jnp.broadcast_to(jnp.sum(dnorm * hat, axis=0, keepdims=True), (8, res.shape[1]))
    part_ref[8:, :] = dot32(dlog, hat * gain_ref[1:2, :], ((0,), (0,)))[0 : part_ref.shape[0] - 8]
    a = gain_ref[1:2, :] * dnorm
    dres = cot_ref[...].astype(f32) + scale * (a - hat * jnp.mean(a * hat, axis=-1, keepdims=True))
    dres_ref[...] = dres
    dmix_ref[...] = dres.astype(bf16)


def back_tokens(rows, dots, col, ids, probs, router, res, cot, gains, count):
    T, D = res.shape
    return pl.pallas_call(
        functools.partial(back_kernel, count=count),
        out_shape=[SHAPE((T, D), f32), SHAPE((T, D), bf16), SHAPE((16, D), f32)],
        compiler_params=params(48),
        cost_estimate=cost(),
    )(*rows, dots, col, ids, probs, router, res, cot, gains)


def step_of(refs, outs, grad, rate, factor, at=Ellipsis):
    weight, velocity, average = (ref[at] for ref in refs)
    g = grad * factor
    momentum = MOMENT * velocity + g
    new = weight - rate * (g + MOMENT * momentum)
    outs[0][at] = new
    outs[1][at] = momentum
    outs[2][at] = SMOOTH * average + (1.0 - SMOOTH) * new
    outs[3][at] = new.astype(bf16)


def upright(a, rows, columns):
    a = a.astype(f32)
    short = -a.shape[0] % LANES
    if short:
        a = jnp.concatenate([a, jnp.zeros((short, a.shape[1]), f32)], axis=0)
    return a.T[0:rows, 0:columns]


def mixer_step_kernel(*refs, factor, own, width, xw, vrows):
    conv_ref, gate_ref, outg_ref = refs[:3]
    ins = [refs[4 + 3 * p : 7 + 3 * p] for p in range(5)]
    outs = [refs[19 + 4 * p : 23 + 4 * p] for p in range(5)]
    inward, select, delta, channel, outward = range(5)
    step_of(ins[inward], outs[inward], conv_ref[0:own, 0:width].astype(f32), LEARNING[0], factor, 0)
    step_of(ins[inward], outs[inward], gate_ref[0:own, :].astype(f32), LEARNING[0], factor, 1)
    at = width
    step_of(ins[select], outs[select], conv_ref[0:own, at : at + LANES].astype(f32)[:, 0:xw], LEARNING[1], factor)
    rest = upright(conv_ref[:, at + LANES : at + 2 * LANES], LANES, own)
    step_of(ins[delta], outs[delta], rest[0:DT_RANK], LEARNING[2], factor)
    step_of(ins[channel], outs[channel], rest[DT_RANK : DT_RANK + vrows], LEARNING[3], factor)
    step_of(ins[outward], outs[outward], outg_ref[0:own, :].astype(f32), LEARNING[4], factor)


def mixer_step(conv, gate, outg, last, triples, factor):
    own, width = triples[4][0].shape
    xw, vrows = triples[1][0].shape[1], triples[3][0].shape[0]
    shapes = []
    for triple in triples:
        shapes += [SHAPE(triple[0].shape, f32)] * 3 + [SHAPE(triple[0].shape, bf16)]
    flat = pl.pallas_call(
        functools.partial(mixer_step_kernel, factor=factor, own=own, width=width, xw=xw, vrows=vrows),
        out_shape=shapes,
        compiler_params=params(56),
        cost_estimate=cost(),
    )(conv, gate, outg, last, *[a for triple in triples for a in triple])
    return [flat[4 * p : 4 * p + 4] for p in range(5)]


def experts_step_kernel(gup_ref, gdown_ref, *refs, factor):
    ups, downs = refs[0:3], refs[3:6]
    rows, columns = ups[0].shape[1:]
    step_of(ups, refs[6:10], upright(gup_ref[...], rows, columns), LEARNING[5], factor, 0)
    step_of(downs, refs[10:14], gdown_ref[...].astype(f32), LEARNING[6], factor, 0)


def experts_step(grads, ups, downs, factor):
    _, D, units = ups[0].shape
    block = LANES if units % LANES == 0 else units
    n = units // block
    up = pl.BlockSpec((1, D, block), lambda i: (0, 0, i))
    down = pl.BlockSpec((1, block, D), lambda i: (0, i, 0))
    shapes = lambda a: [SHAPE(a.shape, f32)] * 3 + [SHAPE(a.shape, bf16)]
    flat = pl.pallas_call(
        functools.partial(experts_step_kernel, factor=factor),
        grid=(n,),
        in_specs=[rows_at(block, D), rows_at(block, D, n)] + [up] * 3 + [down] * 3,
        out_specs=[up] * 4 + [down] * 4,
        out_shape=shapes(ups[0]) + shapes(downs[0]),
        compiler_params=params(48),
        cost_estimate=cost(),
    )(grads, grads, *ups, *downs)
    return list(flat[:4]), list(flat[4:])


START, PIECES = 5, 4


def contract_rows(left, right):
    return dotf(left, right, ((0,), (0,)))


def tie(*values):
    return lax.optimization_barrier(values)


def ring_order(n):
    return list(range(0, n, 2)) + list(range(n - 1, 0, -2))


def ring_gather(ahead_part, back_part, axis, between):
    n = lax.axis_size(axis)
    order = ring_order(n)
    ahead = [(order[i], order[(i + 1) % n]) for i in range(n)]
    back = [(b, a) for a, b in ahead]
    first, second = [ahead_part], [back_part]
    for s in range(n - 1):
        first[-1], second[-1] = between(s, first[-1], second[-1])
        first.append(lax.ppermute(first[-1], axis, ahead))
        second.append(lax.ppermute(second[-1], axis, back))
    place = [order.index(i) for i in range(n)]
    owners = jnp.array([[order[(place[i] - r) % n] for r in range(n)] for i in range(n)], jnp.int32)
    return owners[lax.axis_index(axis)], first, [second[-r % n] for r in range(n)]


class HalvingSum:
    def __init__(self, value, axis):
        self.axis, self.n, self.me = axis, lax.axis_size(axis), lax.axis_index(axis)
        self.value, self.bit, self.sent = value, 1, False

    def launch(self, token):
        if self.bit < self.n:
            self.sent = True
            mine = (self.me // self.bit) % 2
            shape = self.value.shape
            pairs = self.value.reshape((shape[0] // 2, 2) + shape[1:])
            self.keep = lax.dynamic_index_in_dim(pairs, mine, 1, keepdims=False)
            send = lax.dynamic_index_in_dim(pairs, 1 - mine, 1, keepdims=False)
            send, token = tie(send, token)
            self.got = lax.ppermute(send, self.axis, [(i, i ^ self.bit) for i in range(self.n)])
        return token

    def land(self, token):
        if self.sent:
            self.sent = False
            keep, token = tie(self.keep, token)
            self.value = (keep.astype(f32) + self.got.astype(f32)).astype(bf16)
            self.bit *= 2
        return token

    def finish(self):
        while self.bit < self.n:
            token = jnp.zeros((1,), f32)
            self.land(token if self.sent else self.launch(token))
        return self.value[0]


class SharedSum:
    def __init__(self, value, axis):
        self.axis, self.n = axis, lax.axis_size(axis)
        self.value, self.bit, self.got = value, 1, None

    def launch(self, token):
        if self.bit < self.n:
            value, token = tie(self.value, token)
            self.value = value
            self.got = lax.ppermute(value, self.axis, [(i, i ^ self.bit) for i in range(self.n)])
        return token

    def land(self, token):
        if self.got is not None:
            value, token = tie(self.value, token)
            self.value, self.got = value + self.got, None
            self.bit *= 2
        return token

    def finish(self):
        while self.bit < self.n:
            self.land(self.launch(jnp.zeros((1,), f32)))
        return self.value


def swap(value, j):
    n = lax.axis_size("mp")
    return lax.ppermute(value, "mp", [(i, i ^ j) for i in range(n)])


def gather_mp_blocks(rows):
    near = swap(rows, 1)
    across = swap(rows, 2)
    return [rows, near, across, swap(across, 1)]


def in_order(blocks):
    me, n = lax.axis_index("mp"), lax.axis_size("mp")
    rows = blocks[0]
    total = jnp.zeros((n,) + rows.shape, rows.dtype)
    for j, block in enumerate(blocks):
        total = lax.dynamic_update_index_in_dim(total, block, me ^ j, 0)
    return total.reshape(n * rows.shape[0], rows.shape[1])


def sum_mp(value):
    value = value + swap(value, 1)
    return value + swap(value, 2)


def scatter_near(halves):
    me = lax.axis_index("mp")

    def pick(j):
        k = (me ^ j) % 2
        one = lax.dynamic_index_in_dim(halves[0], k, 0, keepdims=False)
        two = lax.dynamic_index_in_dim(halves[1], k, 0, keepdims=False)
        return jnp.where((me ^ j) < 2, one, two)

    return [pick(0), pick(2), swap(jnp.stack([pick(3), pick(1)]), 1)]


def scatter_far(mine, others, near):
    near = near.astype(f32)
    return mine.astype(f32) + near[1], (others.astype(f32) + near[0]).astype(bf16)


def nesterov(weight, velocity, average, step_grad, rate):
    momentum = MOMENT * velocity + step_grad
    new_weight = weight - rate * (step_grad + MOMENT * momentum)
    smoothed = SMOOTH * average + (1.0 - SMOOTH) * new_weight
    return [new_weight, momentum, smoothed, new_weight.astype(jnp.bfloat16)]


def body(
    block_input, cotangent, expert_ids, slot_ids,
    inward_proj, select_proj, delta_proj, channel_params, outward_proj, expert_up, expert_down, norm_gains, router_weight,
    inward_velocity, select_velocity, delta_velocity, channel_velocity, outward_velocity, upward_velocity,
    downward_velocity, gains_velocity, router_velocity,
    inward_average, select_average, delta_average, channel_average, outward_average, upward_average,
    downward_average, gains_average, router_average,
):
    tok_rows, width = block_input.shape
    ring, peers = lax.axis_size("dp"), lax.axis_size("mp")
    me = lax.axis_index("mp")
    own = inward_proj.shape[2]
    slot = -(-own // 16) * 16
    wide = -(-slot * ring // LANES) * LANES
    experts_all = router_weight.shape[1]
    slots = peers * CAP

    source = block_input.astype(f32)
    scale1 = mean_scale(source)
    normed_b = (source * scale1 * norm_gains[0]).astype(bf16)
    blocks = [normed_b]
    piece = tok_rows // PIECES
    pieces = [normed_b[i * piece : (i + 1) * piece] for i in range(PIECES)]

    half = 5 * LANES
    units = expert_down.shape[1]
    ring_a, ring_b = prep(
        jnp.swapaxes(inward_proj, 1, 2), select_proj, delta_proj, channel_params, outward_proj, half
    )

    def exchange(blocks):
        parts = blocks.reshape(peers, CAP, -1)
        return [parts[0]] + [swap(parts[j], j) for j in range(1, peers)]

    slot_index = (expert_ids ^ me) * CAP + slot_ids
    slot_row, slot_col, ids_col = slot_index[None, :], slot_index[:, None], expert_ids[:, None]
    dispatch = (lax.broadcasted_iota(jnp.int32, (slots, tok_rows), 0) == slot_row).astype(bf16)
    early = {"cot": jnp.dot(dispatch, cotangent, preferred_element_type=f32).astype(bf16), "up": expert_up[0]}

    def between(s, a, b):
        if s == START:
            a, b, early["up"] = tie(a, b, early["up"])
        if s < PIECES:
            pieces[s], a, b = tie(pieces[s], a, b)
            pieces[s] = swap(pieces[s], 2)
        if 0 < s <= PIECES:
            a, b, pieces[s - 1] = tie(a, b, pieces[s - 1])
        if s == PIECES:
            blocks.extend([swap(normed_b, 1), jnp.concatenate(pieces)])
            blocks.append(swap(blocks[2], 1))
            a, b, early["cot"] = tie(a, b, early["cot"])
            early["cot"] = exchange(early["cot"])
        if s == PIECES + 1:
            a, b, blocks[1], blocks[3] = tie(a, b, blocks[1], blocks[3])
        return a, b

    owners, mix_a, mix_b = ring_gather(ring_a, ring_b, "dp", between)
    expert_w = lax.all_gather(prep_experts(early["up"], expert_down[0]), "dp", axis=0, tiled=True)
    w_in, selw, delta_w, chan, out_w = mixer_weights(owners, mix_a, mix_b, slot, wide, width, half)
    seq = in_order(blocks)
    seq, *cot_rows = tie(seq, *early["cot"])

    router_pad = jnp.pad(router_weight, ((0, 0), (0, LANES - experts_all)))

    def exchange_row(rows):
        parts = rows[0].reshape(peers, CAP)
        row = jnp.concatenate([parts[0]] + [swap(parts[j], j) for j in range(1, peers)])
        return jnp.broadcast_to(row[None], (8, slots))

    count = seq.shape[0] // 2
    conv_tail, state = jnp.zeros((8, wide), f32), jnp.zeros((NST, wide), f32)
    convs, scans, selections = [], [], []
    for h in range(2):
        convs.append(conv_fwd(seq, h * count, count, w_in, chan, selw, conv_tail))
        conv_tail = convs[-1][6]
        selections.append(sum_mp(convs[-1][5]))
    edges = [state]
    for h in range(2):
        conv_in, gate_in, pre, act, act_b, _, _ = convs[h]
        scans.append(scan_fwd(selections[h], delta_w, act, gate_in, chan, out_w, state))
        state = scans[-1][6]
        edges.append(state)
    near, far = scatter_far(*scatter_near([s[4].reshape(2, tok_rows, width) for s in scans]))
    far = swap(far, 2)
    residual, probs, gate_prob, outgoing, prob_slots = route_tokens(
        block_input, near, far, norm_gains, router_pad, ids_col, slot_row, slot_col, slots, experts_all
    )
    arrived = exchange(outgoing)
    expert_out, d_rows, dots, grad_experts = experts(arrived, cot_rows, exchange_row(prob_slots), expert_w, units)
    experts_grad = lax.psum_scatter(grad_experts, "dp", scatter_dimension=0, tiled=True)

    d_residual, d_mixer, parts = back_tokens(
        exchange(d_rows), exchange_row(dots), slot_col, ids_col, probs, router_pad, residual, cotangent, norm_gains,
        experts_all,
    )
    portion = in_order(gather_mp_blocks(d_mixer))
    expert_out, portion = tie(expert_out, portion)
    returned = exchange(expert_out)

    def both(left, right):
        return contract_rows(left[0], right[:count]) + contract_rows(left[1], right[count:])

    def cut(a):
        return a[: slot * ring]

    by_owner = lambda a: HalvingSum(cut(a).reshape(ring, slot, -1), "dp")
    out_sum = by_owner(both([s[3] for s in scans], portion).astype(bf16))
    q, later = jnp.zeros((NST, wide), f32), jnp.zeros((8, wide), f32)
    tails, sums = [None] * 2, [None] * 2
    for h in (1, 0):
        kept = scans[h][0], convs[h][3], convs[h][1], scans[h][1], scans[h][2]
        q = out_sum.launch(q)
        tails[h] = scan_bwd(portion, h * count, 0, kept, edges[h], q, count, out_w, selections[h], chan, delta_w)
        q = out_sum.land(tails[h][5])
        sums[h] = sum_mp(tails[h][3])
    gate_sum = by_owner(both([t[0] for t in tails], seq).astype(bf16))
    grads, gch = None, jnp.zeros((8, wide), f32)
    tail_sum = tails[0][4] + tails[1][4]
    dnorms, gains = [None] * 2, [None] * 2
    for h in (1, 0):
        later = gate_sum.launch(out_sum.launch(later))
        dnorms[h], gains[h], later, gch, grads = conv_bwd(
            h * count, count, h == 0, tails[h][1], sums[h], selw, convs[h][2], convs[h][0], tails[h][0], w_in, seq,
            chan, later, convs[h][4], tails[h][2], scans[h][5], grads, gch, tail_sum,
        )
        later = gate_sum.land(out_sum.land(later))
    conv_sum = by_owner(grads)
    factor = 1.0 / math.sqrt(tok_rows * ring * peers)
    gain_part = (gains[0][:1] + gains[1][:1]) / norm_gains[:1]
    shared = SharedSum(jnp.concatenate([gain_part, parts[:1], parts[8 : 8 + experts_all]]), "dp")
    near = scatter_near([d.reshape(2, tok_rows, width) for d in dnorms])
    later = gate_sum.launch(conv_sum.launch(later))
    later, experts_grad = tie(shared.launch(later), experts_grad)
    up_new, down_new = experts_step(
        experts_grad,
        (expert_up, upward_velocity, upward_average),
        (expert_down, downward_velocity, downward_average),
        factor,
    )
    later, up_new[3], near[2] = tie(later, up_new[3], near[2])
    near, far_send = scatter_far(*near)
    far_send, later = tie(far_send, later)
    far = swap(far_send, 2)
    later = shared.land(gate_sum.land(conv_sum.land(later)))
    later, returned[0] = tie(shared.launch(conv_sum.launch(later)), returned[0])
    tokens_out = contract_rows(dispatch, jnp.concatenate(returned))
    block_output = (residual + gate_prob[:, :1] * tokens_out).astype(bf16)
    later, block_output = tie(later, block_output)
    later = shared.land(conv_sum.land(later))
    later, far = tie(shared.launch(conv_sum.launch(later)), far)
    d_normed = near + far.astype(f32)
    a1 = norm_gains[0] * d_normed
    hat1 = source * scale1
    block_grad = d_residual + scale1 * (a1 - hat1 * jnp.mean(a1 * hat1, axis=-1, keepdims=True))
    later, block_grad = tie(later, block_grad)
    later = shared.land(conv_sum.land(later))
    shared = sum_mp(shared.finish())
    mixer_new = mixer_step(
        conv_sum.finish(),
        gate_sum.finish(),
        out_sum.finish(),
        later,
        (
            tuple(jnp.swapaxes(a, 1, 2) for a in (inward_proj, inward_velocity, inward_average)),
            (select_proj, select_velocity, select_average),
            (delta_proj, delta_velocity, delta_average),
            (channel_params, channel_velocity, channel_average),
            (outward_proj, outward_velocity, outward_average),
        ),
        factor,
    )
    results = [block_output, block_grad]
    mixer_new[0] = [jnp.swapaxes(a, 1, 2) for a in mixer_new[0]]
    for new in mixer_new:
        results.extend(new)
    results.extend(up_new)
    results.extend(down_new)
    results.extend(nesterov(norm_gains, gains_velocity, gains_average, shared[:2] * factor, LEARNING[7]))
    results.extend(nesterov(router_weight, router_velocity, router_average, shared[2:].T * factor, LEARNING[8]))
    return tuple(results)


def solution(mesh):
    in_specs = (
        P(("dp", "mp"), None),
        P(("dp", "mp"), None),
        P(("dp", "mp")),
        P(("dp", "mp")),
        P(None, None, ("dp", "mp")),
        P(("dp", "mp"), None),
        P(None, ("dp", "mp")),
        P(None, ("dp", "mp")),
        P(("dp", "mp"), None),
        P("mp", None, "dp"),
        P("mp", "dp", None),
        P(),
        P(),
        P(None, None, ("dp", "mp")),
        P(("dp", "mp"), None),
        P(None, ("dp", "mp")),
        P(None, ("dp", "mp")),
        P(("dp", "mp"), None),
        P("mp", None, "dp"),
        P("mp", "dp", None),
        P(),
        P(),
        P(None, None, ("dp", "mp")),
        P(("dp", "mp"), None),
        P(None, ("dp", "mp")),
        P(None, ("dp", "mp")),
        P(("dp", "mp"), None),
        P("mp", None, "dp"),
        P("mp", "dp", None),
        P(),
        P(),
    )
    out_specs = (
        P(("dp", "mp"), None),
        P(("dp", "mp"), None),
        P(None, None, ("dp", "mp")),
        P(None, None, ("dp", "mp")),
        P(None, None, ("dp", "mp")),
        P(None, None, ("dp", "mp")),
        P(("dp", "mp"), None),
        P(("dp", "mp"), None),
        P(("dp", "mp"), None),
        P(("dp", "mp"), None),
        P(None, ("dp", "mp")),
        P(None, ("dp", "mp")),
        P(None, ("dp", "mp")),
        P(None, ("dp", "mp")),
        P(None, ("dp", "mp")),
        P(None, ("dp", "mp")),
        P(None, ("dp", "mp")),
        P(None, ("dp", "mp")),
        P(("dp", "mp"), None),
        P(("dp", "mp"), None),
        P(("dp", "mp"), None),
        P(("dp", "mp"), None),
        P("mp", None, "dp"),
        P("mp", None, "dp"),
        P("mp", None, "dp"),
        P("mp", None, "dp"),
        P("mp", "dp", None),
        P("mp", "dp", None),
        P("mp", "dp", None),
        P("mp", "dp", None),
        P(),
        P(),
        P(),
        P(),
        P(),
        P(),
        P(),
        P(),
    )
    return jax.shard_map(body, mesh=mesh, in_specs=in_specs, out_specs=out_specs, check_vma=False)
```

```python
import functools
import math

import jax
import jax.numpy as jnp
from jax import lax
from jax.experimental import pallas as pl
from jax.experimental.pallas import tpu as pltpu
from jax.sharding import PartitionSpec as P

bf16, f32 = jnp.bfloat16, jnp.float32
CONV, DT_RANK, SUBT, NST = 4, 72, 16, 16
LOG2E = 1.0 / math.log(2.0)
LANES = 128
BLOCK = 256
CAP = 192
EPSILON = 1e-05
MOMENT = 0.9
SMOOTH = 0.6
LEARNING = (0.02, 0.03, 0.4, 0.3, 0.04, 0.07, 0.3, 0.3, 0.01)
HIGHEST = lax.Precision.HIGHEST
MIB = 2**20
SHAPE = jax.ShapeDtypeStruct


def dotf(a, b, dims=((1,), (0,))):
    return lax.dot_general(a, b, (dims, ((), ())), preferred_element_type=f32)


def block_mask():
    r = lax.broadcasted_iota(jnp.int32, (SUBT, SUBT * NST), 0)
    c = lax.broadcasted_iota(jnp.int32, (SUBT, SUBT * NST), 1)
    return (c // NST == r).astype(f32)


def spread(first, rows):
    r = lax.broadcasted_iota(jnp.int32, (rows, SUBT * NST), 0)
    c = lax.broadcasted_iota(jnp.int32, (rows, SUBT * NST), 1)
    return (c % NST + first == r).astype(bf16)


def soft_parts(x):
    e = jnp.exp(-jnp.abs(x))
    return jnp.maximum(x, 0.0) + jnp.log1p(e), jnp.where(x >= 0, 1.0, e) / (1.0 + e)


def row8(ref, k, t):
    d = ref[k, pl.ds(t, 8, stride=0), :]
    return jnp.concatenate([d, d], 0)


def split_states(sel_ref, bts, cts, T):
    selT = sel_ref[...].T
    for k in range(T // SUBT):
        bts[k] = selT[DT_RANK : DT_RANK + NST, SUBT * k : SUBT * k + SUBT]
        cts[k] = selT[DT_RANK + NST : DT_RANK + 2 * NST, SUBT * k : SUBT * k + SUBT]


def blocked(sel_ref, k, place, mask):
    sel = sel_ref[pl.ds(pl.multiple_of(k * SUBT, SUBT), SUBT), :]
    return (dotf(sel.astype(bf16), place) * mask).astype(bf16)


def blocked_all(sel_ref, place, T):
    r = lax.broadcasted_iota(jnp.int32, (T, SUBT * NST), 0)
    c = lax.broadcasted_iota(jnp.int32, (T, SUBT * NST), 1)
    flat = jnp.where(c // NST == r % SUBT, dotf(sel_ref[...].astype(bf16), place), 0.0)
    return flat.astype(bf16).reshape(T // SUBT, SUBT, SUBT * NST)


def rows_at(T, w, first=0):
    return pl.BlockSpec((T, w), lambda i: (first + i, 0))


def rows_back(T, w, last):
    return pl.BlockSpec((T, w), lambda i: (last - i, 0))


def whole(shape):
    shape = tuple(shape)
    return pl.BlockSpec(shape, lambda i: (0,) * len(shape))


def params(mib):
    return pltpu.CompilerParams(vmem_limit_bytes=mib * MIB)


def cost(flops=0, moved=1 << 20):
    return pl.CostEstimate(flops=flops, bytes_accessed=moved, transcendentals=0)


def turned(a):
    short = -a.shape[1] % LANES
    if short:
        a = jnp.concatenate([a, jnp.zeros((a.shape[0], short), f32)], axis=1)
    return a.T


def prep_kernel(in_ref, sel_ref, delta_ref, chan_ref, out_ref, a_ref, b_ref, *, half):
    own = sel_ref.shape[0]
    xw, vrows = sel_ref.shape[1], chan_ref.shape[0]
    width = in_ref.shape[2]
    a_ref[:, 0:width] = in_ref[0].astype(bf16)
    a_ref[:, width:] = out_ref[:, 0:half].astype(bf16)
    small = jnp.concatenate(
        [
            delta_ref[...],
            chan_ref[...],
            jnp.zeros((LANES - DT_RANK - vrows, own), f32),
        ],
        axis=0,
    )
    select = jnp.concatenate([sel_ref[...], jnp.zeros((own, LANES - xw), f32)], axis=1)
    b_ref[:, 0:width] = in_ref[1].astype(bf16)
    b_ref[:, width : width + LANES] = select.astype(bf16)
    b_ref[:, width + LANES : width + 2 * LANES] = turned(small)[0:own].astype(bf16)
    b_ref[:, width + 2 * LANES :] = out_ref[:, half:].astype(bf16)


def prep(inward, select, delta, channel, outward, half):
    own, width = outward.shape
    return pl.pallas_call(
        functools.partial(prep_kernel, half=half),
        out_shape=[SHAPE((own, width + half), bf16), SHAPE((own, 2 * width - half + 2 * LANES), bf16)],
        compiler_params=params(40),
        cost_estimate=cost(),
    )(inward, select, delta, channel, outward)


def prep_experts_kernel(up_ref, down_ref, both_ref):
    units = down_ref.shape[0]
    both_ref[0:units, :] = turned(up_ref[...])[0:units].astype(bf16)
    both_ref[units : 2 * units, :] = down_ref[...].astype(bf16)


def prep_experts(up, down):
    return pl.pallas_call(
        prep_experts_kernel,
        out_shape=SHAPE((2 * down.shape[0], down.shape[1]), bf16),
        compiler_params=params(40),
        cost_estimate=cost(),
    )(up, down)


def mixer_weights_kernel(owner_ref, *refs, ring, own, slot, width, half):
    a, b = refs[:ring], refs[ring : 2 * ring]
    w_ref, selw_ref, delta_ref, chan_ref, out_ref, small = refs[2 * ring :]
    wide = selw_ref.shape[0]
    if wide > ring * slot:
        for ref in (w_ref, selw_ref, out_ref, small):
            ref[...] = jnp.zeros_like(ref)

    def place(ref, at, value):
        if slot > own:
            value = jnp.concatenate([value, jnp.zeros((slot - own, value.shape[1]), value.dtype)], axis=0)
        ref[pl.ds(pl.multiple_of(at, 16), slot), :] = value

    for r in range(ring):
        at = owner_ref[r] * slot
        place(w_ref, at, a[r][:, 0:width])
        place(w_ref, wide + at, b[r][:, 0:width])
        place(selw_ref, at, b[r][:, width : width + LANES])
        place(small, at, b[r][:, width + LANES : width + 2 * LANES].astype(f32))
        place(out_ref, at, jnp.concatenate([a[r][:, width:], b[r][:, width + 2 * LANES :]], axis=1))
    flat = small[...].T
    delta_ref[0:DT_RANK, :] = flat[0:DT_RANK].astype(bf16)
    delta_ref[DT_RANK:LANES, :] = jnp.zeros((LANES - DT_RANK, wide), bf16)
    chan_ref[...] = flat[DT_RANK : DT_RANK + chan_ref.shape[0]]


def mixer_weights(owners, a, b, slot, wide, width, half):
    ring = len(a)
    own = b[0].shape[0]
    return pl.pallas_call(
        functools.partial(mixer_weights_kernel, ring=ring, own=own, slot=slot, width=width, half=half),
        in_specs=[pl.BlockSpec(memory_space=pltpu.SMEM)] + [pl.BlockSpec(memory_space=pltpu.VMEM)] * (2 * ring),
        out_shape=[
            SHAPE((2 * wide, width), bf16),
            SHAPE((wide, LANES), bf16),
            SHAPE((LANES, wide), bf16),
            SHAPE((24, wide), f32),
            SHAPE((wide, width), bf16),
        ],
        scratch_shapes=[pltpu.VMEM((wide, LANES), f32)],
        compiler_params=params(48),
        cost_estimate=cost(),
    )(owners, *a, *b)


def conv_fwd_kernel(seq_ref, w_ref, chan_ref, selw_ref, tail_ref, conv_ref, gate_ref, pre_ref, act_ref, actb_ref, sel_ref, end_ref, buf, *, T):
    C = conv_ref.shape[1]

    @pl.when(pl.program_id(0) == 0)
    def _():
        buf[0:8, :] = tail_ref[...]

    seq = seq_ref[...]
    conv = dotf(seq, w_ref[0:C, :], ((1,), (1,)))
    gate_ref[...] = dotf(seq, w_ref[C : 2 * C, :], ((1,), (1,)))
    conv_ref[...] = conv
    buf[8 : 8 + T, :] = conv
    pre = chan_ref[CONV : CONV + 1, :] + chan_ref[CONV - 1 : CONV, :] * conv
    for tap in range(CONV - 1):
        at = 8 - CONV + 1 + tap
        pre = pre + chan_ref[tap : tap + 1, :] * buf[at : at + T, :]
    buf[0:8, :] = buf[T : T + 8, :]
    end_ref[...] = buf[0:8, :]
    pre_ref[...] = pre
    act = pre / (1.0 + jnp.exp(-pre))
    act_ref[...] = act
    actb = act.astype(bf16)
    actb_ref[...] = actb
    sel_ref[...] = dotf(actb, selw_ref[...])


def conv_fwd(seq, first, count, w_in, chan, selw, tail, T=BLOCK):
    C, D = chan.shape[1], seq.shape[1]
    return pl.pallas_call(
        functools.partial(conv_fwd_kernel, T=T),
        grid=(count // T,),
        in_specs=[rows_at(T, D, first // T), whole(w_in.shape), whole(chan.shape), whole(selw.shape), whole(tail.shape)],
        out_specs=[rows_at(T, C)] * 5 + [rows_at(T, LANES), whole((8, C))],
        out_shape=[SHAPE((count, C), f32)] * 4 + [SHAPE((count, C), bf16), SHAPE((count, LANES), f32), SHAPE((8, C), f32)],
        scratch_shapes=[pltpu.VMEM((T + 8, C), f32)],
        compiler_params=params(48),
        cost_estimate=cost(),
    )(seq, w_in, chan, selw, tail)


def scan_fwd_kernel(
    sel_ref, delta_w_ref, act_ref, gate_ref, chan_ref, out_w_ref, start_ref,
    s_ref, xlin_ref, scanned_ref, gated_ref, mix_ref, rank_ref, end_ref,
    state, dscr, uscr, yscr, bts, cts, blocks, sA, sB, *, T
):
    C = act_ref.shape[1]
    NCH = T // SUBT

    @pl.when(pl.program_id(0) == 0)
    def _():
        state[...] = start_ref[...]

    rank = sel_ref[...].astype(bf16)
    rank_ref[...] = rank
    x = dotf(rank, delta_w_ref[...]) + chan_ref[CONV + 1 : CONV + 2, :]
    xlin_ref[...] = x
    sp, _ = soft_parts(x)
    dscr[...] = sp.reshape(NCH, SUBT, C)
    uscr[...] = (sp * act_ref[...]).reshape(NCH, SUBT, C)
    split_states(sel_ref, bts, cts, T)
    nrate = -LOG2E * jnp.exp(chan_ref[CONV + 3 : CONV + 3 + NST, :])
    blocks[...] = blocked_all(sel_ref, spread(DT_RANK + NST, LANES), T)

    def one(k, S, cur, prev):
        before = jnp.maximum(k - 1, 0)
        yv = dotf(blocks[before], prev[...])
        bt = bts[k]
        for t in range(SUBT):
            d = row8(dscr, k, t)
            u = row8(uscr, k, t)
            S = jnp.exp2(d * nrate) * S + u * jnp.broadcast_to(bt[:, t : t + 1], (NST, C))
            rounded = S.astype(bf16)
            cur[t * NST : t * NST + NST, :] = rounded
            s_ref[k, t * NST : t * NST + NST, :] = rounded
        yscr[before] = yv
        return S

    def pair(j, S):
        S = one(2 * j, S, sA, sB)
        return one(2 * j + 1, S, sB, sA)

    sB[...] = jnp.zeros_like(sB)
    state[...] = lax.fori_loop(0, NCH // 2, pair, state[...])
    end_ref[...] = state[...]
    yscr[NCH - 1] = dotf(blocks[NCH - 1], sB[...])
    scanned = yscr[...].reshape(T, C) + chan_ref[CONV + 2 : CONV + 3, :] * act_ref[...]
    scanned_ref[...] = scanned
    g = gate_ref[...]
    gated = (scanned * (g / (1.0 + jnp.exp(-g)))).astype(bf16)
    gated_ref[...] = gated
    mix_ref[...] = dotf(gated, out_w_ref[...]).astype(mix_ref.dtype)


def scan_fwd(sel, delta_w, act, gate, chan, out_w, start, T=BLOCK):
    N, C = act.shape
    W = out_w.shape[1]
    g, nch = N // T, T // SUBT
    vm = pltpu.VMEM
    return pl.pallas_call(
        functools.partial(scan_fwd_kernel, T=T),
        grid=(g,),
        in_specs=[rows_at(T, LANES), whole(delta_w.shape), rows_at(T, C), rows_at(T, C), whole(chan.shape), whole(out_w.shape), whole(start.shape)],
        out_specs=[pl.BlockSpec((nch, SUBT * NST, C), lambda i: (i, 0, 0))] + [rows_at(T, C)] * 3 + [rows_at(T, W), rows_at(T, LANES), whole((NST, C))],
        out_shape=[
            SHAPE((N // SUBT, SUBT * NST, C), bf16), SHAPE((N, C), f32), SHAPE((N, C), f32), SHAPE((N, C), bf16),
            SHAPE((N, W), bf16), SHAPE((N, LANES), bf16), SHAPE((NST, C), f32),
        ],
        scratch_shapes=[vm((NST, C), f32)] + [vm((nch, SUBT, C), f32)] * 3 + [vm((nch, NST, SUBT), f32)] * 2 + [vm((nch, SUBT, SUBT * NST), bf16)] + [vm((SUBT * NST, C), bf16)] * 2,
        compiler_params=params(48),
        cost_estimate=cost(),
    )(sel, delta_w, act, gate, chan, out_w, start)


def gather_states(first):
    r = lax.broadcasted_iota(jnp.int32, (SUBT * NST, LANES), 0)
    c = lax.broadcasted_iota(jnp.int32, (SUBT * NST, LANES), 1)
    return (r % NST + first == c).astype(bf16)


def fold(a):
    return sum(a[:, i : i + LANES] for i in range(LANES, a.shape[1], LANES)) + a[:, 0:LANES]


def scan_bwd_kernel(
    dmix_ref, out_w_ref, s_ref, before_ref, edge_ref, act_ref, gate_ref, xlin_ref, scanned_ref, sel_ref, chan_ref, delta_w_ref, q_ref,
    dgate_ref, dact_ref, ddl_ref, dsel_ref, gch_ref, qend_ref,
    qscr, dscr, uscr, dyscr, lbscr, wsscr, bts, cts, blocks, rows_b, rows_c, part_b, part_c, *bufs, T, g, opens
):
    C = act_ref.shape[1]
    NCH = T // SUBT
    step = pl.program_id(0)

    @pl.when(step == 0)
    def _():
        qscr[...] = q_ref[...]
        gch_ref[...] = jnp.zeros_like(gch_ref)

    dg = dotf(dmix_ref[...], out_w_ref[...], ((1,), (1,)))
    gt = gate_ref[...]
    sg = 1.0 / (1.0 + jnp.exp(-gt))
    dgate_ref[...] = (dg * scanned_ref[...] * (sg * (1.0 + gt * (1.0 - sg)))).astype(bf16)
    dy = dg * (gt * sg)
    act = act_ref[...]
    sp, sigd = soft_parts(xlin_ref[...])
    dscr[...] = sp.reshape(NCH, SUBT, C)
    uscr[...] = (sp * act).reshape(NCH, SUBT, C)
    dyscr[...] = dy.reshape(NCH, SUBT, C)
    split_states(sel_ref, bts, cts, T)
    nrate = -LOG2E * jnp.exp(chan_ref[CONV + 3 : CONV + 3 + NST, :])
    mask = block_mask()
    eb = spread(DT_RANK, LANES)
    half_rows = lax.broadcasted_iota(jnp.int32, (SUBT, SUBT * NST // 2), 0)
    half_cols = lax.broadcasted_iota(jnp.int32, (SUBT, SUBT * NST // 2), 1)
    halves = (half_cols // (NST // 2) == half_rows).astype(bf16)
    ones = jnp.ones((SUBT, LANES), bf16)
    last = slice(SUBT * NST - NST, SUBT * NST)
    first = before_ref[0, last, :].astype(f32)
    if opens:
        first = jnp.where(step == g - 1, edge_ref[...], first)

    def lanes_summed(partial):
        return (dotf(ones, partial, ((1,), (1,))) * mask).astype(bf16)

    blocks[...] = blocked_all(sel_ref, eb, T)

    def one(k, q, acc, cur, prev):
        kp = jnp.minimum(k + 1, NCH - 1)
        lam_ref, w_ref = prev
        lamb = dotf(blocks[kp], lam_ref[...])
        wsum = dotf(halves, w_ref[...])
        lam_ref, w_ref = cur
        bt = bts[k]
        ct = cts[k]
        s_t = s_ref[k, last, :].astype(f32)
        s_before = jnp.where(k == 0, first, s_ref[jnp.maximum(k - 1, 0), last, :].astype(f32))
        held = None
        for t in range(SUBT - 1, -1, -1):
            d = row8(dscr, k, t)
            u = row8(uscr, k, t)
            dyr = row8(dyscr, k, t)
            lam = jnp.broadcast_to(ct[:, t : t + 1], (NST, C)) * dyr + q
            lam_ref[t * NST : t * NST + NST, :] = lam.astype(bf16)
            q = jnp.exp2(d * nrate) * lam
            part_c[k, t * NST : t * NST + NST, :] = fold(s_t * dyr).astype(bf16)
            part_b[k, t * NST : t * NST + NST, :] = fold(lam * u).astype(bf16)
            s_p = s_ref[k, t * NST - NST : t * NST, :].astype(f32) if t > 0 else s_before
            wr = q * s_p * nrate
            part = wr[0 : NST // 2] + wr[NST // 2 :]
            if t % 2:
                held = part
            else:
                w_ref[t * NST // 2 : t * NST // 2 + NST, :] = jnp.concatenate([part, held], axis=0).astype(bf16)
            acc = acc + wr * d
            s_t = s_p
        lbscr[kp] = lamb
        wsscr[kp] = wsum
        return q, acc

    def pair(j, carry):
        k = NCH - 1 - 2 * j
        carry = one(k, *carry, bufs[0:2], bufs[2:4])
        return one(k - 1, *carry, bufs[2:4], bufs[0:2])

    for ref in bufs[2:4]:
        ref[...] = jnp.zeros_like(ref)
    q, acc = lax.fori_loop(0, NCH // 2, pair, (qscr[...], jnp.zeros((NST, C), f32)))
    lam_ref, w_ref = bufs[2:4]
    lbscr[0] = dotf(blocks[0], lam_ref[...])
    wsscr[0] = dotf(halves, w_ref[...])

    def sums(k, _):
        rows_b[k] = lanes_summed(part_b[k])
        rows_c[k] = lanes_summed(part_c[k])
        return 0

    lax.fori_loop(0, NCH, sums, 0, unroll=4)
    qscr[...] = q
    qend_ref[...] = q
    gch_ref[CONV + 3 : CONV + 3 + NST, :] += acc * (1.0 / LOG2E)
    lamB = lbscr[...].reshape(T, C)
    ws = wsscr[...].reshape(T, C) * (-1.0 / LOG2E)
    dyf = dyscr[...].reshape(T, C)
    spf = dscr[...].reshape(T, C)
    dact_ref[...] = chan_ref[CONV + 2 : CONV + 3, :] * dyf + spf * lamB
    ddl = (act * lamB - ws) * sigd
    ddl_ref[...] = ddl.astype(bf16)
    gch_ref[CONV + 1 : CONV + 2, :] += jnp.sum(ddl, axis=0, keepdims=True)
    gch_ref[CONV + 2 : CONV + 3, :] += jnp.sum(dyf * act, axis=0, keepdims=True)
    flat = lambda ref: ref[...].reshape(T, SUBT * NST)
    dsel = dotf(ddl_ref[...], delta_w_ref[...], ((1,), (1,)))
    dsel = dsel + dotf(flat(rows_b), gather_states(DT_RANK)) + dotf(flat(rows_c), gather_states(DT_RANK + NST))
    dsel_ref[...] = dsel.astype(bf16)


def scan_bwd(dmix, at, half, kept, edge, q, count, out_w, sel, chan, delta_w, T=BLOCK):
    s_all, act, gate, xlin, scanned = kept
    C = act.shape[1]
    g, nch = count // T, T // SUBT
    low = half // T
    row = lambda w: rows_back(T, w, low + g - 1)
    out = lambda w: rows_back(T, w, g - 1)
    vm = pltpu.VMEM
    return pl.pallas_call(
        functools.partial(scan_bwd_kernel, T=T, g=g, opens=low == 0),
        grid=(g,),
        in_specs=[
            rows_back(T, dmix.shape[1], at // T + g - 1), whole(out_w.shape),
            pl.BlockSpec((nch, SUBT * NST, C), lambda i: (low + g - 1 - i, 0, 0)),
            pl.BlockSpec((1, SUBT * NST, C), lambda i: (jnp.maximum((low + g - 1 - i) * nch - 1, 0), 0, 0)),
            whole(edge.shape),
            row(C), row(C), row(C), row(C), row(LANES), whole(chan.shape), whole(delta_w.shape), whole(q.shape),
        ],
        out_specs=[out(C), out(C), out(C), out(LANES), whole((24, C)), whole((NST, C))],
        out_shape=[
            SHAPE((count, C), bf16), SHAPE((count, C), f32), SHAPE((count, C), bf16), SHAPE((count, LANES), bf16),
            SHAPE((24, C), f32), SHAPE((NST, C), f32),
        ],
        scratch_shapes=[vm((NST, C), f32)] + [vm((nch, SUBT, C), f32)] * 5 + [vm((nch, NST, SUBT), f32)] * 2 + [vm((nch, SUBT, SUBT * NST), bf16)] * 3
        + [vm((nch, SUBT * NST, LANES), bf16)] * 2
        + [vm((SUBT * NST, C), bf16), vm((SUBT * NST // 2, C), bf16)] * 2,
        compiler_params=params(56),
        cost_estimate=cost(),
    )(dmix, out_w, s_all, s_all, edge, act, gate, xlin, scanned, sel, chan, delta_w, q)


def conv_bwd_kernel(
    dact_ref, dsel_ref, selw_ref, pre_ref, conv_ref, dgate_ref, w_ref, seq_ref, chan_ref, next_ref,
    actb_ref, ddl_ref, rank_ref, before_ref, gchin_ref, tail_ref,
    dnorm_ref, gain_ref, head_ref, gch_ref, grad_ref, buf, acc, *, T, g, opens, final
):
    C, D = conv_ref.shape[1], seq_ref.shape[1]
    step = pl.program_id(0)

    @pl.when(step == 0)
    def _():
        buf[T : T + 8, :] = next_ref[...]
        gain_ref[...] = jnp.zeros_like(gain_ref)
        if opens:
            gch_ref[...] = jnp.zeros_like(gch_ref)
            acc[...] = jnp.zeros_like(acc)
        else:
            gch_ref[...] = gchin_ref[...]
            acc[...] = before_ref[...]

    pre = pre_ref[...]
    sig = 1.0 / (1.0 + jnp.exp(-pre))
    dsel = dsel_ref[...]
    dact = dact_ref[...] + dotf(dsel, selw_ref[...], ((1,), (1,)))
    dpre = dact * (sig * (1.0 + pre * (1.0 - sig)))
    buf[0:T, :] = dpre
    conv = conv_ref[...]
    total = chan_ref[CONV - 1 : CONV, :] * dpre
    gch_ref[CONV - 1 : CONV, :] += jnp.sum(conv * dpre, axis=0, keepdims=True)
    for tap in range(CONV - 1):
        later = buf[CONV - 1 - tap : CONV - 1 - tap + T, :]
        total = total + chan_ref[tap : tap + 1, :] * later
        gch_ref[tap : tap + 1, :] += jnp.sum(conv * later, axis=0, keepdims=True)
    gch_ref[CONV : CONV + 1, :] += jnp.sum(dpre, axis=0, keepdims=True)
    buf[T : T + 8, :] = buf[0:8, :]
    head_ref[...] = buf[0:8, :]
    dconv = total.astype(bf16)
    seq = seq_ref[...]
    rows = ((0,), (0,))
    acc[:, 0:D] += dotf(dconv, seq, rows)
    acc[:, D : D + LANES] += dotf(actb_ref[...], dsel, rows)
    keep = lax.broadcasted_iota(jnp.int32, (T, LANES), 1) < DT_RANK
    rank = jnp.where(keep, rank_ref[...].astype(f32), 0.0).astype(bf16)
    acc[:, D + LANES :] += dotf(ddl_ref[...], rank, rows)
    dnorm = dotf(dconv, w_ref[0:C, :]) + dotf(dgate_ref[...], w_ref[C : 2 * C, :])
    dnorm_ref[...] = dnorm.astype(bf16)
    gain_ref[0:1, :] += jnp.sum(dnorm * seq.astype(f32), axis=0, keepdims=True)

    @pl.when(step == g - 1)
    def _():
        if final:
            taps = jnp.where(lax.broadcasted_iota(jnp.int32, (8, C), 0) <= CONV, gch_ref[...], tail_ref[0:8, :])
            side = jnp.concatenate(
                [jnp.zeros((DT_RANK, C), f32), taps, tail_ref[8:, :], jnp.zeros((LANES - DT_RANK - 24, C), f32)], axis=0
            )
            acc[:, D + LANES :] += side.T
        grad_ref[...] = acc[...].astype(grad_ref.dtype)


def conv_bwd(at, count, final, dact, dsel, selw, pre, conv, dgate, w_in, seq, chan, later, actb, ddl, rank, before, gch, tail, T=BLOCK):
    C, D = conv.shape[1], seq.shape[1]
    g = count // T
    opens = before is None
    own = lambda w: rows_back(T, w, g - 1)
    packed = SHAPE((C, D + 2 * LANES), bf16 if final else f32)
    return pl.pallas_call(
        functools.partial(conv_bwd_kernel, T=T, g=g, opens=opens, final=final),
        grid=(g,),
        in_specs=[
            own(C), own(LANES), whole(selw.shape), own(C), own(C), own(C), whole(w_in.shape),
            rows_back(T, D, at // T + g - 1), whole(chan.shape), whole(later.shape),
            own(C), own(C), own(LANES), whole((8, LANES) if opens else before.shape), whole(gch.shape), whole(tail.shape),
        ],
        out_specs=[own(D), whole((8, D)), whole((8, C)), whole((8, C)), whole(packed.shape)],
        out_shape=[SHAPE((count, D), bf16), SHAPE((8, D), f32), SHAPE((8, C), f32), SHAPE((8, C), f32), packed],
        scratch_shapes=[pltpu.VMEM((T + 8, C), f32), pltpu.VMEM(packed.shape, f32)],
        compiler_params=params(56),
        cost_estimate=cost(),
    )(dact, dsel, selw, pre, conv, dgate, w_in, seq, chan, later, actb, ddl, rank, jnp.zeros((8, LANES), f32) if opens else before, gch, tail)


def as_column(row, count):
    return jnp.broadcast_to(row[0:1, :], (LANES, count)).T[:, 0:1]


def as_rows(column, count):
    return jnp.broadcast_to(column, (count, LANES)).T[0:8, :]


def experts_kernel(x0, x1, x2, x3, c0, c1, c2, c3, prob_ref, w_ref, out_ref, drow_ref, dot_ref, g_ref, acc_out, acc_row, x_ref, dz_ref, xt_ref, dzt_ref, *, steps, per, units):
    R = x_ref.shape[0]

    @pl.when(pl.program_id(0) == 0)
    def _():
        acc_out[...] = jnp.zeros_like(acc_out)
        acc_row[...] = jnp.zeros_like(acc_row)
        x_ref[...] = jnp.concatenate([x0[...], x1[...], x2[...], x3[...]], axis=0)
        cot = jnp.concatenate([c0[...], c1[...], c2[...], c3[...]], axis=0)
        dz = as_column(prob_ref[...], R) * cot.astype(f32)
        dz_ref[...] = dz.astype(bf16)
        dzt_ref[...] = dz.T.astype(bf16)
        xt_ref[...] = x_ref[...].astype(f32).T.astype(bf16)

    up = jnp.concatenate([w_ref[2 * r * units : (2 * r + 1) * units, :] for r in range(per)], axis=0)
    down = jnp.concatenate([w_ref[(2 * r + 1) * units : (2 * r + 2) * units, :] for r in range(per)], axis=0)
    lin = dotf(up, xt_ref[...])
    cdf = 0.5 * (1.0 + lax.erf(lin * math.sqrt(0.5)))
    act = (lin * cdf).astype(bf16)
    slope = cdf + lin * jnp.exp(-0.5 * lin * lin) * (1.0 / math.sqrt(2.0 * math.pi))
    dlin = (dotf(down, dzt_ref[...]) * slope).astype(bf16)
    gdown = dotf(act, dz_ref[...]).astype(bf16)
    gup = dotf(dlin, x_ref[...]).astype(bf16)
    acc_out[...] += dotf(act, down, ((0,), (0,)))
    acc_row[...] += dotf(dlin, up, ((0,), (0,)))
    for r in range(per):
        g_ref[2 * r * units : (2 * r + 1) * units, :] = gup[r * units : (r + 1) * units]
        g_ref[(2 * r + 1) * units : (2 * r + 2) * units, :] = gdown[r * units : (r + 1) * units]

    @pl.when(pl.program_id(0) == steps - 1)
    def _():
        out = acc_out[...].astype(bf16)
        out_ref[...] = out
        drow_ref[...] = acc_row[...].astype(bf16)
        dot_ref[...] = as_rows(jnp.sum(out.astype(f32) * dz_ref[...].astype(f32), axis=1, keepdims=True), R)


def experts(x, cot, prob, w, units, per=2):
    R, D = len(x) * x[0].shape[0], x[0].shape[1]
    block = 2 * units * per
    steps = w.shape[0] // block
    fix = whole((R, D))
    mov = rows_at(block, D)
    return pl.pallas_call(
        functools.partial(experts_kernel, steps=steps, per=per, units=units),
        grid=(steps,),
        in_specs=[whole(x[0].shape)] * 8 + [whole(prob.shape), mov],
        out_specs=[fix, fix, whole((8, R)), mov],
        out_shape=[SHAPE((R, D), bf16)] * 2 + [SHAPE((8, R), f32), SHAPE(w.shape, bf16)],
        scratch_shapes=[pltpu.VMEM((R, D), f32)] * 2 + [pltpu.VMEM((R, D), bf16)] * 2 + [pltpu.VMEM((D, R), bf16)] * 2,
        compiler_params=params(60),
        cost_estimate=cost(),
    )(*x, *cot, prob, w)


def mean_scale(values):
    return lax.rsqrt(jnp.mean(values * values, axis=-1, keepdims=True) + EPSILON)


def dot32(a, b, dims):
    return lax.dot_general(a, b, (dims, ((), ())), precision=HIGHEST, preferred_element_type=f32)


def route_kernel(src_ref, near_ref, far_ref, gain_ref, router_ref, ids_ref, row_ref, col_ref, res_ref, prob_ref, gate_ref, out_ref, slotp_ref, *, count):
    res = src_ref[...].astype(f32) + near_ref[...] + far_ref[...].astype(f32)
    res_ref[...] = res
    normed = res * mean_scale(res) * gain_ref[1:2, :]
    T, S = res.shape[0], out_ref.shape[0]
    logits = dot32(normed, router_ref[...], ((1,), (0,)))
    lane = lax.broadcasted_iota(jnp.int32, (T, LANES), 1)
    logits = jnp.where(lane < count, logits, -jnp.inf)
    e = jnp.exp(logits - jnp.max(logits, axis=1, keepdims=True))
    probs = e / jnp.sum(e, axis=1, keepdims=True)
    prob_ref[...] = probs
    gate = jnp.sum(jnp.where(lane == ids_ref[...], probs, 0.0), axis=1, keepdims=True)
    gate_ref[...] = jnp.broadcast_to(gate, (T, LANES))
    take = (lax.broadcasted_iota(jnp.int32, (S, T), 0) == row_ref[...]).astype(bf16)
    out_ref[...] = dotf(take, normed.astype(bf16)).astype(bf16)
    put = lax.broadcasted_iota(jnp.int32, (T, S), 1) == col_ref[...]
    slotp_ref[...] = jnp.broadcast_to(jnp.sum(jnp.where(put, gate, 0.0), axis=0, keepdims=True), (8, S))


def route_tokens(source, near, far, gains, router, ids, row, col, slots, count):
    T, D = source.shape
    return pl.pallas_call(
        functools.partial(route_kernel, count=count),
        out_shape=[SHAPE((T, D), f32), SHAPE((T, LANES), f32), SHAPE((T, LANES), f32), SHAPE((slots, D), bf16), SHAPE((8, slots), f32)],
        compiler_params=params(48),
        cost_estimate=cost(),
    )(source, near, far, gains, router, ids, row, col)


def back_kernel(r0, r1, r2, r3, dot_ref, col_ref, ids_ref, prob_ref, router_ref, res_ref, cot_ref, gain_ref, dres_ref, dmix_ref, part_ref, *, count):
    res = res_ref[...]
    T, S = res.shape[0], dot_ref.shape[1]
    rows = jnp.concatenate([r0[...], r1[...], r2[...], r3[...]], axis=0)
    put = lax.broadcasted_iota(jnp.int32, (T, S), 1) == col_ref[...]
    lane = lax.broadcasted_iota(jnp.int32, (T, LANES), 1)
    weighted = jnp.sum(jnp.where(put, dot_ref[0:1, :], 0.0), axis=1, keepdims=True)
    dlog = weighted * (jnp.where(lane == ids_ref[...], 1.0, 0.0) - prob_ref[...])
    dnorm = dotf(put.astype(bf16), rows) + dot32(dlog, router_ref[...], ((1,), (1,)))
    scale = mean_scale(res)
    hat = res * scale
    part_ref[0:8, :] = jnp.broadcast_to(jnp.sum(dnorm * hat, axis=0, keepdims=True), (8, res.shape[1]))
    part_ref[8:, :] = dot32(dlog, hat * gain_ref[1:2, :], ((0,), (0,)))[0 : part_ref.shape[0] - 8]
    a = gain_ref[1:2, :] * dnorm
    dres = cot_ref[...].astype(f32) + scale * (a - hat * jnp.mean(a * hat, axis=-1, keepdims=True))
    dres_ref[...] = dres
    dmix_ref[...] = dres.astype(bf16)


def back_tokens(rows, dots, col, ids, probs, router, res, cot, gains, count):
    T, D = res.shape
    return pl.pallas_call(
        functools.partial(back_kernel, count=count),
        out_shape=[SHAPE((T, D), f32), SHAPE((T, D), bf16), SHAPE((16, D), f32)],
        compiler_params=params(48),
        cost_estimate=cost(),
    )(*rows, dots, col, ids, probs, router, res, cot, gains)


def step_of(refs, outs, grad, rate, factor, at=Ellipsis):
    weight, velocity, average = (ref[at] for ref in refs)
    g = grad * factor
    momentum = MOMENT * velocity + g
    new = weight - rate * (g + MOMENT * momentum)
    outs[0][at] = new
    outs[1][at] = momentum
    outs[2][at] = SMOOTH * average + (1.0 - SMOOTH) * new
    outs[3][at] = new.astype(bf16)


def upright(a, rows, columns):
    a = a.astype(f32)
    short = -a.shape[0] % LANES
    if short:
        a = jnp.concatenate([a, jnp.zeros((short, a.shape[1]), f32)], axis=0)
    return a.T[0:rows, 0:columns]


def mixer_step_kernel(*refs, factor, own, width, xw, vrows):
    conv_ref, gate_ref, outg_ref = refs[:3]
    ins = [refs[4 + 3 * p : 7 + 3 * p] for p in range(5)]
    outs = [refs[19 + 4 * p : 23 + 4 * p] for p in range(5)]
    inward, select, delta, channel, outward = range(5)
    step_of(ins[inward], outs[inward], conv_ref[0:own, 0:width].astype(f32), LEARNING[0], factor, 0)
    step_of(ins[inward], outs[inward], gate_ref[0:own, :].astype(f32), LEARNING[0], factor, 1)
    at = width
    step_of(ins[select], outs[select], conv_ref[0:own, at : at + LANES].astype(f32)[:, 0:xw], LEARNING[1], factor)
    rest = upright(conv_ref[:, at + LANES : at + 2 * LANES], LANES, own)
    step_of(ins[delta], outs[delta], rest[0:DT_RANK], LEARNING[2], factor)
    step_of(ins[channel], outs[channel], rest[DT_RANK : DT_RANK + vrows], LEARNING[3], factor)
    step_of(ins[outward], outs[outward], outg_ref[0:own, :].astype(f32), LEARNING[4], factor)


def mixer_step(conv, gate, outg, last, triples, factor):
    own, width = triples[4][0].shape
    xw, vrows = triples[1][0].shape[1], triples[3][0].shape[0]
    shapes = []
    for triple in triples:
        shapes += [SHAPE(triple[0].shape, f32)] * 3 + [SHAPE(triple[0].shape, bf16)]
    flat = pl.pallas_call(
        functools.partial(mixer_step_kernel, factor=factor, own=own, width=width, xw=xw, vrows=vrows),
        out_shape=shapes,
        compiler_params=params(56),
        cost_estimate=cost(),
    )(conv, gate, outg, last, *[a for triple in triples for a in triple])
    return [flat[4 * p : 4 * p + 4] for p in range(5)]


def experts_step_kernel(gup_ref, gdown_ref, *refs, factor):
    ups, downs = refs[0:3], refs[3:6]
    rows, columns = ups[0].shape[1:]
    step_of(ups, refs[6:10], upright(gup_ref[...], rows, columns), LEARNING[5], factor, 0)
    step_of(downs, refs[10:14], gdown_ref[...].astype(f32), LEARNING[6], factor, 0)


def experts_step(grads, ups, downs, factor):
    _, D, units = ups[0].shape
    block = LANES if units % LANES == 0 else units
    n = units // block
    up = pl.BlockSpec((1, D, block), lambda i: (0, 0, i))
    down = pl.BlockSpec((1, block, D), lambda i: (0, i, 0))
    shapes = lambda a: [SHAPE(a.shape, f32)] * 3 + [SHAPE(a.shape, bf16)]
    flat = pl.pallas_call(
        functools.partial(experts_step_kernel, factor=factor),
        grid=(n,),
        in_specs=[rows_at(block, D), rows_at(block, D, n)] + [up] * 3 + [down] * 3,
        out_specs=[up] * 4 + [down] * 4,
        out_shape=shapes(ups[0]) + shapes(downs[0]),
        compiler_params=params(48),
        cost_estimate=cost(),
    )(grads, grads, *ups, *downs)
    return list(flat[:4]), list(flat[4:])


START, PIECES = 5, 4


def contract_rows(left, right):
    return dotf(left, right, ((0,), (0,)))


def tie(*values):
    return lax.optimization_barrier(values)


def ring_order(n):
    return list(range(0, n, 2)) + list(range(n - 1, 0, -2))


def ring_gather(ahead_part, back_part, axis, between):
    n = lax.axis_size(axis)
    order = ring_order(n)
    ahead = [(order[i], order[(i + 1) % n]) for i in range(n)]
    back = [(b, a) for a, b in ahead]
    first, second = [ahead_part], [back_part]
    for s in range(n - 1):
        first[-1], second[-1] = between(s, first[-1], second[-1])
        first.append(lax.ppermute(first[-1], axis, ahead))
        second.append(lax.ppermute(second[-1], axis, back))
    place = [order.index(i) for i in range(n)]
    owners = jnp.array([[order[(place[i] - r) % n] for r in range(n)] for i in range(n)], jnp.int32)
    return owners[lax.axis_index(axis)], first, [second[-r % n] for r in range(n)]


def land(results, sums, *arrived):
    results = list(results)
    coming = [got for one in sums for got in one.arriving()]
    all_of = list(tie(*results, *arrived, *coming))
    at = len(results)
    coming = all_of[at + len(arrived) :]
    for one in sums:
        one.add(coming)
    return all_of[:at], all_of[at : at + len(arrived)]


class HalvingSum:
    def __init__(self, value, axis):
        self.axis, self.n, self.me = axis, lax.axis_size(axis), lax.axis_index(axis)
        self.value, self.bit, self.sent = value, 1, False

    def launch(self, token):
        if self.bit < self.n:
            self.sent = True
            mine = (self.me // self.bit) % 2
            shape = self.value.shape
            pairs = self.value.reshape((shape[0] // 2, 2) + shape[1:])
            self.keep = lax.dynamic_index_in_dim(pairs, mine, 1, keepdims=False)
            send = lax.dynamic_index_in_dim(pairs, 1 - mine, 1, keepdims=False)
            send, token = tie(send, token)
            self.got = lax.ppermute(send, self.axis, [(i, i ^ self.bit) for i in range(self.n)])
        return token

    def arriving(self):
        return [self.got] if self.sent else []

    def add(self, arrived):
        if self.sent:
            self.sent = False
            self.value = (self.keep.astype(f32) + arrived.pop(0).astype(f32)).astype(bf16)
            self.bit *= 2

    def finish(self):
        while self.bit < self.n:
            if not self.sent:
                self.launch(jnp.zeros((1,), f32))
            self.add(self.arriving())
        return self.value[0]


class SharedSum:
    def __init__(self, value, axis):
        self.axis, self.n = axis, lax.axis_size(axis)
        self.value, self.bit, self.got = value, 1, None

    def launch(self, token):
        if self.bit < self.n:
            value, token = tie(self.value, token)
            self.value = value
            self.got = lax.ppermute(value, self.axis, [(i, i ^ self.bit) for i in range(self.n)])
        return token

    def arriving(self):
        return [] if self.got is None else [self.got]

    def add(self, arrived):
        if self.got is not None:
            self.value, self.got = self.value + arrived.pop(0), None
            self.bit *= 2

    def finish(self):
        while self.bit < self.n:
            if self.got is None:
                self.launch(jnp.zeros((1,), f32))
            self.add(self.arriving())
        return self.value


def swap(value, j):
    n = lax.axis_size("mp")
    return lax.ppermute(value, "mp", [(i, i ^ j) for i in range(n)])


def gather_mp_blocks(rows):
    near = swap(rows, 1)
    across = swap(rows, 2)
    return [rows, near, across, swap(across, 1)]


def in_order(blocks):
    me, n = lax.axis_index("mp"), lax.axis_size("mp")
    rows = blocks[0]
    total = jnp.zeros((n,) + rows.shape, rows.dtype)
    for j, block in enumerate(blocks):
        total = lax.dynamic_update_index_in_dim(total, block, me ^ j, 0)
    return total.reshape(n * rows.shape[0], rows.shape[1])


def sum_mp(value):
    value = value + swap(value, 1)
    return value + swap(value, 2)


def scatter_near(halves):
    me = lax.axis_index("mp")

    def pick(j):
        k = (me ^ j) % 2
        one = lax.dynamic_index_in_dim(halves[0], k, 0, keepdims=False)
        two = lax.dynamic_index_in_dim(halves[1], k, 0, keepdims=False)
        return jnp.where((me ^ j) < 2, one, two)

    return [pick(0), pick(2), swap(jnp.stack([pick(3), pick(1)]), 1)]


def scatter_far(mine, others, near):
    near = near.astype(f32)
    return mine.astype(f32) + near[1], (others.astype(f32) + near[0]).astype(bf16)


def nesterov(weight, velocity, average, step_grad, rate):
    momentum = MOMENT * velocity + step_grad
    new_weight = weight - rate * (step_grad + MOMENT * momentum)
    smoothed = SMOOTH * average + (1.0 - SMOOTH) * new_weight
    return [new_weight, momentum, smoothed, new_weight.astype(jnp.bfloat16)]


def body(
    block_input, cotangent, expert_ids, slot_ids,
    inward_proj, select_proj, delta_proj, channel_params, outward_proj, expert_up, expert_down, norm_gains, router_weight,
    inward_velocity, select_velocity, delta_velocity, channel_velocity, outward_velocity, upward_velocity,
    downward_velocity, gains_velocity, router_velocity,
    inward_average, select_average, delta_average, channel_average, outward_average, upward_average,
    downward_average, gains_average, router_average,
):
    tok_rows, width = block_input.shape
    ring, peers = lax.axis_size("dp"), lax.axis_size("mp")
    me = lax.axis_index("mp")
    own = inward_proj.shape[2]
    slot = -(-own // 16) * 16
    wide = -(-slot * ring // LANES) * LANES
    experts_all = router_weight.shape[1]
    slots = peers * CAP

    source = block_input.astype(f32)
    scale1 = mean_scale(source)
    normed_b = (source * scale1 * norm_gains[0]).astype(bf16)
    blocks = [normed_b]
    piece = tok_rows // PIECES
    pieces = [normed_b[i * piece : (i + 1) * piece] for i in range(PIECES)]

    half = 5 * LANES
    units = expert_down.shape[1]
    ring_a, ring_b = prep(
        jnp.swapaxes(inward_proj, 1, 2), select_proj, delta_proj, channel_params, outward_proj, half
    )

    def exchange(blocks):
        parts = blocks.reshape(peers, CAP, -1)
        return [parts[0]] + [swap(parts[j], j) for j in range(1, peers)]

    slot_index = (expert_ids ^ me) * CAP + slot_ids
    slot_row, slot_col, ids_col = slot_index[None, :], slot_index[:, None], expert_ids[:, None]
    dispatch = (lax.broadcasted_iota(jnp.int32, (slots, tok_rows), 0) == slot_row).astype(bf16)
    early = {"cot": jnp.dot(dispatch, cotangent, preferred_element_type=f32).astype(bf16), "up": expert_up[0]}

    def between(s, a, b):
        if s == START:
            a, b, early["up"] = tie(a, b, early["up"])
        if s < PIECES:
            pieces[s], a, b = tie(pieces[s], a, b)
            pieces[s] = swap(pieces[s], 2)
        if 0 < s <= PIECES:
            a, b, pieces[s - 1] = tie(a, b, pieces[s - 1])
        if s == PIECES:
            blocks.extend([swap(normed_b, 1), jnp.concatenate(pieces)])
            blocks.append(swap(blocks[2], 1))
            a, b, early["cot"] = tie(a, b, early["cot"])
            early["cot"] = exchange(early["cot"])
        if s == PIECES + 1:
            a, b, blocks[1], blocks[3] = tie(a, b, blocks[1], blocks[3])
        return a, b

    owners, mix_a, mix_b = ring_gather(ring_a, ring_b, "dp", between)
    expert_w = lax.all_gather(prep_experts(early["up"], expert_down[0]), "dp", axis=0, tiled=True)
    w_in, selw, delta_w, chan, out_w = mixer_weights(owners, mix_a, mix_b, slot, wide, width, half)
    seq = in_order(blocks)
    seq, *cot_rows = tie(seq, *early["cot"])

    router_pad = jnp.pad(router_weight, ((0, 0), (0, LANES - experts_all)))

    def exchange_row(rows):
        parts = rows[0].reshape(peers, CAP)
        row = jnp.concatenate([parts[0]] + [swap(parts[j], j) for j in range(1, peers)])
        return jnp.broadcast_to(row[None], (8, slots))

    count = seq.shape[0] // 2
    conv_tail, state = jnp.zeros((8, wide), f32), jnp.zeros((NST, wide), f32)
    convs, scans = [None] * 2, [None] * 2
    convs[0] = list(conv_fwd(seq, 0, count, w_in, chan, selw, conv_tail))
    pair = convs[0][5] + swap(convs[0][5], 1)
    pair, conv_tail = tie(pair, convs[0][6])
    other = swap(pair, 2)
    convs[1], (other,) = land(conv_fwd(seq, count, count, w_in, chan, selw, conv_tail), [], other)
    selections = [pair + other]
    pair = convs[1][5] + swap(convs[1][5], 1)
    pair, state = tie(pair, state)
    other = swap(pair, 2)
    edges = [state]
    scans[0], (other,) = land(
        scan_fwd(selections[0], delta_w, convs[0][3], convs[0][1], chan, out_w, state), [], other
    )
    selections.append(pair + other)
    edges.append(scans[0][6])
    scans[1] = scan_fwd(selections[1], delta_w, convs[1][3], convs[1][1], chan, out_w, edges[1])
    near, far = scatter_far(*scatter_near([s[4].reshape(2, tok_rows, width) for s in scans]))
    far = swap(far, 2)
    residual, probs, gate_prob, outgoing, prob_slots = route_tokens(
        block_input, near, far, norm_gains, router_pad, ids_col, slot_row, slot_col, slots, experts_all
    )
    arrived = exchange(outgoing)
    expert_out, d_rows, dots, grad_experts = experts(arrived, cot_rows, exchange_row(prob_slots), expert_w, units)
    experts_grad = lax.psum_scatter(grad_experts, "dp", scatter_dimension=0, tiled=True)

    d_residual, d_mixer, parts = back_tokens(
        exchange(d_rows), exchange_row(dots), slot_col, ids_col, probs, router_pad, residual, cotangent, norm_gains,
        experts_all,
    )
    portion = in_order(gather_mp_blocks(d_mixer))
    def both(left, right):
        return contract_rows(left[0], right[:count]) + contract_rows(left[1], right[count:])

    def cut(a):
        return a[: slot * ring]

    by_owner = lambda a: HalvingSum(cut(a).reshape(ring, slot, -1), "dp")
    out_sum = by_owner(both([s[3] for s in scans], portion).astype(bf16))
    q, later = jnp.zeros((NST, wide), f32), jnp.zeros((8, wide), f32)

    def run_scan(h, q):
        kept = scans[h][0], convs[h][3], convs[h][1], scans[h][1], scans[h][2]
        return scan_bwd(portion, h * count, 0, kept, edges[h], q, count, out_w, selections[h], chan, delta_w)

    tails, sums = [None] * 2, [None] * 2
    expert_out, q = tie(expert_out, out_sum.launch(q))
    returned = exchange(expert_out)
    tails[1], returned[1:] = land(run_scan(1, q), [out_sum], *returned[1:])
    pair = tails[1][3] + swap(tails[1][3], 1)
    pair, q = tie(pair, out_sum.launch(tails[1][5]))
    other = swap(pair, 2)
    tails[0], (other,) = land(run_scan(0, q), [out_sum], other)
    sums[1] = pair + other
    pair = tails[0][3] + swap(tails[0][3], 1)
    gate_sum = by_owner(both([t[0] for t in tails], seq).astype(bf16))
    tail_sum = tails[0][4] + tails[1][4]
    pair, later = tie(pair, gate_sum.launch(out_sum.launch(later)))
    other = swap(pair, 2)

    def run_conv(h, later, gch, grads):
        return conv_bwd(
            h * count, count, h == 0, tails[h][1], sums[h], selw, convs[h][2], convs[h][0], tails[h][0], w_in, seq,
            chan, later, convs[h][4], tails[h][2], scans[h][5], grads, gch, tail_sum,
        )

    backs = [None] * 2
    backs[1], (other,) = land(run_conv(1, later, jnp.zeros((8, wide), f32), None), [out_sum, gate_sum], other)
    sums[0] = pair + other
    later = gate_sum.launch(backs[1][2])
    backs[0] = run_conv(0, later, backs[1][3], backs[1][4])
    later = backs[0][2]
    factor = 1.0 / math.sqrt(tok_rows * ring * peers)

    conv_sum = by_owner(backs[0][4])
    near = scatter_near([b[0].reshape(2, tok_rows, width) for b in backs])
    gain_part = (backs[0][1][:1] + backs[1][1][:1]) / norm_gains[:1]
    shared = SharedSum(jnp.concatenate([gain_part, parts[:1], parts[8 : 8 + experts_all]]), "dp")
    later = shared.launch(conv_sum.launch(later))
    near[0], near[1], experts_grad, later = tie(near[0], near[1], experts_grad, later)
    up_new, down_new = experts_step(
        experts_grad,
        (expert_up, upward_velocity, upward_average),
        (expert_down, downward_velocity, downward_average),
        factor,
    )
    (up_new[3], later), (near[2],) = land([up_new[3], later], [], near[2])
    near, far_send = scatter_far(*near)
    far_send, later = tie(far_send, later)
    far = swap(far_send, 2)
    (later,), _ = land([later], [conv_sum, gate_sum, shared])
    later, returned[0] = tie(shared.launch(gate_sum.launch(conv_sum.launch(later))), returned[0])
    tokens_out = contract_rows(dispatch, jnp.concatenate(returned))
    block_output = (residual + gate_prob[:, :1] * tokens_out).astype(bf16)
    (block_output, later), _ = land([block_output, later], [conv_sum, gate_sum, shared])
    later, far = tie(shared.launch(conv_sum.launch(later)), far)
    d_normed = near + far.astype(f32)
    a1 = norm_gains[0] * d_normed
    hat1 = source * scale1
    block_grad = d_residual + scale1 * (a1 - hat1 * jnp.mean(a1 * hat1, axis=-1, keepdims=True))
    (block_grad, later), _ = land([block_grad, later], [conv_sum, shared])
    shared = sum_mp(shared.finish())
    mixer_new = mixer_step(
        conv_sum.finish(),
        gate_sum.finish(),
        out_sum.finish(),
        later,
        (
            tuple(jnp.swapaxes(a, 1, 2) for a in (inward_proj, inward_velocity, inward_average)),
            (select_proj, select_velocity, select_average),
            (delta_proj, delta_velocity, delta_average),
            (channel_params, channel_velocity, channel_average),
            (outward_proj, outward_velocity, outward_average),
        ),
        factor,
    )
    results = [block_output, block_grad]
    mixer_new[0] = [jnp.swapaxes(a, 1, 2) for a in mixer_new[0]]
    for new in mixer_new:
        results.extend(new)
    results.extend(up_new)
    results.extend(down_new)
    results.extend(nesterov(norm_gains, gains_velocity, gains_average, shared[:2] * factor, LEARNING[7]))
    results.extend(nesterov(router_weight, router_velocity, router_average, shared[2:].T * factor, LEARNING[8]))
    return tuple(results)


def solution(mesh):
    in_specs = (
        P(("dp", "mp"), None),
        P(("dp", "mp"), None),
        P(("dp", "mp")),
        P(("dp", "mp")),
        P(None, None, ("dp", "mp")),
        P(("dp", "mp"), None),
        P(None, ("dp", "mp")),
        P(None, ("dp", "mp")),
        P(("dp", "mp"), None),
        P("mp", None, "dp"),
        P("mp", "dp", None),
        P(),
        P(),
        P(None, None, ("dp", "mp")),
        P(("dp", "mp"), None),
        P(None, ("dp", "mp")),
        P(None, ("dp", "mp")),
        P(("dp", "mp"), None),
        P("mp", None, "dp"),
        P("mp", "dp", None),
        P(),
        P(),
        P(None, None, ("dp", "mp")),
        P(("dp", "mp"), None),
        P(None, ("dp", "mp")),
        P(None, ("dp", "mp")),
        P(("dp", "mp"), None),
        P("mp", None, "dp"),
        P("mp", "dp", None),
        P(),
        P(),
    )
    out_specs = (
        P(("dp", "mp"), None),
        P(("dp", "mp"), None),
        P(None, None, ("dp", "mp")),
        P(None, None, ("dp", "mp")),
        P(None, None, ("dp", "mp")),
        P(None, None, ("dp", "mp")),
        P(("dp", "mp"), None),
        P(("dp", "mp"), None),
        P(("dp", "mp"), None),
        P(("dp", "mp"), None),
        P(None, ("dp", "mp")),
        P(None, ("dp", "mp")),
        P(None, ("dp", "mp")),
        P(None, ("dp", "mp")),
        P(None, ("dp", "mp")),
        P(None, ("dp", "mp")),
        P(None, ("dp", "mp")),
        P(None, ("dp", "mp")),
        P(("dp", "mp"), None),
        P(("dp", "mp"), None),
        P(("dp", "mp"), None),
        P(("dp", "mp"), None),
        P("mp", None, "dp"),
        P("mp", None, "dp"),
        P("mp", None, "dp"),
        P("mp", None, "dp"),
        P("mp", "dp", None),
        P("mp", "dp", None),
        P("mp", "dp", None),
        P("mp", "dp", None),
        P(),
        P(),
        P(),
        P(),
        P(),
        P(),
        P(),
        P(),
    )
    return jax.shard_map(body, mesh=mesh, in_specs=in_specs, out_specs=out_specs, check_vma=False)
```
